128 devices in a mesh: vocab: 16 (over y, z), tokens: 8 (over x, core).
Axes of the slice: x: 4, y: 4, z: 4, core: 2. Of those that a mesh axis runs over, the one named last changes fastest.
Arguments:
- teacher_logits: bfloat16 [2048, 65536], P('tokens', 'vocab'), may hold values from -300 to 350
- student_hidden: bfloat16 [2048, 4096], P('tokens'), may hold values from -18 to 18
- student_unembed: bfloat16 [4096, 32768], P(None, 'vocab'), may hold values from -8 to 8
- tile_weights: bfloat16 [256, 512, 512], P('vocab', 'tokens'), may hold values from 0.0009994507 to 1
- tile_pairs: int32 [256, 2], P('vocab'), may hold values from 0 to 127, as said below
- tile_count: int32 [16], P('vocab'), may hold values from 1 to 16, as said below
Outputs:
- grad_hidden: bfloat16 [2048, 4096], P('tokens', 'vocab')
- divergence: float32 [2048], P('tokens')
The draws below stay inside these ranges and needn't reach their ends.
Inputs may be any that keep to these rules, and one draw needn't show every extreme that they name: `tile_pairs`: row i belongs to vocab index k = i // 16. Its first entry, the teacher block, lies in k * 8 to (k + 1) * 8 - 1; its second, the student block b, has (b % 4) // 1 equal to k % 4. Dead slots follow the same rule. `tile_count`: entry k counts the live slots of vocab index k, which are its first ones.
All inputs are finite; a program needn't handle non-finite values.
Results may differ from the reference program's by a relative error of at most 0.015.
Values may be sent and summed in bfloat16 or wider, within the bound.
No kernel may reach another device: no remote copies, remote signals or barrier semaphores. Data moves between devices by JAX's collectives and lax.ppermute only.
A program may use at most 192 MiB of HBM per device.

```python
import math
import jax
import jax.numpy as jnp
from jax import lax

DS = 4096
VT = 65536
VS = 32768
BLK = 512
TILE_DEV = 16
TOKENS = 2048
TB_DEV = 8
SB_DEV = 4
QUART = 1
NTILES = 256
N_VOCAB = 16


def draw_teacher_logits(key, part):
    base_key, row_key, col_key = jax.random.split(jax.random.fold_in(key, 3), 3)
    base = jnp.clip(jax.random.normal(base_key, (TOKENS, VT), jnp.float32), -6.0, 6.0)
    row_scale = jnp.exp(jax.random.uniform(row_key, (TOKENS, 1), jnp.float32, 0.0, math.log(10.0)))
    col_scale = jnp.exp(jax.random.uniform(col_key, (1, VT), jnp.float32, 0.0, math.log(10.0)))
    values = 0.5 * base * row_scale * col_scale
    return values.astype(jnp.bfloat16)


def draw_student_hidden(key, part):
    base_key, row_key = jax.random.split(jax.random.fold_in(key, 5), 2)
    base = jnp.clip(jax.random.normal(base_key, (TOKENS, DS), jnp.float32), -6.0, 6.0)
    row_scale = jnp.exp(jax.random.uniform(row_key, (TOKENS, 1), jnp.float32, 0.0, math.log(10.0)))
    values = 0.3 * base * row_scale
    return values.astype(jnp.bfloat16)


def draw_student_unembed(key, part):
    base_key, col_key = jax.random.split(jax.random.fold_in(key, 7), 2)
    base = jnp.clip(jax.random.normal(base_key, (DS, VS), jnp.float32), -6.0, 6.0)
    col_scale = jnp.exp(jax.random.uniform(col_key, (1, VS), jnp.float32, 0.0, math.log(10.0)))
    values = base * col_scale / math.sqrt(DS)
    return values.astype(jnp.bfloat16)


def draw_tile_pairs(key, part):
    groups = NTILES // TILE_DEV
    keys = jax.random.split(jax.random.fold_in(key, 11), 7)
    row_ids = jnp.arange(NTILES, dtype=jnp.int32)
    owner_dev = row_ids // TILE_DEV
    slot_ids = row_ids % TILE_DEV
    teacher_local = jax.random.randint(keys[0], (NTILES,), 0, TB_DEV, dtype=jnp.int32)
    top_slot = jax.random.randint(keys[1], (groups,), 0, TILE_DEV, dtype=jnp.int32)
    low_slot = (top_slot + 1 + jax.random.randint(keys[2], (groups,), 0, TILE_DEV - 1, dtype=jnp.int32)) % TILE_DEV
    teacher_local = jnp.where(slot_ids == top_slot[owner_dev], TB_DEV - 1, teacher_local)
    teacher_local = jnp.where(slot_ids == low_slot[owner_dev], 0, teacher_local)
    first_pick = jax.random.randint(keys[3], (NTILES,), 0, groups, dtype=jnp.int32)
    second_pick = jax.random.randint(keys[4], (NTILES,), 0, groups, dtype=jnp.int32)
    order = jax.random.permutation(keys[5], groups)
    student_owner = order[jnp.minimum(first_pick, second_pick)]
    within = owner_dev % 4 * QUART + jax.random.randint(keys[6], (NTILES,), 0, QUART, dtype=jnp.int32)
    student = student_owner * SB_DEV + within
    teacher = owner_dev * TB_DEV + teacher_local
    return jnp.stack([teacher, student], axis=1).astype(jnp.int32)


def draw_tile_count(key, part):
    groups = NTILES // TILE_DEV
    first_key, second_key, full_key = jax.random.split(jax.random.fold_in(key, 23), 3)
    first_draw = jax.random.randint(first_key, (groups,), 0, TILE_DEV, dtype=jnp.int32)
    second_draw = jax.random.randint(second_key, (groups,), 0, TILE_DEV, dtype=jnp.int32)
    counts = 1 + first_draw * second_draw // TILE_DEV
    full_index = jax.random.randint(full_key, (), 0, groups, dtype=jnp.int32)
    return jnp.where(jnp.arange(groups, dtype=jnp.int32) == full_index, TILE_DEV, counts).astype(jnp.int32)


def block_levels(own_key, dims, cuts, smallest, high):
    gain = 1.0
    for dim, parts in cuts:
        draws = jax.random.uniform(jax.random.fold_in(jax.random.fold_in(own_key, 6), dim), (parts,), jnp.float32, smallest / len(cuts), high / len(cuts))
        gain = gain * jnp.repeat(jnp.exp(draws), dims[dim] // parts).reshape((-1,) + (1,) * (len(dims) - 1 - dim))
    return gain


def setup_inputs(seed: int = 0) -> dict:
    streams_of = jax.random.split(jax.random.key(seed), 7)
    teacher_logits = draw_teacher_logits(jax.random.fold_in(streams_of[6], 71), 0)
    student_hidden = draw_student_hidden(jax.random.fold_in(streams_of[6], 71), 0)
    student_unembed = draw_student_unembed(jax.random.fold_in(streams_of[6], 71), 0)
    tile_weights = jnp.clip(jnp.exp(math.log(1.0) - 6.9083047 * jax.random.uniform(streams_of[3], (NTILES, BLK, BLK), jnp.float32) ** block_levels(streams_of[3], (NTILES, BLK, BLK), ((0, 16), (1, 8)), -0.2, 0.2)), 0.0009994507, 1.0).astype(jnp.bfloat16)
    tile_pairs = draw_tile_pairs(jax.random.fold_in(streams_of[6], 71), 0)
    tile_count = draw_tile_count(jax.random.fold_in(streams_of[6], 71), 0)
    return {"teacher_logits": teacher_logits, "student_hidden": student_hidden, "student_unembed": student_unembed, "tile_weights": tile_weights, "tile_pairs": tile_pairs, "tile_count": tile_count}


def reference(teacher_logits, student_hidden, student_unembed, tile_weights, tile_pairs, tile_count):
    teacher_f32 = teacher_logits.astype(jnp.float32)
    teacher_peak = jnp.max(teacher_f32, axis=1, keepdims=True)
    shifted = jnp.exp(teacher_f32 - teacher_peak)
    teacher_probs = (shifted / jnp.sum(shifted, axis=1, keepdims=True)).astype(jnp.bfloat16)
    student_blocks = VS // BLK

    def per_owner(raw_sum, owner_index):
        def per_tile(slot_index, partial_value):
            position = jnp.asarray(slot_index).astype(jnp.int32)
            row_index = (owner_index * TILE_DEV + position).astype(jnp.int32)
            pair_row = lax.dynamic_index_in_dim(tile_pairs, row_index, 0, keepdims=False)
            teacher_start = (pair_row[0] * BLK).astype(jnp.int32)
            columns = lax.dynamic_slice_in_dim(teacher_probs, teacher_start, BLK, 1)
            weights = lax.dynamic_index_in_dim(tile_weights, row_index, 0, keepdims=False)
            product = jnp.dot(columns, weights, preferred_element_type=jnp.float32)
            alive = position < tile_count[owner_index]
            product = jnp.where(alive, product, jnp.zeros_like(product))
            target_block = pair_row[1].astype(jnp.int32)
            current = lax.dynamic_index_in_dim(partial_value, target_block, 0, keepdims=False)
            return lax.dynamic_update_index_in_dim(partial_value, current + product, target_block, 0)

        partial_value = lax.fori_loop(0, TILE_DEV, per_tile, jnp.zeros((student_blocks, TOKENS, BLK), jnp.float32))
        rounded = lax.optimization_barrier(partial_value.astype(jnp.bfloat16))
        return raw_sum + rounded.astype(jnp.float32), None

    raw_blocks, _ = lax.scan(per_owner, jnp.zeros((student_blocks, TOKENS, BLK), jnp.float32),
                             jnp.arange(N_VOCAB, dtype=jnp.int32))
    raw_target = raw_blocks.transpose(1, 0, 2).reshape(TOKENS, VS)
    target_total = jnp.sum(raw_target, axis=1, keepdims=True)
    floored = jnp.maximum(target_total, 1.0)
    mass_share = target_total / floored
    target = raw_target / floored
    student_logits = jnp.dot(student_hidden, student_unembed, preferred_element_type=jnp.float32)
    student_peak = jnp.max(student_logits, axis=1, keepdims=True)
    student_exp = jnp.exp(student_logits - student_peak)
    student_mass = jnp.sum(student_exp, axis=1, keepdims=True)
    student_probs = student_exp / student_mass
    logit_grad = (mass_share * student_probs - target).astype(jnp.bfloat16)
    grad_hidden = jnp.dot(logit_grad, student_unembed.T, preferred_element_type=jnp.float32).astype(jnp.bfloat16)
    log_norm = student_peak + jnp.log(student_mass)
    positive = target > 0
    entropy = jnp.where(positive, target * jnp.log(jnp.where(positive, target, 1.0)), 0.0)
    divergence = jnp.sum(entropy - target * (student_logits - log_norm), axis=1)
    return grad_hidden, divergence
```

```python
import functools

import jax
import jax.numpy as jnp
from jax import lax
from jax.experimental import pallas as pl
from jax.experimental.pallas import tpu as pltpu
from jax.sharding import Mesh
from jax.sharding import PartitionSpec as P

F32 = jnp.float32
BF16 = jnp.bfloat16
SIDE = 4
WIDTHS = (128, 128, 128, 128)
VMEM = pl.BlockSpec(memory_space=pltpu.VMEM)
SMEM = pl.BlockSpec(memory_space=pltpu.SMEM)
LIMIT = 40 * 1024 * 1024


def params():
    return pltpu.CompilerParams(vmem_limit_bytes=LIMIT)


def cost(flops, moved, transcendentals=0):
    return pl.CostEstimate(flops=flops, bytes_accessed=moved, transcendentals=transcendentals)


def send(value, axis, step):
    return lax.ppermute(value, axis, [(i, (i + step) % SIDE) for i in range(SIDE)])


def thirds(value):
    high = value.astype(BF16).astype(F32)
    rest = value - high
    middle = rest.astype(BF16).astype(F32)
    return high, middle, rest - middle


def product_kernel(place, pairs, count, probs, weights, *rest):
    outs, total = rest[:SIDE], rest[SIDE]
    block = weights.shape[0] * 64
    width = weights.shape[2]
    vocab_y = place[0]
    first_block = (vocab_y * SIDE + place[1]) * (probs.shape[1] // block)
    total[...] = jnp.zeros_like(total)

    def tile(slot, carry):
        teacher = pairs[slot, 0] - first_block
        owner = pairs[slot, 1] // SIDE
        columns = probs[:, pl.ds(pl.multiple_of(teacher * block, block), block)]
        rows = weights[:, pl.ds(pl.multiple_of(slot * 64, 64), 64), :].reshape(block, width)
        total[owner] += jnp.dot(columns, rows, preferred_element_type=F32)
        return carry

    lax.fori_loop(0, count[0], tile, 0)
    for step in range(SIDE):
        start = lax.rem(vocab_y + step, SIDE) * SIDE
        for z in range(SIDE):
            outs[step][z] = total[start + z].astype(BF16)


def products(place, pairs, count, probs, weights):
    rows, width = probs.shape[0], weights.shape[2]
    return pl.pallas_call(
        product_kernel,
        out_shape=[jax.ShapeDtypeStruct((SIDE, rows, width), BF16)] * SIDE,
        in_specs=[SMEM, SMEM, SMEM, VMEM, VMEM],
        out_specs=[VMEM] * SIDE,
        scratch_shapes=[pltpu.VMEM((SIDE * SIDE, rows, width), F32)],
        compiler_params=params(),
        cost_estimate=cost(16 * 2 * rows * 512 * width, 2 * probs.size + 2 * weights.size + 32 * rows * width),
        name="tile_products",
    )(place, pairs, count, probs, weights)


def stats_kernel(*refs):
    parts, out = refs[:-1], refs[-1]
    peaks = [part[:, 0, :] for part in parts]
    peak = functools.reduce(jnp.maximum, [jnp.max(v, axis=0, keepdims=True) for v in peaks])
    speaks = [part[:, 3, :] for part in parts]
    speak = functools.reduce(jnp.maximum, [jnp.max(v, axis=0, keepdims=True) for v in speaks])
    mass = jnp.zeros_like(peak)
    total = jnp.zeros_like(peak)
    smass = jnp.zeros_like(peak)
    scales = []
    for part, own, sown in zip(parts, peaks, speaks):
        factor = jnp.exp(own - peak)
        scales.append(factor[0:1])
        mass += jnp.sum(part[:, 1, :] * factor, axis=0, keepdims=True)
        total += jnp.sum(part[:, 2, :] * factor, axis=0, keepdims=True)
        smass += jnp.sum(part[:, 4, :] * jnp.exp(sown - speak), axis=0, keepdims=True)
    total = total / mass
    floored = jnp.maximum(total, 1.0)
    share = total / floored
    table = [s / mass for s in scales] + [1.0 / floored, share / smass, speak, speak + jnp.log(smass)]
    table = jnp.concatenate(table + [jnp.zeros((128 - len(table), peak.shape[1]), F32)], axis=0)
    out[...] = table.T


def statistics(parts):
    rows = parts[0].shape[2]
    return pl.pallas_call(
        stats_kernel,
        out_shape=jax.ShapeDtypeStruct((rows, 128), F32),
        in_specs=[VMEM] * SIDE,
        out_specs=VMEM,
        compiler_params=params(),
        cost_estimate=cost(16 * rows * 20, 64 * 8 * rows, 32 * rows),
        name="row_stats",
    )(*parts)


def merge_kernel(place, table, *refs):
    parts, outs = refs[:SIDE], refs[SIDE:]
    for step in range(SIDE):
        z = lax.rem(place[1] + step, SIDE)
        value = table[:, 0:1] * parts[0][z].astype(F32)
        for d in range(1, SIDE):
            value += table[:, d : d + 1] * parts[d][z].astype(F32)
        outs[step][...] = value.astype(BF16)


def merged(place, table, parts):
    _, rows, width = parts[0].shape
    return pl.pallas_call(
        merge_kernel,
        out_shape=[jax.ShapeDtypeStruct((rows, width), BF16)] * SIDE,
        in_specs=[SMEM] + [VMEM] * (1 + SIDE),
        out_specs=[VMEM] * SIDE,
        compiler_params=params(),
        cost_estimate=cost(32 * rows * width, 40 * rows * width),
        name="merge_targets",
    )(place, table, *parts)


def gradient_kernel(offset, place, table, logits, *refs):
    parts, grad, loss = refs[:SIDE], refs[SIDE], refs[SIDE + 1]
    width = parts[0].shape[1]
    inverse, share, peak, norm = (table[:, c : c + 1] for c in range(4, 8))
    terms = jnp.zeros(parts[0].shape, F32)
    for step in range(SIDE):
        block = lax.rem(place[1] + SIDE - step, SIDE)
        scores = logits[:, pl.ds(pl.multiple_of(block * 512 + offset, 128), width)]
        target = parts[step][...].astype(F32) * inverse
        positive = target > 0
        entropy = jnp.where(positive, target * jnp.log(jnp.where(positive, target, 1.0)), 0.0)
        terms += entropy - target * (scores - norm)
        value = share * jnp.exp(scores - peak) - target
        grad[block] = value.T.astype(BF16)
    loss[...] = jnp.broadcast_to(jnp.sum(terms.T, axis=0, keepdims=True), loss.shape)


def gradients(offset, place, table, logits, parts):
    rows, width = parts[0].shape
    return pl.pallas_call(
        functools.partial(gradient_kernel, offset),
        out_shape=[
            jax.ShapeDtypeStruct((SIDE, width, rows), BF16),
            jax.ShapeDtypeStruct((8, rows), F32),
        ],
        in_specs=[SMEM] + [VMEM] * (2 + SIDE),
        out_specs=[VMEM, VMEM],
        compiler_params=params(),
        cost_estimate=cost(60 * rows * width, 16 * rows * width + 4 * logits.size, 8 * rows * width),
        name="logit_grad",
    )(place, table, logits, *parts)


def hidden_kernel(chunks, place, unembed, *refs):
    grads, losses = refs[:chunks], refs[chunks : 2 * chunks]
    first = refs[2 * chunks : 2 * chunks + SIDE]
    second = refs[2 * chunks + SIDE : 2 * chunks + 2 * SIDE]
    turned = refs[2 * chunks + 2 * SIDE]
    index = pl.program_id(0)
    rows = turned.shape[1]

    @pl.when(index == 0)
    def _():
        offset = 0
        loss = jnp.zeros((1, rows), F32)
        for part, term in zip(grads, losses):
            width = part.shape[1]
            for block in range(SIDE):
                turned[block * 512 + offset : block * 512 + offset + width, :] = part[block]
            offset += width
            loss += term[0:1]
        packed = jnp.concatenate(list(thirds(loss)) + [jnp.zeros((13, rows), F32)], axis=0).astype(BF16)
        for out in first:
            out[512:528, :] = packed

    result = jnp.dot(unembed[...], turned[...], preferred_element_type=F32).astype(BF16)
    for half in range(2):
        owner = index * 2 + half
        owner_y, owner_z = owner // SIDE, lax.rem(owner, SIDE)
        top = result[half * 256 : half * 256 + 128]
        low = result[half * 256 + 128 : half * 256 + 256]
        for step in range(SIDE):

            @pl.when(lax.rem(place[0] + step, SIDE) == owner_y)
            def _():
                first[step][pl.ds(pl.multiple_of(owner_z * 128, 128), 128), :] = top

            @pl.when(lax.rem(place[1] + step, SIDE) == owner_z)
            def _():
                second[step][pl.ds(pl.multiple_of(owner_y * 128, 128), 128), :] = low


def hidden_parts(place, unembed, grads, losses):
    chunks = len(grads)
    width, cols = unembed.shape
    rows = grads[0].shape[2]
    whole = lambda shape: pl.BlockSpec(shape, lambda i: (0,) * len(shape))
    return pl.pallas_call(
        functools.partial(hidden_kernel, chunks),
        grid=(8,),
        out_shape=[jax.ShapeDtypeStruct((528, rows), BF16)] * SIDE
        + [jax.ShapeDtypeStruct((512, rows), BF16)] * SIDE,
        in_specs=[SMEM, pl.BlockSpec((width // 8, cols), lambda i: (i, 0))]
        + [whole(g.shape) for g in grads]
        + [whole(v.shape) for v in losses],
        out_specs=[whole((528, rows))] * SIDE + [whole((512, rows))] * SIDE,
        scratch_shapes=[pltpu.VMEM((cols, rows), BF16)],
        compiler_params=params(),
        cost_estimate=cost(2 * width * cols * rows, 2 * width * cols + 4 * width * rows),
        name="hidden_grad",
    )(place, unembed, *grads, *losses)


def packed_loss(place_index, parts, at, ordered):
    for step in range(SIDE):
        piece = parts[step][at : at + 16, :].astype(F32)
        ordered[lax.rem(place_index + SIDE - step, SIDE)] = piece[0:1] + piece[1:2] + piece[2:3]
    return ((ordered[0] + ordered[1]) + ordered[2]) + ordered[3]


def middle_kernel(place, *refs):
    first, second = refs[:SIDE], refs[SIDE : 2 * SIDE]
    first_out, second_out = refs[2 * SIDE : 3 * SIDE], refs[3 * SIDE : 4 * SIDE]
    ordered = refs[4 * SIDE]
    rows = ordered.shape[2]
    loss = packed_loss(place[0], first, 512, ordered)
    packed = jnp.concatenate(list(thirds(loss)) + [jnp.zeros((13, rows), F32)], axis=0).astype(BF16)
    for step in range(SIDE):
        at = pl.ds(pl.multiple_of(lax.rem(place[1] + step, SIDE) * 128, 128), 128)
        value = first[0][at, :].astype(F32)
        for part in first[1:]:
            value += part[at, :].astype(F32)
        first_out[step][0:128, :] = value.astype(BF16)
        first_out[step][128:144, :] = packed
        at = pl.ds(pl.multiple_of(lax.rem(place[0] + step, SIDE) * 128, 128), 128)
        value = second[0][at, :].astype(F32)
        for part in second[1:]:
            value += part[at, :].astype(F32)
        second_out[step][...] = value.astype(BF16)


def middle(place, first, second):
    rows = first[0].shape[1]
    return pl.pallas_call(
        middle_kernel,
        out_shape=[jax.ShapeDtypeStruct((144, rows), BF16)] * SIDE
        + [jax.ShapeDtypeStruct((128, rows), BF16)] * SIDE,
        in_specs=[SMEM] + [VMEM] * (2 * SIDE),
        out_specs=[VMEM] * (2 * SIDE),
        scratch_shapes=[pltpu.VMEM((SIDE, 1, rows), F32)],
        compiler_params=params(),
        cost_estimate=cost(8 * 512 * rows, 20 * 512 * rows),
        name="merge_grads",
    )(place, *first, *second)


def last_kernel(place, *refs):
    first, second = refs[:SIDE], refs[SIDE : 2 * SIDE]
    grad, loss, ordered = refs[2 * SIDE :]
    loss[...] = jnp.broadcast_to(packed_loss(place[1], first, 128, ordered), loss.shape)
    top = first[0][0:128, :].astype(F32)
    low = second[0][...].astype(F32)
    for a, b in zip(first[1:], second[1:]):
        top += a[0:128, :].astype(F32)
        low += b[...].astype(F32)
    grad[:, 0:128] = top.T.astype(BF16)
    grad[:, 128:256] = low.T.astype(BF16)


def last(place, first, second):
    rows = first[0].shape[1]
    return pl.pallas_call(
        last_kernel,
        out_shape=[jax.ShapeDtypeStruct((rows, 256), BF16), jax.ShapeDtypeStruct((8, rows), F32)],
        in_specs=[SMEM] + [VMEM] * (2 * SIDE),
        out_specs=[VMEM, VMEM],
        scratch_shapes=[pltpu.VMEM((SIDE, 1, rows), F32)],
        compiler_params=params(),
        cost_estimate=cost(8 * 256 * rows, 20 * 256 * rows),
        name="last_sum",
    )(place, *first, *second)


def shards(teacher_logits, student_hidden, student_unembed, tile_weights, tile_pairs, tile_count):
    place = jnp.stack([lax.axis_index("vy"), lax.axis_index("vz")]).astype(jnp.int32)
    rows = teacher_logits.shape[0]
    slots, shard_rows, block = tile_weights.shape

    row_sums = jnp.sum(tile_weights.astype(F32), axis=2)
    high = lax.reduce_precision(row_sums, 8, 7)
    mid = lax.reduce_precision(row_sums - high, 8, 7)
    low = row_sums - high - mid
    gathered = []
    offset = 0
    for index, width in enumerate(WIDTHS):
        piece = tile_weights[:, :, offset : offset + width].reshape(slots * shard_rows, width)
        if index == 1:
            extra = jnp.stack([high, mid, low]).astype(BF16).reshape(-1, width)
            extra = jnp.pad(extra, ((0, -extra.shape[0] % 16), (0, 0)))
            piece = jnp.concatenate([piece, extra], axis=0)
        gathered.append(lax.all_gather(piece, ("tx", "tc"), axis=0))
        offset += width

    teacher = teacher_logits.astype(F32)
    peak = jnp.max(teacher, axis=1)
    shifted = jnp.exp(teacher - peak[:, None])
    mass = jnp.sum(shifted, axis=1)
    probs = shifted.astype(BF16)

    logits = jnp.dot(student_hidden, student_unembed, preferred_element_type=F32)
    speak = jnp.max(logits, axis=1)
    smass = jnp.sum(jnp.exp(logits - speak[:, None]), axis=1)

    extra = gathered[1][:, slots * shard_rows :, :].reshape(8, -1)[:, : 3 * slots * shard_rows]
    sums = jnp.sum(extra.reshape(8, 3, slots, shard_rows).astype(F32), axis=1)
    sums = sums.transpose(1, 0, 2).reshape(slots, block)
    blocks = teacher.shape[1] // block
    live = jnp.arange(slots) < tile_count[0]
    chosen = (tile_pairs[:, 0] % blocks)[:, None] == jnp.arange(blocks)[None, :]
    chosen = jnp.where(live[:, None], chosen, False)
    spread = jnp.sum(jnp.where(chosen[:, :, None], sums[:, None, :], 0.0), axis=0).reshape(-1)
    total = jnp.sum(probs.astype(F32) * spread[None, :], axis=1)

    own = jnp.stack([peak, mass, total, speak, smass, smass, smass, smass])
    column = jnp.stack([own] + [send(own, "vz", step) for step in (1, 2, 3)])
    table = statistics([column] + [send(column, "vy", step) for step in (1, 2, 3)])

    grads, losses = [], []
    offset = 0
    for weights, width in zip(gathered, WIDTHS):
        parts = products(place, tile_pairs, tile_count, probs, weights)
        parts = [parts[0]] + [send(parts[step], "vy", step) for step in (1, 2, 3)]
        parts = merged(place, table, parts)
        parts = [parts[0]] + [send(parts[step], "vz", step) for step in (1, 2, 3)]
        grad, loss = gradients(offset, place, table, logits, parts)
        grads.append(grad)
        losses.append(loss)
        offset += width

    parts = hidden_parts(place, student_unembed, grads, losses)
    first, second = parts[:SIDE], parts[SIDE:]
    first = [first[0]] + [send(first[step], "vy", step) for step in (1, 2, 3)]
    second = [second[0]] + [send(second[step], "vz", step) for step in (1, 2, 3)]
    parts = middle(place, first, second)
    first, second = parts[:SIDE], parts[SIDE:]
    first = [first[0]] + [send(first[step], "vz", step) for step in (1, 2, 3)]
    second = [second[0]] + [send(second[step], "vy", step) for step in (1, 2, 3)]
    grad_hidden, loss = last(place, first, second)
    return grad_hidden, loss[0]


def solution(mesh):
    grid = Mesh(mesh.devices.reshape(SIDE, SIDE, SIDE, 2), ("vy", "vz", "tx", "tc"))
    vocab, tokens = ("vy", "vz"), ("tx", "tc")
    return jax.shard_map(
        shards,
        mesh=grid,
        in_specs=(
            P(tokens, vocab),
            P(tokens, None),
            P(None, vocab),
            P(vocab, tokens, None),
            P(vocab, None),
            P(vocab),
        ),
        out_specs=(P(tokens, vocab), P(tokens)),
        check_vma=False,
    )
```

```python
import functools

import jax
import jax.numpy as jnp
from jax import lax
from jax.experimental import pallas as pl
from jax.experimental.pallas import tpu as pltpu
from jax.sharding import Mesh
from jax.sharding import PartitionSpec as P

F32 = jnp.float32
BF16 = jnp.bfloat16
SIDE = 4
WIDTHS = (256, 256)
VMEM = pl.BlockSpec(memory_space=pltpu.VMEM)
SMEM = pl.BlockSpec(memory_space=pltpu.SMEM)
ANY = pl.BlockSpec(memory_space=pl.ANY)
MIB = 1024 * 1024


def params(mib=16):
    return pltpu.CompilerParams(vmem_limit_bytes=mib * MIB)


def cost(flops, moved, transcendentals=0):
    return pl.CostEstimate(flops=flops, bytes_accessed=moved, transcendentals=transcendentals)


def send(value, axis, step):
    return lax.ppermute(value, axis, [(i, (i + step) % SIDE) for i in range(SIDE)])


def swap(value):
    return lax.ppermute(value, "tc", [(0, 1), (1, 0)])


def thirds(value):
    high = value.astype(BF16).astype(F32)
    rest = value - high
    middle = rest.astype(BF16).astype(F32)
    return high, middle, rest - middle


def prepare_kernel(weights, piece):
    slots, shard_rows, _ = weights.shape
    width = piece.shape[1]
    rows = slots * shard_rows
    piece[0:rows, :] = weights[:, :, 0:width].reshape(rows, width)
    sums = jnp.sum(weights[...].astype(F32), axis=2, keepdims=True).reshape(rows, 1)
    line = jnp.broadcast_to(sums, (rows, 128)).T[0:1]
    lines = jnp.concatenate(list(thirds(line)) + [jnp.zeros((5, rows), F32)], axis=0)
    extra = jnp.concatenate([lines[:, i * 128 : (i + 1) * 128] for i in range(8)], axis=0)
    if width > 128:
        extra = jnp.concatenate([extra, jnp.zeros((64, width - 128), F32)], axis=1)
    piece[rows : rows + 64, :] = extra.astype(BF16)


def prepared(weights, width):
    slots, shard_rows, _ = weights.shape
    return pl.pallas_call(
        prepare_kernel,
        out_shape=jax.ShapeDtypeStruct((slots * shard_rows + 64, width), BF16),
        in_specs=[VMEM],
        out_specs=VMEM,
        compiler_params=params(),
        cost_estimate=cost(2 * weights.size, 3 * weights.size),
        name="prepare_weights",
    )(weights)


def slice_kernel(offset, weights, *refs):
    piece = refs[-1]
    piece[...] = weights[:, :, offset : offset + piece.shape[1]].reshape(piece.shape)


def sliced(weights, offset, width, behind):
    slots, shard_rows, _ = weights.shape
    return pl.pallas_call(
        functools.partial(slice_kernel, offset),
        out_shape=jax.ShapeDtypeStruct((slots * shard_rows, width), BF16),
        in_specs=[VMEM] + [ANY] * len(behind),
        out_specs=VMEM,
        compiler_params=params(),
        cost_estimate=cost(0, 3 * weights.size),
        name="slice_weights",
    )(weights, *behind)


def product_kernel(with_totals, place, pairs, count, probs, *rest):
    pieces, rest = rest[: 2 * SIDE], rest[2 * SIDE :]
    if with_totals:
        before, rest = rest[0], rest[1:]
    outs, rest = rest[:SIDE], rest[SIDE:]
    if with_totals:
        after, sums, line = rest[0], rest[3], rest[4]
        rest = rest[1:]
    weights, total = rest[:2]
    block = weights.shape[0] * 64
    width = weights.shape[2]
    vocab_y = place[0]
    first_block = (vocab_y * SIDE + place[1]) * (probs.shape[1] // block)
    total[...] = jnp.zeros_like(total)
    for step in range(SIDE):
        at = lax.rem(place[2] + SIDE - step, SIDE) * 2
        weights[at + place[3]] = pieces[step][...]
        weights[at + 1 - place[3]] = pieces[SIDE + step][...]
    if with_totals:
        line[...] = jnp.zeros_like(line)
        lane = lax.broadcasted_iota(jnp.int32, (64, 128), 1)
        for pair in range(SIDE):
            even = weights[2 * pair, 1024:1088, 0:128].astype(F32)
            odd = weights[2 * pair + 1, 1024:1088, 0:128].astype(F32)
            lanes = slice(pair * 128, pair * 128 + 128)
            sums[0, :, lanes] = jnp.where(lane < 64, even, pltpu.roll(odd, 64, 1))
            sums[1, :, lanes] = jnp.where(lane < 64, pltpu.roll(even, 64, 1), odd)

    def tile(slot, carry):
        teacher = pairs[slot, 0] - first_block
        owner = pairs[slot, 1] // SIDE
        columns = probs[:, pl.ds(pl.multiple_of(teacher * block, block), block)]
        rows = weights[:, pl.ds(pl.multiple_of(slot * 64, 64), 64), :].reshape(block, width)
        total[owner] += jnp.dot(columns, rows, preferred_element_type=F32)
        if with_totals:
            row_sums = sums[lax.rem(slot, 2), pl.ds(pl.multiple_of(slot // 2 * 8, 8), 8), :]
            line[...] += lax.dot_general(
                row_sums.astype(BF16), columns, (((1,), (1,)), ((), ())), preferred_element_type=F32
            )
        return carry

    lax.fori_loop(0, count[0], tile, 0)
    for step in range(SIDE):
        start = lax.rem(vocab_y + step, SIDE) * SIDE
        for z in range(SIDE):
            outs[step][z] = total[start + z].astype(BF16)
    if with_totals:
        value = line[0:1] + line[1:2] + line[2:3]
        index = lax.broadcasted_iota(jnp.int32, before.shape, 0)
        after[...] = jnp.where(index == 2, jnp.broadcast_to(value, before.shape), before[...])


def products(place, pairs, count, probs, pieces, before=None):
    rows = probs.shape[0]
    depth, width = pieces[0].shape
    outs = [jax.ShapeDtypeStruct((SIDE, rows, width), BF16)] * SIDE
    scratch = [
        pltpu.VMEM((2 * SIDE, depth, width), BF16),
        pltpu.VMEM((SIDE * SIDE, rows, width), F32),
    ]
    extra = []
    if before is not None:
        outs = outs + [jax.ShapeDtypeStruct((8, rows), F32)]
        scratch += [pltpu.VMEM((2, 64, 512), F32), pltpu.VMEM((8, rows), F32)]
        extra = [before]
    return pl.pallas_call(
        functools.partial(product_kernel, before is not None),
        out_shape=outs,
        in_specs=[SMEM, SMEM, SMEM] + [VMEM] * (1 + 2 * SIDE + len(extra)),
        out_specs=[VMEM] * len(outs),
        scratch_shapes=scratch,
        compiler_params=params(24),
        cost_estimate=cost(
            16 * 2 * rows * 512 * width, 2 * probs.size + 16 * depth * width + 32 * rows * width
        ),
        name="tile_products",
    )(place, pairs, count, probs, *pieces, *extra)


def stats_kernel(*refs):
    parts, out = refs[:-1], refs[-1]
    peaks = [part[:, 0, :] for part in parts]
    peak = functools.reduce(jnp.maximum, [jnp.max(v, axis=0, keepdims=True) for v in peaks])
    speaks = [part[:, 3, :] for part in parts]
    speak = functools.reduce(jnp.maximum, [jnp.max(v, axis=0, keepdims=True) for v in speaks])
    mass = jnp.zeros_like(peak)
    total = jnp.zeros_like(peak)
    smass = jnp.zeros_like(peak)
    scales = []
    for part, own, sown in zip(parts, peaks, speaks):
        factor = jnp.exp(own - peak)
        scales.append(factor[0:1])
        mass += jnp.sum(part[:, 1, :] * factor, axis=0, keepdims=True)
        total += jnp.sum(part[:, 2, :] * factor, axis=0, keepdims=True)
        smass += jnp.sum(part[:, 4, :] * jnp.exp(sown - speak), axis=0, keepdims=True)
    total = total / mass
    floored = jnp.maximum(total, 1.0)
    share = total / floored
    table = [s / mass for s in scales] + [1.0 / floored, share / smass, speak, speak + jnp.log(smass)]
    table = jnp.concatenate(table + [jnp.zeros((128 - len(table), peak.shape[1]), F32)], axis=0)
    out[...] = table.T


def statistics(parts):
    rows = parts[0].shape[2]
    return pl.pallas_call(
        stats_kernel,
        out_shape=jax.ShapeDtypeStruct((rows, 128), F32),
        in_specs=[VMEM] * SIDE,
        out_specs=VMEM,
        compiler_params=params(),
        cost_estimate=cost(16 * rows * 20, 64 * 8 * rows, 32 * rows),
        name="row_stats",
    )(*parts)


def merge_kernel(place, table, *refs):
    parts, outs = refs[:SIDE], refs[SIDE:]
    for step in range(SIDE):
        z = lax.rem(place[1] + step, SIDE)
        value = table[:, 0:1] * parts[0][z].astype(F32)
        for d in range(1, SIDE):
            value += table[:, d : d + 1] * parts[d][z].astype(F32)
        outs[step][...] = value.astype(BF16)


def merged(place, table, parts):
    _, rows, width = parts[0].shape
    return pl.pallas_call(
        merge_kernel,
        out_shape=[jax.ShapeDtypeStruct((rows, width), BF16)] * SIDE,
        in_specs=[SMEM] + [VMEM] * (1 + SIDE),
        out_specs=[VMEM] * SIDE,
        compiler_params=params(),
        cost_estimate=cost(32 * rows * width, 40 * rows * width),
        name="merge_targets",
    )(place, table, *parts)


def gradient_kernel(offset, place, table, logits, *refs):
    parts, grad, loss = refs[:SIDE], refs[SIDE], refs[SIDE + 1]
    width = parts[0].shape[1]
    inverse, share, peak, norm = (table[:, c : c + 1] for c in range(4, 8))
    terms = jnp.zeros(parts[0].shape, F32)
    for step in range(SIDE):
        block = lax.rem(place[1] + SIDE - step, SIDE)
        scores = logits[:, pl.ds(pl.multiple_of(block * 512 + offset, 128), width)]
        target = parts[step][...].astype(F32) * inverse
        positive = target > 0
        entropy = jnp.where(positive, target * jnp.log(jnp.where(positive, target, 1.0)), 0.0)
        terms += entropy - target * (scores - norm)
        value = share * jnp.exp(scores - peak) - target
        grad[block] = value.T.astype(BF16)
    loss[...] = jnp.broadcast_to(jnp.sum(terms.T, axis=0, keepdims=True), loss.shape)


def gradients(offset, place, table, logits, parts):
    rows, width = parts[0].shape
    return pl.pallas_call(
        functools.partial(gradient_kernel, offset),
        out_shape=[
            jax.ShapeDtypeStruct((SIDE, width, rows), BF16),
            jax.ShapeDtypeStruct((8, rows), F32),
        ],
        in_specs=[SMEM] + [VMEM] * (2 + SIDE),
        out_specs=[VMEM, VMEM],
        compiler_params=params(),
        cost_estimate=cost(60 * rows * width, 16 * rows * width + 4 * logits.size, 8 * rows * width),
        name="logit_grad",
    )(place, table, logits, *parts)


def hidden_kernel(chunks, place, unembed, *refs):
    grads, losses = refs[:chunks], refs[chunks : 2 * chunks]
    first = refs[2 * chunks : 2 * chunks + SIDE]
    second = refs[2 * chunks + SIDE : 2 * chunks + 2 * SIDE]
    turned = refs[2 * chunks + 2 * SIDE]
    index = pl.program_id(0)
    rows = turned.shape[1]

    @pl.when(index == 0)
    def _():
        offset = 0
        loss = jnp.zeros((1, rows), F32)
        for part, term in zip(grads, losses):
            width = part.shape[1]
            for block in range(SIDE):
                turned[block * 512 + offset : block * 512 + offset + width, :] = part[block]
            offset += width
            loss += term[0:1]
        packed = jnp.concatenate(list(thirds(loss)) + [jnp.zeros((13, rows), F32)], axis=0).astype(BF16)
        for out in first:
            out[512:528, :] = packed

    result = jnp.dot(unembed[...], turned[...], preferred_element_type=F32).astype(BF16)
    for half in range(2):
        owner = index * 2 + half
        owner_y, owner_z = owner // SIDE, lax.rem(owner, SIDE)
        top = result[half * 256 : half * 256 + 128]
        low = result[half * 256 + 128 : half * 256 + 256]
        for step in range(SIDE):

            @pl.when(lax.rem(place[0] + step, SIDE) == owner_y)
            def _():
                first[step][pl.ds(pl.multiple_of(owner_z * 128, 128), 128), :] = top

            @pl.when(lax.rem(place[1] + step, SIDE) == owner_z)
            def _():
                second[step][pl.ds(pl.multiple_of(owner_y * 128, 128), 128), :] = low


def hidden_parts(place, unembed, grads, losses):
    chunks = len(grads)
    width, cols = unembed.shape
    rows = grads[0].shape[2]
    whole = lambda shape: pl.BlockSpec(shape, lambda i: (0,) * len(shape))
    return pl.pallas_call(
        functools.partial(hidden_kernel, chunks),
        grid=(8,),
        out_shape=[jax.ShapeDtypeStruct((528, rows), BF16)] * SIDE
        + [jax.ShapeDtypeStruct((512, rows), BF16)] * SIDE,
        in_specs=[SMEM, pl.BlockSpec((width // 8, cols), lambda i: (i, 0))]
        + [whole(g.shape) for g in grads]
        + [whole(v.shape) for v in losses],
        out_specs=[whole((528, rows))] * SIDE + [whole((512, rows))] * SIDE,
        scratch_shapes=[pltpu.VMEM((cols, rows), BF16)],
        compiler_params=params(),
        cost_estimate=cost(2 * width * cols * rows, 2 * width * cols + 4 * width * rows),
        name="hidden_grad",
    )(place, unembed, *grads, *losses)


def packed_loss(place_index, parts, at, ordered):
    for step in range(SIDE):
        piece = parts[step][at : at + 16, :].astype(F32)
        ordered[lax.rem(place_index + SIDE - step, SIDE)] = piece[0:1] + piece[1:2] + piece[2:3]
    return ((ordered[0] + ordered[1]) + ordered[2]) + ordered[3]


def middle_kernel(place, *refs):
    first, second = refs[:SIDE], refs[SIDE : 2 * SIDE]
    first_out, second_out = refs[2 * SIDE : 3 * SIDE], refs[3 * SIDE : 4 * SIDE]
    ordered = refs[4 * SIDE]
    rows = ordered.shape[2]
    loss = packed_loss(place[0], first, 512, ordered)
    packed = jnp.concatenate(list(thirds(loss)) + [jnp.zeros((13, rows), F32)], axis=0).astype(BF16)
    for step in range(SIDE):
        at = pl.ds(pl.multiple_of(lax.rem(place[1] + step, SIDE) * 128, 128), 128)
        value = first[0][at, :].astype(F32)
        for part in first[1:]:
            value += part[at, :].astype(F32)
        first_out[step][0:128, :] = value.astype(BF16)
        first_out[step][128:144, :] = packed
        at = pl.ds(pl.multiple_of(lax.rem(place[0] + step, SIDE) * 128, 128), 128)
        value = second[0][at, :].astype(F32)
        for part in second[1:]:
            value += part[at, :].astype(F32)
        second_out[step][...] = value.astype(BF16)


def middle(place, first, second):
    rows = first[0].shape[1]
    return pl.pallas_call(
        middle_kernel,
        out_shape=[jax.ShapeDtypeStruct((144, rows), BF16)] * SIDE
        + [jax.ShapeDtypeStruct((128, rows), BF16)] * SIDE,
        in_specs=[SMEM] + [VMEM] * (2 * SIDE),
        out_specs=[VMEM] * (2 * SIDE),
        scratch_shapes=[pltpu.VMEM((SIDE, 1, rows), F32)],
        compiler_params=params(),
        cost_estimate=cost(8 * 512 * rows, 20 * 512 * rows),
        name="merge_grads",
    )(place, *first, *second)


def last_kernel(place, *refs):
    first, second = refs[:SIDE], refs[SIDE : 2 * SIDE]
    grad, loss, ordered = refs[2 * SIDE :]
    loss[...] = jnp.broadcast_to(packed_loss(place[1], first, 128, ordered), loss.shape)
    top = first[0][0:128, :].astype(F32)
    low = second[0][...].astype(F32)
    for a, b in zip(first[1:], second[1:]):
        top += a[0:128, :].astype(F32)
        low += b[...].astype(F32)
    grad[:, 0:128] = top.T.astype(BF16)
    grad[:, 128:256] = low.T.astype(BF16)


def last(place, first, second):
    rows = first[0].shape[1]
    return pl.pallas_call(
        last_kernel,
        out_shape=[jax.ShapeDtypeStruct((rows, 256), BF16), jax.ShapeDtypeStruct((8, rows), F32)],
        in_specs=[SMEM] + [VMEM] * (2 * SIDE),
        out_specs=[VMEM, VMEM],
        scratch_shapes=[pltpu.VMEM((SIDE, 1, rows), F32)],
        compiler_params=params(),
        cost_estimate=cost(8 * 256 * rows, 20 * 256 * rows),
        name="last_sum",
    )(place, *first, *second)


def shards(teacher_logits, student_hidden, student_unembed, tile_weights, tile_pairs, tile_count):
    place = jnp.stack([lax.axis_index("vy"), lax.axis_index("vz"), lax.axis_index("tx"), lax.axis_index("tc")]).astype(jnp.int32)
    teacher = teacher_logits.astype(F32)
    peak = jnp.max(teacher, axis=1)
    shifted = jnp.exp(teacher - peak[:, None])
    mass = jnp.sum(shifted, axis=1)
    probs = shifted.astype(BF16)

    logits = jnp.dot(student_hidden, student_unembed, preferred_element_type=F32)
    speak = jnp.max(logits, axis=1)
    smass = jnp.sum(jnp.exp(logits - speak[:, None]), axis=1)

    gathered = []
    offset = 0
    for index, width in enumerate(WIDTHS):
        if index == 0:
            piece = prepared(tile_weights, width)
        else:
            piece = sliced(tile_weights, offset, width, [pieces[2], mass, smass])
        pieces = [piece] + [send(piece, "tx", step) for step in (1, 2, 3)]
        gathered.append(pieces + [swap(piece) for piece in pieces])
        offset += width

    blank = jnp.zeros_like(peak)
    before = jnp.stack([peak, mass, blank, speak, smass, blank, blank, blank])
    outs = []
    for pieces in gathered:
        outs.append(products(place, tile_pairs, tile_count, probs, pieces, None if outs else before))
    own = outs[0][SIDE]
    column = jnp.stack([own] + [send(own, "vz", step) for step in (1, 2, 3)])
    table = statistics([column] + [send(column, "vy", step) for step in (1, 2, 3)])

    grads, losses = [], []
    offset = 0
    for parts, width in zip(outs, WIDTHS):
        parts = [parts[0]] + [send(parts[step], "vy", step) for step in (1, 2, 3)]
        parts = merged(place, table, parts)
        parts = [parts[0]] + [send(parts[step], "vz", step) for step in (1, 2, 3)]
        grad, loss = gradients(offset, place, table, logits, parts)
        grads.append(grad)
        losses.append(loss)
        offset += width

    parts = hidden_parts(place, student_unembed, grads, losses)
    first, second = parts[:SIDE], parts[SIDE:]
    first = [first[0]] + [send(first[step], "vy", step) for step in (1, 2, 3)]
    second = [second[0]] + [send(second[step], "vz", step) for step in (1, 2, 3)]
    parts = middle(place, first, second)
    first, second = parts[:SIDE], parts[SIDE:]
    first = [first[0]] + [send(first[step], "vz", step) for step in (1, 2, 3)]
    second = [second[0]] + [send(second[step], "vy", step) for step in (1, 2, 3)]
    grad_hidden, loss = last(place, first, second)
    return grad_hidden, loss[0]


def solution(mesh):
    grid = Mesh(mesh.devices.reshape(SIDE, SIDE, SIDE, 2), ("vy", "vz", "tx", "tc"))
    vocab, tokens = ("vy", "vz"), ("tx", "tc")
    return jax.shard_map(
        shards,
        mesh=grid,
        in_specs=(
            P(tokens, vocab),
            P(tokens, None),
            P(None, vocab),
            P(vocab, tokens, None),
            P(vocab, None),
            P(vocab),
        ),
        out_specs=(P(tokens, vocab), P(tokens)),
        check_vma=False,
    )
```

```python
import functools

import jax
import jax.numpy as jnp
from jax import lax
from jax.experimental import pallas as pl
from jax.experimental.pallas import tpu as pltpu
from jax.sharding import Mesh
from jax.sharding import PartitionSpec as P

F32 = jnp.float32
BF16 = jnp.bfloat16
SIDE = 4
VMEM = pl.BlockSpec(memory_space=pltpu.VMEM)
SMEM = pl.BlockSpec(memory_space=pltpu.SMEM)
ANY = pl.BlockSpec(memory_space=pl.ANY)
MIB = 1024 * 1024


def params(mib=16):
    return pltpu.CompilerParams(vmem_limit_bytes=mib * MIB)


def cost(flops, moved, transcendentals=0):
    return pl.CostEstimate(flops=flops, bytes_accessed=moved, transcendentals=transcendentals)


def send(value, axis, step):
    return lax.ppermute(value, axis, [(i, (i + step) % SIDE) for i in range(SIDE)])


def swap(value):
    return lax.ppermute(value, "tc", [(0, 1), (1, 0)])


def thirds(value):
    high = value.astype(BF16).astype(F32)
    rest = value - high
    middle = rest.astype(BF16).astype(F32)
    return high, middle, rest - middle


def prepare_kernel(weights, piece):
    slots, shard_rows, _ = weights.shape
    width = piece.shape[1]
    rows = slots * shard_rows
    piece[0:rows, :] = weights[:, :, 0:width].reshape(rows, width)
    sums = jnp.sum(weights[...].astype(F32), axis=2, keepdims=True).reshape(rows, 1)
    line = jnp.broadcast_to(sums, (rows, 128)).T[0:1]
    lines = jnp.concatenate(list(thirds(line)) + [jnp.zeros((5, rows), F32)], axis=0)
    extra = jnp.concatenate([lines[:, i * 128 : (i + 1) * 128] for i in range(8)], axis=0)
    if width > 128:
        extra = jnp.concatenate([extra, jnp.zeros((64, width - 128), F32)], axis=1)
    piece[rows : rows + 64, :] = extra.astype(BF16)


def prepared(weights, width):
    slots, shard_rows, _ = weights.shape
    return pl.pallas_call(
        prepare_kernel,
        out_shape=jax.ShapeDtypeStruct((slots * shard_rows + 64, width), BF16),
        in_specs=[VMEM],
        out_specs=VMEM,
        compiler_params=params(),
        cost_estimate=cost(2 * weights.size, 3 * weights.size),
        name="prepare_weights",
    )(weights)


def slice_kernel(offset, weights, *refs):
    piece = refs[-1]
    piece[...] = weights[:, :, offset : offset + piece.shape[1]].reshape(piece.shape)


def sliced(weights, offset, width, behind):
    slots, shard_rows, _ = weights.shape
    return pl.pallas_call(
        functools.partial(slice_kernel, offset),
        out_shape=jax.ShapeDtypeStruct((slots * shard_rows, width), BF16),
        in_specs=[VMEM] + [ANY] * len(behind),
        out_specs=VMEM,
        compiler_params=params(),
        cost_estimate=cost(0, 3 * weights.size),
        name="slice_weights",
    )(weights, *behind)


def pack_kernel(number, *refs):
    out = refs[-1]
    at = 0
    for part in refs[:number]:
        out[at : at + part.shape[0], :] = part[...]
        at += part.shape[0]


def packed_pieces(parts, behind):
    depth = sum(part.shape[0] for part in parts)
    width = parts[0].shape[1]
    return pl.pallas_call(
        functools.partial(pack_kernel, len(parts)),
        out_shape=jax.ShapeDtypeStruct((depth, width), BF16),
        in_specs=[VMEM] * len(parts) + [ANY] * len(behind),
        out_specs=VMEM,
        compiler_params=params(),
        cost_estimate=cost(0, 4 * depth * width),
        name="pack_weights",
    )(*parts, *behind)


def halves_kernel(right, left, *refs):
    top, low = refs[-2:]
    top[...] = right[...]
    low[...] = left[...]


def halves(right, left, behind):
    depth, width = right.shape
    shape = (depth // 2, width)
    return pl.pallas_call(
        halves_kernel,
        grid=(1,),
        out_shape=[jax.ShapeDtypeStruct(shape, BF16)] * 2,
        in_specs=[
            pl.BlockSpec(shape, lambda i: (0, 0)),
            pl.BlockSpec(shape, lambda i: (1, 0)),
        ]
        + [ANY] * len(behind),
        out_specs=[pl.BlockSpec(shape, lambda i: (0, 0))] * 2,
        compiler_params=params(),
        cost_estimate=cost(0, 4 * depth * width),
        name="take_halves",
    )(right, left, *behind)


def product_kernel(with_stats, place, pairs, count, probs, mine, other, *rest):
    if with_stats:
        before, rest = rest[0], rest[1:]
    outs, rest = rest[:SIDE], rest[SIDE:]
    weights, total = rest[:2]
    block = weights.shape[0] * 64
    width = weights.shape[2]
    rows = probs.shape[0]
    vocab_y = place[0]
    first_block = (vocab_y * SIDE + place[1]) * (probs.shape[1] // block)
    total[...] = jnp.zeros_like(total)
    depth = weights.shape[1]
    for step in range(SIDE):
        at = lax.rem(place[2] + SIDE - step, SIDE) * 2
        weights[at + place[3]] = mine[step * depth : step * depth + depth, :]
        weights[at + 1 - place[3]] = other[step * depth : step * depth + depth, :]
    if with_stats:
        sums, line = rest[2:]
        line[...] = jnp.zeros_like(line)
        lane = lax.broadcasted_iota(jnp.int32, (64, 128), 1)
        for pair in range(SIDE):
            even = weights[2 * pair, 1024:1088, 0:128].astype(F32)
            odd = weights[2 * pair + 1, 1024:1088, 0:128].astype(F32)
            lanes = slice(pair * 128, pair * 128 + 128)
            sums[0, :, lanes] = jnp.where(lane < 64, even, pltpu.roll(odd, 64, 1))
            sums[1, :, lanes] = jnp.where(lane < 64, pltpu.roll(even, 64, 1), odd)

    def tile(slot, carry):
        teacher = pairs[slot, 0] - first_block
        owner = pairs[slot, 1] // SIDE
        columns = probs[:, pl.ds(pl.multiple_of(teacher * block, block), block)]
        matrix = weights[:, pl.ds(pl.multiple_of(slot * 64, 64), 64), :].reshape(block, width)
        total[owner] += jnp.dot(columns, matrix, preferred_element_type=F32)
        if with_stats:
            row_sums = sums[lax.rem(slot, 2), pl.ds(pl.multiple_of(slot // 2 * 8, 8), 8), :]
            line[...] += lax.dot_general(
                row_sums.astype(BF16), columns, (((1,), (1,)), ((), ())), preferred_element_type=F32
            )
        return carry

    lax.fori_loop(0, count[0], tile, 0)
    for step in range(SIDE):
        start = lax.rem(vocab_y + step, SIDE) * SIDE
        for z in range(SIDE):
            outs[step][z * rows : z * rows + rows, :] = total[start + z].astype(BF16)
    if with_stats:
        sent = line[0:1] + line[1:2] + line[2:3]
        packed = pack_rows([before[0:1], before[1:2], sent, before[3:4], before[4:5]])
        for out in outs:
            out[SIDE * rows : SIDE * rows + 16, :] = packed


def products(place, pairs, count, probs, mine, other, before=None):
    rows = probs.shape[0]
    depth, width = mine.shape[0] // SIDE, mine.shape[1]
    extra = [] if before is None else [before]
    scratch = [
        pltpu.VMEM((2 * SIDE, depth, width), BF16),
        pltpu.VMEM((SIDE * SIDE, rows, width), F32),
    ]
    if extra:
        scratch += [pltpu.VMEM((2, 64, 512), F32), pltpu.VMEM((8, rows), F32)]
    return pl.pallas_call(
        functools.partial(product_kernel, bool(extra)),
        out_shape=[jax.ShapeDtypeStruct((SIDE * rows + 16 * len(extra), width), BF16)] * SIDE,
        in_specs=[SMEM, SMEM, SMEM] + [VMEM] * (3 + len(extra)),
        out_specs=[VMEM] * SIDE,
        scratch_shapes=scratch,
        compiler_params=params(24),
        cost_estimate=cost(
            16 * 2 * rows * 512 * width, 2 * probs.size + 16 * depth * width + 32 * rows * width
        ),
        name="tile_products",
    )(place, pairs, count, probs, mine, other, *extra)


def pack_rows(lines):
    rows = [part for line in lines for part in thirds(line)]
    rows.append(jnp.zeros((16 - len(rows), rows[0].shape[1]), F32))
    return jnp.concatenate(rows, axis=0).astype(BF16)


def unpack_rows(packed, number):
    packed = packed.astype(F32)
    return [
        packed[3 * i : 3 * i + 1] + packed[3 * i + 1 : 3 * i + 2] + packed[3 * i + 2 : 3 * i + 3]
        for i in range(number)
    ]


def joined(stats):
    peak = functools.reduce(jnp.maximum, [line[0] for line in stats])
    speak = functools.reduce(jnp.maximum, [line[3] for line in stats])
    factors = [jnp.exp(line[0] - peak) for line in stats]
    mass = sum(line[1] * factor for line, factor in zip(stats, factors))
    total = sum(line[2] * factor for line, factor in zip(stats, factors))
    smass = sum(line[4] * jnp.exp(line[3] - speak) for line in stats)
    return (peak, mass, total, speak, smass), factors


def columns_of(lines):
    lines = list(lines) + [jnp.zeros((128 - len(lines), lines[0].shape[1]), F32)]
    return jnp.concatenate(lines, axis=0).T


def merge_kernel(with_stats, place, *refs):
    if with_stats:
        parts, outs, kept = refs[:SIDE], refs[SIDE : 2 * SIDE], refs[2 * SIDE]
        rows = outs[0].shape[0] - 16
        stats, factors = joined([unpack_rows(part[SIDE * rows :, :], 5) for part in parts])
        packed = pack_rows(stats)
        for out in outs:
            out[rows : rows + 16, :] = packed
        table = columns_of(factors)
        kept[...] = table
    else:
        table, parts, outs = refs[0][...], refs[1 : 1 + SIDE], refs[1 + SIDE :]
        rows = outs[0].shape[0]
    for step in range(SIDE):
        at = pl.ds(pl.multiple_of(lax.rem(place[1] + step, SIDE) * rows, rows), rows)
        value = table[:, 0:1] * parts[0][at, :].astype(F32)
        for d in range(1, SIDE):
            value += table[:, d : d + 1] * parts[d][at, :].astype(F32)
        outs[step][0:rows, :] = value.astype(BF16)


def merged(place, parts, rows, table=None):
    width = parts[0].shape[1]
    first = table is None
    outs = [jax.ShapeDtypeStruct((rows + (16 if first else 0), width), BF16)] * SIDE
    if first:
        outs = outs + [jax.ShapeDtypeStruct((rows, 128), F32)]
    return pl.pallas_call(
        functools.partial(merge_kernel, first),
        out_shape=outs,
        in_specs=[SMEM] + [VMEM] * (SIDE if first else 1 + SIDE),
        out_specs=[VMEM] * len(outs),
        compiler_params=params(),
        cost_estimate=cost(32 * rows * width, 40 * rows * width),
        name="merge_targets",
    )(place, *([] if first else [table]), *parts)


def gradient_kernel(offset, with_stats, place, logits, *refs):
    if with_stats:
        parts, grad, loss, kept = refs[:SIDE], refs[SIDE], refs[SIDE + 1], refs[SIDE + 2]
        rows = logits.shape[0]
        stats, factors = joined([unpack_rows(part[rows:, :], 5) for part in parts])
        _, mass, total, peak, smass = stats
        total = total / mass
        floored = jnp.maximum(total, 1.0)
        share = total / floored
        scales = [factor / mass / floored for factor in factors]
        table = columns_of(scales + [share / smass, peak, peak + jnp.log(smass)])
        kept[...] = table
    else:
        table, parts, grad, loss = refs[0][...], refs[1 : 1 + SIDE], refs[1 + SIDE], refs[2 + SIDE]
    rows, width = logits.shape[0], parts[0].shape[1]
    share, peak, norm = (table[:, c : c + 1] for c in range(4, 7))
    terms = jnp.zeros((rows, width), F32)
    for step in range(SIDE):
        block = lax.rem(place[1] + SIDE - step, SIDE)
        scores = logits[:, pl.ds(pl.multiple_of(block * 512 + offset, 128), width)]
        target = parts[step][0:rows, :].astype(F32) * table[:, step : step + 1]
        positive = target > 0
        entropy = jnp.where(positive, target * jnp.log(jnp.where(positive, target, 1.0)), 0.0)
        terms += entropy - target * (scores - norm)
        value = share * jnp.exp(scores - peak) - target
        grad[block] = value.T.astype(BF16)
    loss[...] = jnp.broadcast_to(jnp.sum(terms.T, axis=0, keepdims=True), loss.shape)


def gradients(offset, place, logits, parts, table=None):
    rows, width = logits.shape[0], parts[0].shape[1]
    first = table is None
    outs = [jax.ShapeDtypeStruct((SIDE, width, rows), BF16), jax.ShapeDtypeStruct((8, rows), F32)]
    if first:
        outs.append(jax.ShapeDtypeStruct((rows, 128), F32))
    return pl.pallas_call(
        functools.partial(gradient_kernel, offset, first),
        out_shape=outs,
        in_specs=[SMEM] + [VMEM] * (1 + SIDE if first else 2 + SIDE),
        out_specs=[VMEM] * len(outs),
        compiler_params=params(),
        cost_estimate=cost(60 * rows * width, 16 * rows * width + 4 * logits.size, 8 * rows * width),
        name="logit_grad",
    )(place, logits, *([] if first else [table]), *parts)


def early_kernel(*refs):
    unembed, grad, out = refs[:SIDE], refs[SIDE], refs[SIDE + 1]
    result = jnp.dot(unembed[0][...], grad[0], preferred_element_type=F32)
    for block in range(1, SIDE):
        result += jnp.dot(unembed[block][...], grad[block], preferred_element_type=F32)
    out[...] = result


def early_hidden(unembed, grad):
    depth, cols = unembed.shape
    _, width, rows = grad.shape
    per = cols // SIDE // width
    step = depth // 8
    views = [pl.BlockSpec((step, width), lambda i, at=per * b: (i, at)) for b in range(SIDE)]
    return pl.pallas_call(
        early_kernel,
        grid=(8,),
        out_shape=jax.ShapeDtypeStruct((depth, rows), F32),
        in_specs=views + [pl.BlockSpec(grad.shape, lambda i: (0, 0, 0))],
        out_specs=pl.BlockSpec((step, rows), lambda i: (i, 0)),
        compiler_params=params(48),
        cost_estimate=cost(2 * depth * SIDE * width * rows, 2 * depth * SIDE * width + 4 * depth * rows),
        name="early_hidden",
    )(*[unembed] * SIDE, grad)


def late_kernel(half, place, *refs):
    unembed, grad, early = refs[:SIDE], refs[SIDE], refs[SIDE + 1]
    if half == 0:
        losses, outs = refs[SIDE + 2 : SIDE + 4], refs[SIDE + 4 :]
    else:
        losses, outs = (), refs[SIDE + 2 :]
    index = pl.program_id(0)
    rows = grad.shape[2]
    result = early[...].reshape(512, rows)
    for block in range(SIDE):
        result += jnp.dot(
            unembed[block][...].reshape(512, -1), grad[block], preferred_element_type=F32
        )
    result = result.astype(BF16)
    for step in range(SIDE):

        @pl.when(index == step)
        def _():
            outs[step][0:512, :] = result

    if losses:

        @pl.when(index == 0)
        def _():
            packed = pack_rows([losses[0][0:1] + losses[1][0:1]])
            for out in outs:
                out[512:528, :] = packed


def late_hidden(half, place, unembed, grad, early, losses=()):
    depth, cols = unembed.shape
    _, width, rows = grad.shape
    per = cols // SIDE // width
    unembed = unembed.reshape(SIDE, SIDE, 2, 128, cols)
    early = early.reshape(SIDE, SIDE, 2, 128, rows)
    if half == 0:
        shape = lambda n: (1, SIDE, 1, 128, n)
        where = lambda i, p, at: (lax.rem(p[0] + i, SIDE), 0, 0, 0, at)
    else:
        shape = lambda n: (SIDE, 1, 1, 128, n)
        where = lambda i, p, at: (0, lax.rem(p[1] + i, SIDE), 1, 0, at)
    views = [
        pl.BlockSpec(shape(width), lambda i, p, at=per * b + per - 1: where(i, p, at))
        for b in range(SIDE)
    ]
    whole = lambda array: pl.BlockSpec(array.shape, lambda i, p: (0,) * len(array.shape))
    out = jax.ShapeDtypeStruct((512 + (16 if losses else 0), rows), BF16)
    return pl.pallas_call(
        functools.partial(late_kernel, half),
        grid_spec=pltpu.PrefetchScalarGridSpec(
            num_scalar_prefetch=1,
            grid=(SIDE,),
            in_specs=views
            + [whole(grad), pl.BlockSpec(shape(rows), lambda i, p: where(i, p, 0))]
            + [whole(v) for v in losses],
            out_specs=[whole(out)] * SIDE,
        ),
        out_shape=[out] * SIDE,
        compiler_params=params(48),
        cost_estimate=cost(depth * SIDE * width * rows, depth * SIDE * width + 3 * depth * rows),
        name="late_hidden",
    )(place, *[unembed] * SIDE, grad, early, *losses)


def packed_loss(place_index, parts, at, ordered):
    for step in range(SIDE):
        ordered[lax.rem(place_index + SIDE - step, SIDE)] = unpack_rows(parts[step][at : at + 16, :], 1)[0]
    return ((ordered[0] + ordered[1]) + ordered[2]) + ordered[3]


def middle_kernel(half, place, *refs):
    parts, outs = refs[:SIDE], refs[SIDE : 2 * SIDE]
    for step in range(SIDE):
        at = pl.ds(pl.multiple_of(lax.rem(place[1 - half] + step, SIDE) * 128, 128), 128)
        value = parts[0][at, :].astype(F32)
        for part in parts[1:]:
            value += part[at, :].astype(F32)
        outs[step][0:128, :] = value.astype(BF16)
    if half == 0:
        packed = pack_rows([packed_loss(place[0], parts, 512, refs[2 * SIDE])])
        for out in outs:
            out[128:144, :] = packed


def middle(half, place, parts):
    rows = parts[0].shape[1]
    return pl.pallas_call(
        functools.partial(middle_kernel, half),
        out_shape=[jax.ShapeDtypeStruct((128 if half else 144, rows), BF16)] * SIDE,
        in_specs=[SMEM] + [VMEM] * SIDE,
        out_specs=[VMEM] * SIDE,
        scratch_shapes=[] if half else [pltpu.VMEM((SIDE, 1, rows), F32)],
        compiler_params=params(),
        cost_estimate=cost(4 * 512 * rows, 10 * 512 * rows),
        name="merge_grads",
    )(place, *parts)


def last_kernel(place, *refs):
    first, second = refs[:SIDE], refs[SIDE : 2 * SIDE]
    grad, loss, ordered = refs[2 * SIDE :]
    loss[...] = jnp.broadcast_to(packed_loss(place[1], first, 128, ordered), loss.shape)
    top = first[0][0:128, :].astype(F32)
    low = second[0][...].astype(F32)
    for a, b in zip(first[1:], second[1:]):
        top += a[0:128, :].astype(F32)
        low += b[...].astype(F32)
    grad[:, 0:128] = top.T.astype(BF16)
    grad[:, 128:256] = low.T.astype(BF16)


def last(place, first, second):
    rows = first[0].shape[1]
    return pl.pallas_call(
        last_kernel,
        out_shape=[jax.ShapeDtypeStruct((rows, 256), BF16), jax.ShapeDtypeStruct((8, rows), F32)],
        in_specs=[SMEM] + [VMEM] * (2 * SIDE),
        out_specs=[VMEM, VMEM],
        scratch_shapes=[pltpu.VMEM((SIDE, 1, rows), F32)],
        compiler_params=params(),
        cost_estimate=cost(8 * 256 * rows, 20 * 256 * rows),
        name="last_sum",
    )(place, *first, *second)


def spread(parts, axis):
    return [parts[0]] + [send(parts[step], axis, step) for step in (1, 2, 3)]


def shards(teacher_logits, student_hidden, student_unembed, tile_weights, tile_pairs, tile_count):
    place = jnp.stack([lax.axis_index("vy"), lax.axis_index("vz"), lax.axis_index("tx"), lax.axis_index("tc")]).astype(jnp.int32)
    rows = teacher_logits.shape[0]
    teacher = teacher_logits.astype(F32)
    peak = jnp.max(teacher, axis=1)
    shifted = jnp.exp(teacher - peak[:, None])
    mass = jnp.sum(shifted, axis=1)
    probs = shifted.astype(BF16)

    logits = jnp.dot(student_hidden, student_unembed, preferred_element_type=F32)
    speak = jnp.max(logits, axis=1)
    smass = jnp.sum(jnp.exp(logits - speak[:, None]), axis=1)

    blank = jnp.zeros_like(peak)
    before = jnp.stack([peak, mass, blank, speak, smass, blank, blank, blank])

    width = tile_weights.shape[2] // 2
    piece = prepared(tile_weights, width)
    mine = packed_pieces(spread([piece] * SIDE, "tx"), [mass, smass])
    other = swap(mine)
    parts = products(place, tile_pairs, tile_count, probs, mine, other, before)

    piece = sliced(tile_weights, width, width, [mine])
    right, left = send(piece, "tx", 1), send(piece, "tx", 3)
    top, low = halves(right, left, [parts[0]])
    parts = spread(parts, "vy")
    pieces = [piece, right, send(top, "tx", 1), send(low, "tx", 3), left]
    mine = packed_pieces(pieces, [parts[1], parts[3]])
    later = products(place, tile_pairs, tile_count, probs, mine, swap(mine))

    *parts, factors = merged(place, parts, rows)
    early_grad, early_loss, table = gradients(0, place, logits, spread(parts, "vz"))
    early = early_hidden(student_unembed, early_grad)
    parts = merged(place, spread(later, "vy"), rows, factors)
    late_grad, late_loss = gradients(width, place, logits, spread(parts, "vz"), table)

    first = late_hidden(0, place, student_unembed, late_grad, early, (early_loss, late_loss))
    first = middle(0, place, spread(first, "vy"))
    second = late_hidden(1, place, student_unembed, late_grad, early)
    second = middle(1, place, spread(second, "vz"))
    grad_hidden, loss = last(place, spread(first, "vz"), spread(second, "vy"))
    return grad_hidden, loss[0]


def solution(mesh):
    grid = Mesh(mesh.devices.reshape(SIDE, SIDE, SIDE, 2), ("vy", "vz", "tx", "tc"))
    vocab, tokens = ("vy", "vz"), ("tx", "tc")
    return jax.shard_map(
        shards,
        mesh=grid,
        in_specs=(
            P(tokens, vocab),
            P(tokens, None),
            P(None, vocab),
            P(vocab, tokens, None),
            P(vocab, None),
            P(vocab),
        ),
        out_specs=(P(tokens, vocab), P(tokens)),
        check_vma=False,
    )
```

```python
import functools

import jax
import jax.numpy as jnp
from jax import lax
from jax.experimental import pallas as pl
from jax.experimental.pallas import tpu as pltpu
from jax.sharding import Mesh
from jax.sharding import PartitionSpec as P

F32 = jnp.float32
BF16 = jnp.bfloat16
SIDE = 4
VMEM = pl.BlockSpec(memory_space=pltpu.VMEM)
SMEM = pl.BlockSpec(memory_space=pltpu.SMEM)
ANY = pl.BlockSpec(memory_space=pl.ANY)
MIB = 1024 * 1024


def params(mib=16):
    return pltpu.CompilerParams(vmem_limit_bytes=mib * MIB)


def cost(flops, moved, transcendentals=0):
    return pl.CostEstimate(flops=flops, bytes_accessed=moved, transcendentals=transcendentals)


def send(value, axis, step):
    return lax.ppermute(value, axis, [(i, (i + step) % SIDE) for i in range(SIDE)])


def swap(value):
    return lax.ppermute(value, "tc", [(0, 1), (1, 0)])


def thirds(value):
    high = value.astype(BF16).astype(F32)
    rest = value - high
    middle = rest.astype(BF16).astype(F32)
    return high, middle, rest - middle


def prepare_kernel(weights, piece):
    slots, shard_rows, _ = weights.shape
    width = piece.shape[1]
    rows = slots * shard_rows
    piece[0:rows, :] = weights[:, :, 0:width].reshape(rows, width)
    sums = jnp.sum(weights[...].astype(F32), axis=2, keepdims=True).reshape(rows, 1)
    line = jnp.broadcast_to(sums, (rows, 128)).T[0:1]
    lines = jnp.concatenate(list(thirds(line)) + [jnp.zeros((5, rows), F32)], axis=0)
    extra = jnp.concatenate([lines[:, i * 128 : (i + 1) * 128] for i in range(8)], axis=0)
    if width > 128:
        extra = jnp.concatenate([extra, jnp.zeros((64, width - 128), F32)], axis=1)
    piece[rows : rows + 64, :] = extra.astype(BF16)


def prepared(weights, width):
    slots, shard_rows, _ = weights.shape
    return pl.pallas_call(
        prepare_kernel,
        out_shape=jax.ShapeDtypeStruct((slots * shard_rows + 64, width), BF16),
        in_specs=[VMEM],
        out_specs=VMEM,
        compiler_params=params(),
        cost_estimate=cost(2 * weights.size, 3 * weights.size),
        name="prepare_weights",
    )(weights)


def slice_kernel(offset, weights, *refs):
    piece = refs[-1]
    piece[...] = weights[:, :, offset : offset + piece.shape[1]].reshape(piece.shape)


def sliced(weights, offset, width, behind):
    slots, shard_rows, _ = weights.shape
    return pl.pallas_call(
        functools.partial(slice_kernel, offset),
        out_shape=jax.ShapeDtypeStruct((slots * shard_rows, width), BF16),
        in_specs=[VMEM] + [ANY] * len(behind),
        out_specs=VMEM,
        compiler_params=params(),
        cost_estimate=cost(0, 3 * weights.size),
        name="slice_weights",
    )(weights, *behind)


def pack_kernel(number, *refs):
    out = refs[-1]
    at = 0
    for part in refs[:number]:
        out[at : at + part.shape[0], :] = part[...]
        at += part.shape[0]


def packed_pieces(parts, behind):
    depth = sum(part.shape[0] for part in parts)
    width = parts[0].shape[1]
    return pl.pallas_call(
        functools.partial(pack_kernel, len(parts)),
        out_shape=jax.ShapeDtypeStruct((depth, width), BF16),
        in_specs=[VMEM] * len(parts) + [ANY] * len(behind),
        out_specs=VMEM,
        compiler_params=params(),
        cost_estimate=cost(0, 4 * depth * width),
        name="pack_weights",
    )(*parts, *behind)


def halves_kernel(right, left, *refs):
    top, low = refs[-2:]
    top[...] = right[...]
    low[...] = left[...]


def halves(right, left, behind):
    depth, width = right.shape
    shape = (depth // 2, width)
    return pl.pallas_call(
        halves_kernel,
        grid=(1,),
        out_shape=[jax.ShapeDtypeStruct(shape, BF16)] * 2,
        in_specs=[
            pl.BlockSpec(shape, lambda i: (0, 0)),
            pl.BlockSpec(shape, lambda i: (1, 0)),
        ]
        + [ANY] * len(behind),
        out_specs=[pl.BlockSpec(shape, lambda i: (0, 0))] * 2,
        compiler_params=params(),
        cost_estimate=cost(0, 4 * depth * width),
        name="take_halves",
    )(right, left, *behind)


def product_kernel(with_stats, place, pairs, count, probs, mine, other, *rest):
    if with_stats:
        before, rest = rest[0], rest[1:]
    outs, rest = rest[:SIDE], rest[SIDE:]
    weights, total = rest[:2]
    block = weights.shape[0] * 64
    width = weights.shape[2]
    rows = probs.shape[0]
    vocab_y = place[0]
    first_block = (vocab_y * SIDE + place[1]) * (probs.shape[1] // block)
    total[...] = jnp.zeros_like(total)
    depth = weights.shape[1]
    for step in range(SIDE):
        at = lax.rem(place[2] + SIDE - step, SIDE) * 2
        weights[at + place[3]] = mine[step * depth : step * depth + depth, :]
        weights[at + 1 - place[3]] = other[step * depth : step * depth + depth, :]
    if with_stats:
        sums, line = rest[2:]
        line[...] = jnp.zeros_like(line)
        lane = lax.broadcasted_iota(jnp.int32, (64, 128), 1)
        for pair in range(SIDE):
            even = weights[2 * pair, 1024:1088, 0:128].astype(F32)
            odd = weights[2 * pair + 1, 1024:1088, 0:128].astype(F32)
            lanes = slice(pair * 128, pair * 128 + 128)
            sums[0, :, lanes] = jnp.where(lane < 64, even, pltpu.roll(odd, 64, 1))
            sums[1, :, lanes] = jnp.where(lane < 64, pltpu.roll(even, 64, 1), odd)

    def tile(slot, carry):
        teacher = pairs[slot, 0] - first_block
        owner = pairs[slot, 1] // SIDE
        columns = probs[:, pl.ds(pl.multiple_of(teacher * block, block), block)]
        matrix = weights[:, pl.ds(pl.multiple_of(slot * 64, 64), 64), :].reshape(block, width)
        total[owner] += jnp.dot(columns, matrix, preferred_element_type=F32)
        if with_stats:
            row_sums = sums[lax.rem(slot, 2), pl.ds(pl.multiple_of(slot // 2 * 8, 8), 8), :]
            line[...] += lax.dot_general(
                row_sums.astype(BF16), columns, (((1,), (1,)), ((), ())), preferred_element_type=F32
            )
        return carry

    lax.fori_loop(0, count[0], tile, 0)
    for step in range(SIDE):
        start = lax.rem(vocab_y + step, SIDE) * SIDE
        for z in range(SIDE):
            outs[step][z * rows : z * rows + rows, :] = total[start + z].astype(BF16)
    if with_stats:
        sent = line[0:1] + line[1:2] + line[2:3]
        packed = pack_rows([before[0:1], before[1:2], sent, before[3:4], before[4:5]])
        for out in outs:
            out[SIDE * rows : SIDE * rows + 16, :] = packed


def products(place, pairs, count, probs, mine, other, before=None):
    rows = probs.shape[0]
    depth, width = mine.shape[0] // SIDE, mine.shape[1]
    extra = [] if before is None else [before]
    scratch = [
        pltpu.VMEM((2 * SIDE, depth, width), BF16),
        pltpu.VMEM((SIDE * SIDE, rows, width), F32),
    ]
    if extra:
        scratch += [pltpu.VMEM((2, 64, 512), F32), pltpu.VMEM((8, rows), F32)]
    return pl.pallas_call(
        functools.partial(product_kernel, bool(extra)),
        out_shape=[jax.ShapeDtypeStruct((SIDE * rows + 16 * len(extra), width), BF16)] * SIDE,
        in_specs=[SMEM, SMEM, SMEM] + [VMEM] * (3 + len(extra)),
        out_specs=[VMEM] * SIDE,
        scratch_shapes=scratch,
        compiler_params=params(24),
        cost_estimate=cost(
            16 * 2 * rows * 512 * width, 2 * probs.size + 16 * depth * width + 32 * rows * width
        ),
        name="tile_products",
    )(place, pairs, count, probs, mine, other, *extra)


def pack_rows(lines):
    rows = [part for line in lines for part in thirds(line)]
    rows.append(jnp.zeros((16 - len(rows), rows[0].shape[1]), F32))
    return jnp.concatenate(rows, axis=0).astype(BF16)


def unpack_rows(packed, number):
    packed = packed.astype(F32)
    return [
        packed[3 * i : 3 * i + 1] + packed[3 * i + 1 : 3 * i + 2] + packed[3 * i + 2 : 3 * i + 3]
        for i in range(number)
    ]


def joined(stats):
    peak = functools.reduce(jnp.maximum, [line[0] for line in stats])
    speak = functools.reduce(jnp.maximum, [line[3] for line in stats])
    factors = [jnp.exp(line[0] - peak) for line in stats]
    mass = sum(line[1] * factor for line, factor in zip(stats, factors))
    total = sum(line[2] * factor for line, factor in zip(stats, factors))
    smass = sum(line[4] * jnp.exp(line[3] - speak) for line in stats)
    return (peak, mass, total, speak, smass), factors


def columns_of(lines):
    lines = list(lines) + [jnp.zeros((128 - len(lines), lines[0].shape[1]), F32)]
    return jnp.concatenate(lines, axis=0).T


def merge_kernel(with_stats, place, *refs):
    if with_stats:
        parts, outs, kept = refs[:SIDE], refs[-1 - SIDE : -1], refs[-1]
        rows = outs[0].shape[0] - 16
        stats, factors = joined([unpack_rows(part[SIDE * rows :, :], 5) for part in parts])
        packed = pack_rows(stats)
        for out in outs:
            out[rows : rows + 16, :] = packed
        table = columns_of(factors)
        kept[...] = table
    else:
        table, parts, outs = refs[0][...], refs[1 : 1 + SIDE], refs[-SIDE:]
        rows = outs[0].shape[0]
    for step in range(SIDE):
        at = pl.ds(pl.multiple_of(lax.rem(place[1] + step, SIDE) * rows, rows), rows)
        value = table[:, 0:1] * parts[0][at, :].astype(F32)
        for d in range(1, SIDE):
            value += table[:, d : d + 1] * parts[d][at, :].astype(F32)
        outs[step][0:rows, :] = value.astype(BF16)


def merged(place, parts, rows, table=None, behind=()):
    width = parts[0].shape[1]
    first = table is None
    outs = [jax.ShapeDtypeStruct((rows + (16 if first else 0), width), BF16)] * SIDE
    if first:
        outs = outs + [jax.ShapeDtypeStruct((rows, 128), F32)]
    return pl.pallas_call(
        functools.partial(merge_kernel, first),
        out_shape=outs,
        in_specs=[SMEM] + [VMEM] * (SIDE if first else 1 + SIDE) + [ANY] * len(behind),
        out_specs=[VMEM] * len(outs),
        compiler_params=params(),
        cost_estimate=cost(rows * width, rows * width),
        name="merge_targets",
    )(place, *([] if first else [table]), *parts, *behind)


def gradient_kernel(offset, with_stats, place, logits, *refs):
    if with_stats:
        parts, (grad, loss, kept) = refs[:SIDE], refs[-3:]
        rows = logits.shape[0]
        stats, factors = joined([unpack_rows(part[rows:, :], 5) for part in parts])
        _, mass, total, peak, smass = stats
        total = total / mass
        floored = jnp.maximum(total, 1.0)
        share = total / floored
        scales = [factor / mass / floored for factor in factors]
        table = columns_of(scales + [share / smass, peak, peak + jnp.log(smass)])
        kept[...] = table
    else:
        table, loss, parts, grad = refs[0][...], refs[1], refs[2 : 2 + SIDE], refs[-1]
    rows, width = logits.shape[0], parts[0].shape[1]
    share, peak, norm = (table[:, c : c + 1] for c in range(4, 7))
    terms = jnp.zeros((rows, width), F32)
    for step in range(SIDE):
        block = lax.rem(place[1] + SIDE - step, SIDE)
        scores = logits[:, pl.ds(pl.multiple_of(block * 512 + offset, 128), width)]
        target = parts[step][0:rows, :].astype(F32) * table[:, step : step + 1]
        positive = target > 0
        entropy = jnp.where(positive, target * jnp.log(jnp.where(positive, target, 1.0)), 0.0)
        terms += entropy - target * (scores - norm)
        value = share * jnp.exp(scores - peak) - target
        at = pl.ds(pl.multiple_of(block * width, width), width)
        grad[at, :] = value.T.astype(BF16)
    sum_of_terms = jnp.sum(terms.T, axis=0, keepdims=True)
    if with_stats:
        loss[...] = jnp.broadcast_to(sum_of_terms, loss.shape)
    else:
        grad[SIDE * width :, :] = pack_rows([sum_of_terms + loss[0:1]])


def gradients(offset, place, logits, parts, before=(), behind=()):
    rows, width = logits.shape[0], parts[0].shape[1]
    first = not before
    outs = [jax.ShapeDtypeStruct((SIDE * width + (0 if first else 16), rows), BF16)]
    if first:
        outs.append(jax.ShapeDtypeStruct((8, rows), F32))
        outs.append(jax.ShapeDtypeStruct((rows, 128), F32))
    return pl.pallas_call(
        functools.partial(gradient_kernel, offset, first),
        out_shape=outs,
        in_specs=[SMEM] + [VMEM] * (1 + SIDE + len(before)) + [ANY] * len(behind),
        out_specs=[VMEM] * len(outs),
        compiler_params=params(),
        cost_estimate=cost(rows * width, rows * width),
        name="logit_grad",
    )(place, logits, *before, *parts, *behind)


def both_cores(core, mine, other, depth, out):
    rows = mine.shape[1]
    out[:, pl.ds(pl.multiple_of(core * rows, rows), rows)] = mine[0:depth, :]
    out[:, pl.ds(pl.multiple_of((1 - core) * rows, rows), rows)] = other[0:depth, :]


def early_kernel(place, *refs):
    unembed = refs[:SIDE]
    mine, other, out, stage, both = refs[SIDE:]
    depth = both.shape[0]
    width = depth // SIDE

    @pl.when(pl.program_id(0) == 0)
    def _():
        both_cores(place[3], mine, other, depth, both)

    for owner in range(SIDE):
        rows = slice(owner * 128, owner * 128 + 128)
        block = unembed[owner][...].reshape(128, 2 * depth)
        now = [block[:, 2 * width * b : 2 * width * b + width] for b in range(SIDE)]
        later = [block[:, 2 * width * b + width : 2 * width * (b + 1)] for b in range(SIDE)]
        stage[rows, :] = jnp.concatenate(later, axis=1)
        out[rows, :] = jnp.dot(jnp.concatenate(now, axis=1), both[...], preferred_element_type=F32)


def early_hidden(place, unembed, mine, other):
    depth, cols = unembed.shape
    width, rows = mine.shape
    unembed = unembed.reshape(SIDE, SIDE, 2, 128, cols)

    def where(i, p, k):
        first = p[3] == 0
        return (jnp.where(first, i, k), jnp.where(first, k, i), p[3], 0, 0)

    views = [
        pl.BlockSpec((1, 1, 1, 128, cols), lambda i, p, k=k: where(i, p, k)) for k in range(SIDE)
    ]
    whole = pl.BlockSpec((width, rows), lambda i, p: (0, 0))
    outs = [
        jax.ShapeDtypeStruct((depth // 2, 2 * rows), F32),
        jax.ShapeDtypeStruct((depth // 2, width), BF16),
    ]
    return pl.pallas_call(
        early_kernel,
        grid_spec=pltpu.PrefetchScalarGridSpec(
            num_scalar_prefetch=1,
            grid=(SIDE,),
            in_specs=views + [whole, whole],
            out_specs=[pl.BlockSpec((512, v.shape[1]), lambda i, p: (i, 0)) for v in outs],
            scratch_shapes=[pltpu.VMEM((width, 2 * rows), BF16)],
        ),
        out_shape=outs,
        compiler_params=params(24),
        cost_estimate=cost(2 * depth * width * rows, depth * cols + 6 * depth * rows),
        name="early_hidden",
    )(place, *[unembed] * SIDE, mine, other)


def late_kernel(place, stage, mine, other, early, *refs):
    outs, both = refs[:SIDE], refs[SIDE]
    depth = both.shape[0]
    rows = mine.shape[1]
    both_cores(place[3], mine, other, depth, both)
    for step in range(SIDE):
        at = pl.ds(pl.multiple_of(lax.rem(place[4] + step, SIDE) * 512, 512), 512)
        result = early[at, :] + jnp.dot(stage[at, :], both[...], preferred_element_type=F32)
        outs[step][0:512, :] = result.astype(BF16)
        for part, core in ((mine, place[3]), (other, 1 - place[3])):
            lanes = pl.ds(pl.multiple_of(core * rows, rows), rows)
            outs[step][512:528, lanes] = part[depth : depth + 16, :]


def late_hidden(place, stage, mine, other, early):
    width = stage.shape[1]
    rows = early.shape[1]
    return pl.pallas_call(
        late_kernel,
        out_shape=[jax.ShapeDtypeStruct((528, rows), BF16)] * SIDE,
        in_specs=[SMEM] + [VMEM] * 4,
        out_specs=[VMEM] * SIDE,
        scratch_shapes=[pltpu.VMEM((width, rows), BF16)],
        compiler_params=params(24),
        cost_estimate=cost(4096 * width * rows, 4096 * width + 6 * 2048 * rows),
        name="late_hidden",
    )(place, stage, mine, other, early)


def packed_loss(index, parts, at, ordered):
    for step in range(SIDE):
        ordered[lax.rem(index + SIDE - step, SIDE)] = unpack_rows(parts[step][at : at + 16, :], 1)[0]
    return ((ordered[0] + ordered[1]) + ordered[2]) + ordered[3]


def middle_kernel(place, *refs):
    parts, outs, ordered = refs[:SIDE], refs[SIDE : 2 * SIDE], refs[2 * SIDE]
    packed = pack_rows([packed_loss(place[4], parts, 512, ordered)])
    for step in range(SIDE):
        at = pl.ds(pl.multiple_of(lax.rem(place[5] + step, SIDE) * 128, 128), 128)
        value = parts[0][at, :].astype(F32)
        for part in parts[1:]:
            value += part[at, :].astype(F32)
        outs[step][0:128, :] = value.astype(BF16)
        outs[step][128:144, :] = packed


def middle(place, parts):
    rows = parts[0].shape[1]
    return pl.pallas_call(
        middle_kernel,
        out_shape=[jax.ShapeDtypeStruct((144, rows), BF16)] * SIDE,
        in_specs=[SMEM] + [VMEM] * SIDE,
        out_specs=[VMEM] * SIDE,
        scratch_shapes=[pltpu.VMEM((SIDE, 1, rows), F32)],
        compiler_params=params(),
        cost_estimate=cost(4 * 512 * rows, 10 * 512 * rows),
        name="merge_grads",
    )(place, *parts)


def total_kernel(place, *refs):
    parts = refs[:SIDE]
    keep, give, loss, ordered = refs[SIDE:]
    rows = keep.shape[1]
    mine = pl.ds(pl.multiple_of(place[3] * rows, rows), rows)
    other = pl.ds(pl.multiple_of((1 - place[3]) * rows, rows), rows)
    ordered[4] = packed_loss(place[5], parts, 128, ordered)
    loss[...] = jnp.broadcast_to(ordered[4, :, mine], loss.shape)
    for lanes, out in ((other, give), (mine, keep)):
        value = parts[0][0:128, lanes].astype(F32)
        for part in parts[1:]:
            value += part[0:128, lanes].astype(F32)
        out[...] = value.astype(BF16)


def totals(place, parts):
    rows = parts[0].shape[1] // 2
    half = jax.ShapeDtypeStruct((128, rows), BF16)
    return pl.pallas_call(
        total_kernel,
        out_shape=[half, half, jax.ShapeDtypeStruct((8, rows), F32)],
        in_specs=[SMEM] + [VMEM] * SIDE,
        out_specs=[VMEM] * 3,
        scratch_shapes=[pltpu.VMEM((SIDE + 1, 1, 2 * rows), F32)],
        compiler_params=params(),
        cost_estimate=cost(8 * 128 * rows, 20 * 128 * rows),
        name="sum_grads",
    )(place, *parts)


def turn_kernel(place, keep, given, grad):
    mine = pl.ds(pl.multiple_of(place[3] * 128, 128), 128)
    other = pl.ds(pl.multiple_of((1 - place[3]) * 128, 128), 128)
    grad[:, mine] = keep[...].astype(F32).T.astype(BF16)
    grad[:, other] = given[...].astype(F32).T.astype(BF16)


def turned(place, keep, given):
    rows = keep.shape[1]
    return pl.pallas_call(
        turn_kernel,
        out_shape=jax.ShapeDtypeStruct((rows, 256), BF16),
        in_specs=[SMEM, VMEM, VMEM],
        out_specs=VMEM,
        compiler_params=params(),
        cost_estimate=cost(0, 4 * 256 * rows),
        name="turn_grads",
    )(place, keep, given)


def spread(parts, axis):
    return [parts[0]] + [send(parts[step], axis, step) for step in (1, 2, 3)]


def crossed(parts, first):
    def target(y, z, core, step):
        if (core == 0) == first:
            y = (y + step) % SIDE
        else:
            z = (z + step) % SIDE
        return (y * SIDE + z) * 2 + core

    places = [(y, z, core) for y in range(SIDE) for z in range(SIDE) for core in range(2)]
    received = [parts[0]]
    for step in (1, 2, 3):
        pairs = [(i, target(*at, step)) for i, at in enumerate(places)]
        received.append(lax.ppermute(parts[step], ("vy", "vz", "tc"), pairs))
    return received


def shards(teacher_logits, student_hidden, student_unembed, tile_weights, tile_pairs, tile_count):
    y, z, x, core = (lax.axis_index(name) for name in ("vy", "vz", "tx", "tc"))
    crossing = [jnp.where(core == 0, y, z), jnp.where(core == 0, z, y)]
    place = jnp.stack([y, z, x, core] + crossing).astype(jnp.int32)
    rows = teacher_logits.shape[0]
    teacher = teacher_logits.astype(F32)
    peak = jnp.max(teacher, axis=1)
    shifted = jnp.exp(teacher - peak[:, None])
    mass = jnp.sum(shifted, axis=1)
    probs = shifted.astype(BF16)

    logits = jnp.dot(student_hidden, student_unembed, preferred_element_type=F32)
    speak = jnp.max(logits, axis=1)
    smass = jnp.sum(jnp.exp(logits - speak[:, None]), axis=1)

    blank = jnp.zeros_like(peak)
    before = jnp.stack([peak, mass, blank, speak, smass, blank, blank, blank])

    width = tile_weights.shape[2] // 2
    piece = prepared(tile_weights, width)
    mine = packed_pieces(spread([piece] * SIDE, "tx"), [mass, smass])
    other = swap(mine)
    parts = products(place, tile_pairs, tile_count, probs, mine, other, before)

    piece = sliced(tile_weights, width, width, [mine])
    right, left = send(piece, "tx", 1), send(piece, "tx", 3)
    top, low = halves(right, left, [parts[0]])
    parts = spread(parts, "vy")
    pieces = [piece, right, send(top, "tx", 1), send(low, "tx", 3), left]
    mine = packed_pieces(pieces, [parts[1], parts[3]])
    later = products(place, tile_pairs, tile_count, probs, mine, swap(mine))

    *parts, factors = merged(place, parts, rows, None, [later[0]])
    later = spread(later, "vy")
    grad, *before = gradients(0, place, logits, spread(parts, "vz"), (), later[1:])
    early, stage = early_hidden(place, student_unembed, grad, swap(grad))
    before = [before[1], before[0]]
    parts = merged(place, later, rows, factors)
    (grad,) = gradients(width, place, logits, spread(parts, "vz"), before, [early])

    parts = late_hidden(place, stage, grad, swap(grad), early)
    parts = middle(place, crossed(parts, True))
    keep, give, loss = totals(place, crossed(parts, False))
    return turned(place, keep, swap(give)), loss[0]


def solution(mesh):
    grid = Mesh(mesh.devices.reshape(SIDE, SIDE, SIDE, 2), ("vy", "vz", "tx", "tc"))
    vocab, tokens = ("vy", "vz"), ("tx", "tc")
    return jax.shard_map(
        shards,
        mesh=grid,
        in_specs=(
            P(tokens, vocab),
            P(tokens, None),
            P(None, vocab),
            P(vocab, tokens, None),
            P(vocab, None),
            P(vocab),
        ),
        out_specs=(P(tokens, vocab), P(tokens)),
        check_vma=False,
    )
```

```python
import functools

import jax
import jax.numpy as jnp
from jax import lax
from jax.experimental import pallas as pl
from jax.experimental.pallas import tpu as pltpu
from jax.sharding import Mesh
from jax.sharding import PartitionSpec as P

F32 = jnp.float32
BF16 = jnp.bfloat16
SIDE = 4
VMEM = pl.BlockSpec(memory_space=pltpu.VMEM)
SMEM = pl.BlockSpec(memory_space=pltpu.SMEM)
ANY = pl.BlockSpec(memory_space=pl.ANY)
MIB = 1024 * 1024


def params(mib=16):
    return pltpu.CompilerParams(vmem_limit_bytes=mib * MIB)


def cost(flops, moved, transcendentals=0):
    return pl.CostEstimate(flops=flops, bytes_accessed=moved, transcendentals=transcendentals)


def send(value, axis, step):
    return lax.ppermute(value, axis, [(i, (i + step) % SIDE) for i in range(SIDE)])


def swap(value):
    return lax.ppermute(value, "tc", [(0, 1), (1, 0)])


def thirds(value):
    high = value.astype(BF16).astype(F32)
    rest = value - high
    middle = rest.astype(BF16).astype(F32)
    return high, middle, rest - middle


def prepare_kernel(weights, piece):
    slots, shard_rows, _ = weights.shape
    width = piece.shape[1]
    rows = slots * shard_rows
    piece[0:rows, :] = weights[:, :, 0:width].reshape(rows, width)
    sums = jnp.sum(weights[...].astype(F32), axis=2, keepdims=True).reshape(rows, 1)
    line = jnp.broadcast_to(sums, (rows, 128)).T[0:1]
    lines = jnp.concatenate(list(thirds(line)) + [jnp.zeros((5, rows), F32)], axis=0)
    extra = jnp.concatenate([lines[:, i * 128 : (i + 1) * 128] for i in range(8)], axis=0)
    if width > 128:
        extra = jnp.concatenate([extra, jnp.zeros((64, width - 128), F32)], axis=1)
    piece[rows : rows + 64, :] = extra.astype(BF16)


def prepared(weights, width):
    slots, shard_rows, _ = weights.shape
    return pl.pallas_call(
        prepare_kernel,
        out_shape=jax.ShapeDtypeStruct((slots * shard_rows + 64, width), BF16),
        in_specs=[VMEM],
        out_specs=VMEM,
        compiler_params=params(),
        cost_estimate=cost(2 * weights.size, 3 * weights.size),
        name="prepare_weights",
    )(weights)


def slice_kernel(offset, weights, *refs):
    piece = refs[-1]
    piece[...] = weights[:, :, offset : offset + piece.shape[1]].reshape(piece.shape)


def sliced(weights, offset, width, behind):
    slots, shard_rows, _ = weights.shape
    return pl.pallas_call(
        functools.partial(slice_kernel, offset),
        out_shape=jax.ShapeDtypeStruct((slots * shard_rows, width), BF16),
        in_specs=[VMEM] + [ANY] * len(behind),
        out_specs=VMEM,
        compiler_params=params(),
        cost_estimate=cost(0, 3 * weights.size),
        name="slice_weights",
    )(weights, *behind)


def gate_kernel(*refs):
    pass


def gated(parts, behind):
    return pl.pallas_call(
        gate_kernel,
        out_shape=[jax.ShapeDtypeStruct(part.shape, part.dtype) for part in parts],
        in_specs=[ANY] * (len(parts) + len(behind)),
        out_specs=[ANY] * len(parts),
        input_output_aliases={i: i for i in range(len(parts))},
        compiler_params=params(),
        cost_estimate=cost(0, 0),
        name="gate",
    )(*parts, *behind)


def pack_kernel(number, *refs):
    out = refs[-1]
    at = 0
    for part in refs[:number]:
        out[at : at + part.shape[0], :] = part[...]
        at += part.shape[0]


def packed_pieces(parts, behind):
    depth = sum(part.shape[0] for part in parts)
    width = parts[0].shape[1]
    return pl.pallas_call(
        functools.partial(pack_kernel, len(parts)),
        out_shape=jax.ShapeDtypeStruct((depth, width), BF16),
        in_specs=[VMEM] * len(parts) + [ANY] * len(behind),
        out_specs=VMEM,
        compiler_params=params(),
        cost_estimate=cost(0, 4 * depth * width),
        name="pack_weights",
    )(*parts, *behind)


def halves_kernel(right, left, *refs):
    top, low = refs[-2:]
    top[...] = right[...]
    low[...] = left[...]


def halves(right, left, behind):
    depth, width = right.shape
    shape = (depth // 2, width)
    return pl.pallas_call(
        halves_kernel,
        grid=(1,),
        out_shape=[jax.ShapeDtypeStruct(shape, BF16)] * 2,
        in_specs=[
            pl.BlockSpec(shape, lambda i: (0, 0)),
            pl.BlockSpec(shape, lambda i: (1, 0)),
        ]
        + [ANY] * len(behind),
        out_specs=[pl.BlockSpec(shape, lambda i: (0, 0))] * 2,
        compiler_params=params(),
        cost_estimate=cost(0, 4 * depth * width),
        name="take_halves",
    )(right, left, *behind)


def product_kernel(number, with_stats, place, pairs, count, probs, *rest):
    mine, other, rest = rest[:number], rest[number : 2 * number], rest[2 * number :]
    if with_stats:
        before, rest = rest[0], rest[1:]
    outs, rest = rest[:SIDE], rest[SIDE:]
    weights, total = rest[:2]
    block = weights.shape[0] * 64
    width = weights.shape[2]
    rows = probs.shape[0]
    vocab_y = place[0]
    first_block = (vocab_y * SIDE + place[1]) * (probs.shape[1] // block)
    total[...] = jnp.zeros_like(total)
    depth = weights.shape[1]
    for step in range(SIDE):
        at = lax.rem(place[2] + SIDE - step, SIDE) * 2
        for parts, core in ((mine, place[3]), (other, 1 - place[3])):
            if number == 1:
                weights[at + core] = parts[0][step * depth : step * depth + depth, :]
            else:
                weights[at + core] = parts[step][...]
    if with_stats:
        sums, line = rest[2:]
        line[...] = jnp.zeros_like(line)
        lane = lax.broadcasted_iota(jnp.int32, (64, 128), 1)
        for pair in range(SIDE):
            even = weights[2 * pair, 1024:1088, 0:128].astype(F32)
            odd = weights[2 * pair + 1, 1024:1088, 0:128].astype(F32)
            lanes = slice(pair * 128, pair * 128 + 128)
            sums[0, :, lanes] = jnp.where(lane < 64, even, pltpu.roll(odd, 64, 1))
            sums[1, :, lanes] = jnp.where(lane < 64, pltpu.roll(even, 64, 1), odd)

    def tile(slot, carry):
        teacher = pairs[slot, 0] - first_block
        owner = pairs[slot, 1] // SIDE
        columns = probs[:, pl.ds(pl.multiple_of(teacher * block, block), block)]
        matrix = weights[:, pl.ds(pl.multiple_of(slot * 64, 64), 64), :].reshape(block, width)
        total[owner] += jnp.dot(columns, matrix, preferred_element_type=F32)
        if with_stats:
            row_sums = sums[lax.rem(slot, 2), pl.ds(pl.multiple_of(slot // 2 * 8, 8), 8), :]
            line[...] += lax.dot_general(
                row_sums.astype(BF16), columns, (((1,), (1,)), ((), ())), preferred_element_type=F32
            )
        return carry

    lax.fori_loop(0, count[0], tile, 0)
    for step in range(SIDE):
        start = lax.rem(vocab_y + step, SIDE) * SIDE
        for z in range(SIDE):
            outs[step][z * rows : z * rows + rows, :] = total[start + z].astype(BF16)
    if with_stats:
        sent = line[0:1] + line[1:2] + line[2:3]
        packed = pack_rows([before[0:1], before[1:2], sent, before[3:4], before[4:5]])
        for out in outs:
            out[SIDE * rows : SIDE * rows + 16, :] = packed


def products(place, pairs, count, probs, mine, other, before=None):
    rows = probs.shape[0]
    depth, width = sum(part.shape[0] for part in mine) // SIDE, mine[0].shape[1]
    extra = [] if before is None else [before]
    scratch = [
        pltpu.VMEM((2 * SIDE, depth, width), BF16),
        pltpu.VMEM((SIDE * SIDE, rows, width), F32),
    ]
    if extra:
        scratch += [pltpu.VMEM((2, 64, 512), F32), pltpu.VMEM((8, rows), F32)]
    return pl.pallas_call(
        functools.partial(product_kernel, len(mine), bool(extra)),
        out_shape=[jax.ShapeDtypeStruct((SIDE * rows + 16 * len(extra), width), BF16)] * SIDE,
        in_specs=[SMEM, SMEM, SMEM] + [VMEM] * (1 + 2 * len(mine) + len(extra)),
        out_specs=[VMEM] * SIDE,
        scratch_shapes=scratch,
        compiler_params=params(24),
        cost_estimate=cost(
            16 * 2 * rows * 512 * width, 2 * probs.size + 16 * depth * width + 32 * rows * width
        ),
        name="tile_products",
    )(place, pairs, count, probs, *mine, *other, *extra)


def pack_rows(lines):
    rows = [part for line in lines for part in thirds(line)]
    rows.append(jnp.zeros((16 - len(rows), rows[0].shape[1]), F32))
    return jnp.concatenate(rows, axis=0).astype(BF16)


def unpack_rows(packed, number):
    packed = packed.astype(F32)
    return [
        packed[3 * i : 3 * i + 1] + packed[3 * i + 1 : 3 * i + 2] + packed[3 * i + 2 : 3 * i + 3]
        for i in range(number)
    ]


def joined(stats):
    peak = functools.reduce(jnp.maximum, [line[0] for line in stats])
    speak = functools.reduce(jnp.maximum, [line[3] for line in stats])
    factors = [jnp.exp(line[0] - peak) for line in stats]
    mass = sum(line[1] * factor for line, factor in zip(stats, factors))
    total = sum(line[2] * factor for line, factor in zip(stats, factors))
    smass = sum(line[4] * jnp.exp(line[3] - speak) for line in stats)
    return (peak, mass, total, speak, smass), factors


def columns_of(lines):
    lines = list(lines) + [jnp.zeros((128 - len(lines), lines[0].shape[1]), F32)]
    return jnp.concatenate(lines, axis=0).T


def merge_kernel(with_stats, place, *refs):
    if with_stats:
        parts, outs, kept = refs[:SIDE], refs[-1 - SIDE : -1], refs[-1]
        rows = outs[0].shape[0] - 16
        stats, factors = joined([unpack_rows(part[SIDE * rows :, :], 5) for part in parts])
        packed = pack_rows(stats)
        for out in outs:
            out[rows : rows + 16, :] = packed
        table = columns_of(factors)
        kept[...] = table
    else:
        table, parts, outs = refs[0][...], refs[1 : 1 + SIDE], refs[-SIDE:]
        rows = outs[0].shape[0]
    for step in range(SIDE):
        at = pl.ds(pl.multiple_of(lax.rem(place[1] + step, SIDE) * rows, rows), rows)
        value = table[:, 0:1] * parts[0][at, :].astype(F32)
        for d in range(1, SIDE):
            value += table[:, d : d + 1] * parts[d][at, :].astype(F32)
        outs[step][0:rows, :] = value.astype(BF16)


def merged(place, parts, rows, table=None, behind=()):
    width = parts[0].shape[1]
    first = table is None
    outs = [jax.ShapeDtypeStruct((rows + (16 if first else 0), width), BF16)] * SIDE
    if first:
        outs = outs + [jax.ShapeDtypeStruct((rows, 128), F32)]
    return pl.pallas_call(
        functools.partial(merge_kernel, first),
        out_shape=outs,
        in_specs=[SMEM] + [VMEM] * (SIDE if first else 1 + SIDE) + [ANY] * len(behind),
        out_specs=[VMEM] * len(outs),
        compiler_params=params(),
        cost_estimate=cost(rows * width, rows * width),
        name="merge_targets",
    )(place, *([] if first else [table]), *parts, *behind)


def gradient_kernel(offset, with_stats, place, logits, *refs):
    if with_stats:
        parts, (grad, loss, kept) = refs[:SIDE], refs[-3:]
        rows = logits.shape[0]
        stats, factors = joined([unpack_rows(part[rows:, :], 5) for part in parts])
        _, mass, total, peak, smass = stats
        total = total / mass
        floored = jnp.maximum(total, 1.0)
        share = total / floored
        scales = [factor / mass / floored for factor in factors]
        table = columns_of(scales + [share / smass, peak, peak + jnp.log(smass)])
        kept[...] = table
    else:
        table, loss, parts, grad = refs[0][...], refs[1], refs[2 : 2 + SIDE], refs[-1]
    rows, width = logits.shape[0], parts[0].shape[1]
    share, peak, norm = (table[:, c : c + 1] for c in range(4, 7))
    terms = jnp.zeros((rows, width), F32)
    for step in range(SIDE):
        block = lax.rem(place[1] + SIDE - step, SIDE)
        scores = logits[:, pl.ds(pl.multiple_of(block * 512 + offset, 128), width)]
        target = parts[step][0:rows, :].astype(F32) * table[:, step : step + 1]
        positive = target > 0
        entropy = jnp.where(positive, target * jnp.log(jnp.where(positive, target, 1.0)), 0.0)
        terms += entropy - target * (scores - norm)
        value = share * jnp.exp(scores - peak) - target
        at = pl.ds(pl.multiple_of(block * width, width), width)
        grad[at, :] = value.T.astype(BF16)
    sum_of_terms = jnp.sum(terms.T, axis=0, keepdims=True)
    if with_stats:
        loss[...] = jnp.broadcast_to(sum_of_terms, loss.shape)
    else:
        grad[SIDE * width :, :] = pack_rows([sum_of_terms + loss[0:1]])


def gradients(offset, place, logits, parts, before=(), behind=()):
    rows, width = logits.shape[0], parts[0].shape[1]
    first = not before
    outs = [jax.ShapeDtypeStruct((SIDE * width + (0 if first else 16), rows), BF16)]
    if first:
        outs.append(jax.ShapeDtypeStruct((8, rows), F32))
        outs.append(jax.ShapeDtypeStruct((rows, 128), F32))
    return pl.pallas_call(
        functools.partial(gradient_kernel, offset, first),
        out_shape=outs,
        in_specs=[SMEM] + [VMEM] * (1 + SIDE + len(before)) + [ANY] * len(behind),
        out_specs=[VMEM] * len(outs),
        compiler_params=params(),
        cost_estimate=cost(rows * width, rows * width),
        name="logit_grad",
    )(place, logits, *before, *parts, *behind)


def both_cores(core, mine, other, depth, out):
    rows = mine.shape[1]
    out[:, pl.ds(pl.multiple_of(core * rows, rows), rows)] = mine[0:depth, :]
    out[:, pl.ds(pl.multiple_of((1 - core) * rows, rows), rows)] = other[0:depth, :]


def stage_kernel(place, *refs):
    unembed, stage = refs[:SIDE], refs[-1]
    half = stage.shape[1] // 2
    width = half // SIDE
    for owner in range(SIDE):
        rows = slice(owner * 128, owner * 128 + 128)
        block = unembed[owner][...].reshape(128, 2 * half)
        for b in range(SIDE):
            for c in range(2):
                part = block[:, (2 * b + c) * width : (2 * b + c + 1) * width]
                stage[rows, c * half + b * width : c * half + (b + 1) * width] = part


def staged(place, unembed, behind):
    depth, cols = unembed.shape
    unembed = unembed.reshape(SIDE, SIDE, 2, 128, cols)

    def where(i, p, k):
        first = p[3] == 0
        return (jnp.where(first, i, k), jnp.where(first, k, i), p[3], 0, 0)

    views = [
        pl.BlockSpec((1, 1, 1, 128, cols), lambda i, p, k=k: where(i, p, k)) for k in range(SIDE)
    ]
    return pl.pallas_call(
        stage_kernel,
        grid_spec=pltpu.PrefetchScalarGridSpec(
            num_scalar_prefetch=1,
            grid=(SIDE,),
            in_specs=views + [ANY] * len(behind),
            out_specs=pl.BlockSpec((512, cols), lambda i, p: (i, 0)),
        ),
        out_shape=jax.ShapeDtypeStruct((depth // 2, cols), BF16),
        compiler_params=params(48),
        cost_estimate=cost(0, 2 * depth * cols),
        name="stage_unembed",
    )(place, *[unembed] * SIDE, *behind)


def early_kernel(place, stage, mine, other, out, both):
    depth = both.shape[0]
    both_cores(place[3], mine, other, depth, both)
    for step in range(SIDE):
        rows = slice(step * 512, step * 512 + 512)
        out[rows, :] = jnp.dot(stage[rows, 0:depth], both[...], preferred_element_type=F32)


def early_hidden(place, stage, mine, other):
    depth = stage.shape[0]
    width, rows = mine.shape
    return pl.pallas_call(
        early_kernel,
        out_shape=jax.ShapeDtypeStruct((depth, 2 * rows), F32),
        in_specs=[SMEM] + [VMEM] * 3,
        out_specs=VMEM,
        scratch_shapes=[pltpu.VMEM((width, 2 * rows), BF16)],
        compiler_params=params(),
        cost_estimate=cost(4 * depth * width * rows, 4 * depth * width + 8 * depth * rows),
        name="early_hidden",
    )(place, stage, mine, other)


def late_kernel(place, stage, mine, other, early, *refs):
    outs, both = refs[:SIDE], refs[SIDE]
    depth = both.shape[0]
    rows = mine.shape[1]
    both_cores(place[3], mine, other, depth, both)
    for step in range(SIDE):
        at = pl.ds(pl.multiple_of(lax.rem(place[4] + step, SIDE) * 512, 512), 512)
        result = jnp.dot(stage[at, depth : 2 * depth], both[...], preferred_element_type=F32)
        outs[step][0:512, :] = (early[at, :] + result).astype(BF16)
        for part, core in ((mine, place[3]), (other, 1 - place[3])):
            lanes = pl.ds(pl.multiple_of(core * rows, rows), rows)
            outs[step][512:528, lanes] = part[depth : depth + 16, :]


def late_hidden(place, stage, mine, other, early):
    depth, width = stage.shape
    width, rows = width // 2, early.shape[1]
    return pl.pallas_call(
        late_kernel,
        out_shape=[jax.ShapeDtypeStruct((528, rows), BF16)] * SIDE,
        in_specs=[SMEM] + [VMEM] * 4,
        out_specs=[VMEM] * SIDE,
        scratch_shapes=[pltpu.VMEM((width, rows), BF16)],
        compiler_params=params(),
        cost_estimate=cost(2 * depth * width * rows, 2 * depth * width + 6 * depth * rows),
        name="late_hidden",
    )(place, stage, mine, other, early)


def packed_loss(index, parts, at, ordered):
    for step in range(SIDE):
        ordered[lax.rem(index + SIDE - step, SIDE)] = unpack_rows(parts[step][at : at + 16, :], 1)[0]
    return ((ordered[0] + ordered[1]) + ordered[2]) + ordered[3]


def middle_kernel(place, *refs):
    parts, outs, ordered = refs[:SIDE], refs[SIDE : 2 * SIDE], refs[2 * SIDE]
    packed = pack_rows([packed_loss(place[4], parts, 512, ordered)])
    for step in range(SIDE):
        at = pl.ds(pl.multiple_of(lax.rem(place[5] + step, SIDE) * 128, 128), 128)
        value = parts[0][at, :].astype(F32)
        for part in parts[1:]:
            value += part[at, :].astype(F32)
        outs[step][0:128, :] = value.astype(BF16)
        outs[step][128:144, :] = packed


def middle(place, parts):
    rows = parts[0].shape[1]
    return pl.pallas_call(
        middle_kernel,
        out_shape=[jax.ShapeDtypeStruct((144, rows), BF16)] * SIDE,
        in_specs=[SMEM] + [VMEM] * SIDE,
        out_specs=[VMEM] * SIDE,
        scratch_shapes=[pltpu.VMEM((SIDE, 1, rows), F32)],
        compiler_params=params(),
        cost_estimate=cost(4 * 512 * rows, 10 * 512 * rows),
        name="merge_grads",
    )(place, *parts)


def total_kernel(place, *refs):
    parts = refs[:SIDE]
    keep, give, loss, ordered = refs[SIDE:]
    rows = keep.shape[1]
    mine = pl.ds(pl.multiple_of(place[3] * rows, rows), rows)
    other = pl.ds(pl.multiple_of((1 - place[3]) * rows, rows), rows)
    ordered[4] = packed_loss(place[5], parts, 128, ordered)
    loss[...] = jnp.broadcast_to(ordered[4, :, mine], loss.shape)
    for lanes, out in ((other, give), (mine, keep)):
        value = parts[0][0:128, lanes].astype(F32)
        for part in parts[1:]:
            value += part[0:128, lanes].astype(F32)
        out[...] = value.astype(BF16)


def totals(place, parts):
    rows = parts[0].shape[1] // 2
    half = jax.ShapeDtypeStruct((128, rows), BF16)
    return pl.pallas_call(
        total_kernel,
        out_shape=[half, half, jax.ShapeDtypeStruct((8, rows), F32)],
        in_specs=[SMEM] + [VMEM] * SIDE,
        out_specs=[VMEM] * 3,
        scratch_shapes=[pltpu.VMEM((SIDE + 1, 1, 2 * rows), F32)],
        compiler_params=params(),
        cost_estimate=cost(8 * 128 * rows, 20 * 128 * rows),
        name="sum_grads",
    )(place, *parts)


def turn_kernel(place, keep, given, grad):
    mine = pl.ds(pl.multiple_of(place[3] * 128, 128), 128)
    other = pl.ds(pl.multiple_of((1 - place[3]) * 128, 128), 128)
    grad[:, mine] = keep[...].astype(F32).T.astype(BF16)
    grad[:, other] = given[...].astype(F32).T.astype(BF16)


def turned(place, keep, given):
    rows = keep.shape[1]
    return pl.pallas_call(
        turn_kernel,
        out_shape=jax.ShapeDtypeStruct((rows, 256), BF16),
        in_specs=[SMEM, VMEM, VMEM],
        out_specs=VMEM,
        compiler_params=params(),
        cost_estimate=cost(0, 4 * 256 * rows),
        name="turn_grads",
    )(place, keep, given)


def spread(parts, axis):
    return [parts[0]] + [send(parts[step], axis, step) for step in (1, 2, 3)]


def crossed(parts, first):
    def target(y, z, core, step):
        if (core == 0) == first:
            y = (y + step) % SIDE
        else:
            z = (z + step) % SIDE
        return (y * SIDE + z) * 2 + core

    places = [(y, z, core) for y in range(SIDE) for z in range(SIDE) for core in range(2)]
    received = [parts[0]]
    for step in (1, 2, 3):
        pairs = [(i, target(*at, step)) for i, at in enumerate(places)]
        received.append(lax.ppermute(parts[step], ("vy", "vz", "tc"), pairs))
    return received


def shards(teacher_logits, student_hidden, student_unembed, tile_weights, tile_pairs, tile_count):
    y, z, x, core = (lax.axis_index(name) for name in ("vy", "vz", "tx", "tc"))
    crossing = [jnp.where(core == 0, y, z), jnp.where(core == 0, z, y)]
    place = jnp.stack([y, z, x, core] + crossing).astype(jnp.int32)
    rows = teacher_logits.shape[0]
    teacher = teacher_logits.astype(F32)
    peak = jnp.max(teacher, axis=1)
    shifted = jnp.exp(teacher - peak[:, None])
    mass = jnp.sum(shifted, axis=1)
    probs = shifted.astype(BF16)

    logits = jnp.dot(student_hidden, student_unembed, preferred_element_type=F32)
    speak = jnp.max(logits, axis=1)
    smass = jnp.sum(jnp.exp(logits - speak[:, None]), axis=1)

    blank = jnp.zeros_like(peak)
    before = jnp.stack([peak, mass, blank, speak, smass, blank, blank, blank])

    width = tile_weights.shape[2] // 2
    piece = prepared(tile_weights, width)
    mine = [piece, *gated(spread([piece] * SIDE, "tx")[1:], [mass, smass])]
    other = [swap(piece) for piece in mine]
    parts = products(place, tile_pairs, tile_count, probs, mine, other, before)

    piece = sliced(tile_weights, width, width, [mine[1]])
    right, left = send(piece, "tx", 1), send(piece, "tx", 3)
    top, low = halves(right, left, [parts[0]])
    parts = spread(parts, "vy")
    pieces = [piece, right, send(top, "tx", 1), send(low, "tx", 3), left]
    mine = packed_pieces(pieces, [parts[1], parts[3]])
    later = products(place, tile_pairs, tile_count, probs, [mine], [swap(mine)])

    *parts, factors = merged(place, parts, rows, None, [later[0]])
    later = spread(later, "vy")
    stage = staged(place, student_unembed, [parts[0]])
    grad, *before = gradients(0, place, logits, spread(parts, "vz"), (), later[1:] + [stage])
    early = early_hidden(place, stage, grad, swap(grad))
    before = [before[1], before[0]]
    parts = merged(place, later, rows, factors)
    (grad,) = gradients(width, place, logits, spread(parts, "vz"), before, [early])

    parts = late_hidden(place, stage, grad, swap(grad), early)
    parts = middle(place, crossed(parts, True))
    keep, give, loss = totals(place, crossed(parts, False))
    return turned(place, keep, swap(give)), loss[0]


def solution(mesh):
    grid = Mesh(mesh.devices.reshape(SIDE, SIDE, SIDE, 2), ("vy", "vz", "tx", "tc"))
    vocab, tokens = ("vy", "vz"), ("tx", "tc")
    return jax.shard_map(
        shards,
        mesh=grid,
        in_specs=(
            P(tokens, vocab),
            P(tokens, None),
            P(None, vocab),
            P(vocab, tokens, None),
            P(vocab, None),
            P(vocab),
        ),
        out_specs=(P(tokens, vocab), P(tokens)),
        check_vma=False,
    )
```

```python
import functools

import jax
import jax.numpy as jnp
from jax import lax
from jax.experimental import pallas as pl
from jax.experimental.pallas import tpu as pltpu
from jax.sharding import Mesh
from jax.sharding import PartitionSpec as P

F32 = jnp.float32
BF16 = jnp.bfloat16
SIDE = 4
VMEM = pl.BlockSpec(memory_space=pltpu.VMEM)
SMEM = pl.BlockSpec(memory_space=pltpu.SMEM)
ANY = pl.BlockSpec(memory_space=pl.ANY)
MIB = 1024 * 1024


def params(mib=16):
    return pltpu.CompilerParams(vmem_limit_bytes=mib * MIB)


def cost(flops, moved, transcendentals=0):
    return pl.CostEstimate(flops=flops, bytes_accessed=moved, transcendentals=transcendentals)


def send(value, axis, step):
    return lax.ppermute(value, axis, [(i, (i + step) % SIDE) for i in range(SIDE)])


def swap(value):
    return lax.ppermute(value, "tc", [(0, 1), (1, 0)])


def thirds(value):
    high = value.astype(BF16).astype(F32)
    rest = value - high
    middle = rest.astype(BF16).astype(F32)
    return high, middle, rest - middle


def prepare_kernel(weights, piece):
    slots, shard_rows, _ = weights.shape
    width = piece.shape[1]
    rows = slots * shard_rows
    piece[0:rows, :] = weights[:, :, 0:width].reshape(rows, width)
    sums = jnp.sum(weights[...].astype(F32), axis=2, keepdims=True).reshape(rows, 1)
    line = jnp.broadcast_to(sums, (rows, 128)).T[0:1]
    lines = jnp.concatenate(list(thirds(line)) + [jnp.zeros((5, rows), F32)], axis=0)
    extra = jnp.concatenate([lines[:, i * 128 : (i + 1) * 128] for i in range(8)], axis=0)
    if width > 128:
        extra = jnp.concatenate([extra, jnp.zeros((64, width - 128), F32)], axis=1)
    piece[rows : rows + 64, :] = extra.astype(BF16)


def prepared(weights, width):
    slots, shard_rows, _ = weights.shape
    return pl.pallas_call(
        prepare_kernel,
        out_shape=jax.ShapeDtypeStruct((slots * shard_rows + 64, width), BF16),
        in_specs=[VMEM],
        out_specs=VMEM,
        compiler_params=params(),
        cost_estimate=cost(2 * weights.size, 3 * weights.size),
        name="prepare_weights",
    )(weights)


def slice_kernel(offset, weights, *refs):
    piece = refs[-1]
    piece[...] = weights[:, :, offset : offset + piece.shape[1]].reshape(piece.shape)


def sliced(weights, offset, width, behind):
    slots, shard_rows, _ = weights.shape
    return pl.pallas_call(
        functools.partial(slice_kernel, offset),
        out_shape=jax.ShapeDtypeStruct((slots * shard_rows, width), BF16),
        in_specs=[VMEM] + [ANY] * len(behind),
        out_specs=VMEM,
        compiler_params=params(),
        cost_estimate=cost(0, 3 * weights.size),
        name="slice_weights",
    )(weights, *behind)


def gate_kernel(*refs):
    pass


def gated(parts, behind):
    return pl.pallas_call(
        gate_kernel,
        out_shape=[jax.ShapeDtypeStruct(part.shape, part.dtype) for part in parts],
        in_specs=[ANY] * (len(parts) + len(behind)),
        out_specs=[ANY] * len(parts),
        input_output_aliases={i: i for i in range(len(parts))},
        compiler_params=params(),
        cost_estimate=cost(0, 0),
        name="gate",
    )(*parts, *behind)


def pack_kernel(number, *refs):
    out = refs[-1]
    at = 0
    for part in refs[:number]:
        out[at : at + part.shape[0], :] = part[...]
        at += part.shape[0]


def packed_pieces(parts, behind):
    depth = sum(part.shape[0] for part in parts)
    width = parts[0].shape[1]
    return pl.pallas_call(
        functools.partial(pack_kernel, len(parts)),
        out_shape=jax.ShapeDtypeStruct((depth, width), BF16),
        in_specs=[VMEM] * len(parts) + [ANY] * len(behind),
        out_specs=VMEM,
        compiler_params=params(),
        cost_estimate=cost(0, 4 * depth * width),
        name="pack_weights",
    )(*parts, *behind)


def halves_kernel(right, left, *refs):
    top, low = refs[-2:]
    top[...] = right[...]
    low[...] = left[...]


def halves(right, left, behind):
    depth, width = right.shape
    shape = (depth // 2, width)
    return pl.pallas_call(
        halves_kernel,
        grid=(1,),
        out_shape=[jax.ShapeDtypeStruct(shape, BF16)] * 2,
        in_specs=[
            pl.BlockSpec(shape, lambda i: (0, 0)),
            pl.BlockSpec(shape, lambda i: (1, 0)),
        ]
        + [ANY] * len(behind),
        out_specs=[pl.BlockSpec(shape, lambda i: (0, 0))] * 2,
        compiler_params=params(),
        cost_estimate=cost(0, 4 * depth * width),
        name="take_halves",
    )(right, left, *behind)


def product_kernel(number, with_stats, place, pairs, count, probs, *rest):
    mine, other, rest = rest[:number], rest[number : 2 * number], rest[2 * number :]
    if with_stats:
        before, rest = rest[0], rest[1:]
    first = len(rest) - (SIDE + 5 if with_stats else SIDE + 3)
    outs, rest = rest[first : first + SIDE + 1], rest[first + SIDE + 1 :]
    weights, total = rest[:2]
    block = weights.shape[0] * 64
    width = weights.shape[2]
    rows = probs.shape[0]
    vocab_y = place[0]
    first_block = (vocab_y * SIDE + place[1]) * (probs.shape[1] // block)
    total[...] = jnp.zeros_like(total)
    depth = weights.shape[1]
    for step in range(SIDE):
        at = lax.rem(place[2] + SIDE - step, SIDE) * 2
        for parts, core in ((mine, place[3]), (other, 1 - place[3])):
            if number == 1:
                weights[at + core] = parts[0][step * depth : step * depth + depth, :]
            else:
                weights[at + core] = parts[step][...]
    if with_stats:
        sums, line = rest[2:]
        line[...] = jnp.zeros_like(line)
        lane = lax.broadcasted_iota(jnp.int32, (64, 128), 1)
        for pair in range(SIDE):
            even = weights[2 * pair, 1024:1088, 0:128].astype(F32)
            odd = weights[2 * pair + 1, 1024:1088, 0:128].astype(F32)
            lanes = slice(pair * 128, pair * 128 + 128)
            sums[0, :, lanes] = jnp.where(lane < 64, even, pltpu.roll(odd, 64, 1))
            sums[1, :, lanes] = jnp.where(lane < 64, pltpu.roll(even, 64, 1), odd)

    def tile(slot, carry):
        teacher = pairs[slot, 0] - first_block
        owner = pairs[slot, 1] // SIDE
        columns = probs[:, pl.ds(pl.multiple_of(teacher * block, block), block)]
        matrix = weights[:, pl.ds(pl.multiple_of(slot * 64, 64), 64), :].reshape(block, width)
        total[owner] += jnp.dot(columns, matrix, preferred_element_type=F32)
        if with_stats:
            row_sums = sums[lax.rem(slot, 2), pl.ds(pl.multiple_of(slot // 2 * 8, 8), 8), :]
            line[...] += lax.dot_general(
                row_sums.astype(BF16), columns, (((1,), (1,)), ((), ())), preferred_element_type=F32
            )
        return carry

    lax.fori_loop(0, count[0], tile, 0)
    half = rows // 2
    for step in range(SIDE):
        start = lax.rem(vocab_y + step, SIDE) * SIDE
        for z in range(SIDE):
            value = total[start + z].astype(BF16)
            if step == 2:
                outs[3][z * half : z * half + half, :] = value[:half]
                outs[4][z * half : z * half + half, :] = value[half:]
            else:
                outs[step - step // 3][z * rows : z * rows + rows, :] = value
    if with_stats:
        sent = line[0:1] + line[1:2] + line[2:3]
        packed = pack_rows([before[0:1], before[1:2], sent, before[3:4], before[4:5]])
        for out in outs[3:]:
            out[SIDE * half : SIDE * half + 16, :] = packed


def products(place, pairs, count, probs, mine, other, before=None, behind=()):
    rows = probs.shape[0]
    depth, width = sum(part.shape[0] for part in mine) // SIDE, mine[0].shape[1]
    extra = [] if before is None else [before]
    scratch = [
        pltpu.VMEM((2 * SIDE, depth, width), BF16),
        pltpu.VMEM((SIDE * SIDE, rows, width), F32),
    ]
    if extra:
        scratch += [pltpu.VMEM((2, 64, 512), F32), pltpu.VMEM((8, rows), F32)]
    return pl.pallas_call(
        functools.partial(product_kernel, len(mine), bool(extra)),
        out_shape=[jax.ShapeDtypeStruct((SIDE * rows, width), BF16)] * 3
        + [jax.ShapeDtypeStruct((SIDE * rows // 2 + 16 * len(extra), width), BF16)] * 2,
        in_specs=[SMEM, SMEM, SMEM] + [VMEM] * (1 + 2 * len(mine) + len(extra)) + [ANY] * len(behind),
        out_specs=[VMEM] * (SIDE + 1),
        scratch_shapes=scratch,
        compiler_params=params(24),
        cost_estimate=cost(
            16 * 2 * rows * 512 * width, 2 * probs.size + 16 * depth * width + 32 * rows * width
        ),
        name="tile_products",
    )(place, pairs, count, probs, *mine, *other, *extra, *behind)


def pack_rows(lines):
    rows = [part for line in lines for part in thirds(line)]
    rows.append(jnp.zeros((16 - len(rows), rows[0].shape[1]), F32))
    return jnp.concatenate(rows, axis=0).astype(BF16)


def unpack_rows(packed, number):
    packed = packed.astype(F32)
    return [
        packed[3 * i : 3 * i + 1] + packed[3 * i + 1 : 3 * i + 2] + packed[3 * i + 2 : 3 * i + 3]
        for i in range(number)
    ]


def joined(stats):
    peak = functools.reduce(jnp.maximum, [line[0] for line in stats])
    speak = functools.reduce(jnp.maximum, [line[3] for line in stats])
    factors = [jnp.exp(line[0] - peak) for line in stats]
    mass = sum(line[1] * factor for line, factor in zip(stats, factors))
    total = sum(line[2] * factor for line, factor in zip(stats, factors))
    smass = sum(line[4] * jnp.exp(line[3] - speak) for line in stats)
    return (peak, mass, total, speak, smass), factors


def columns_of(lines):
    lines = list(lines) + [jnp.zeros((128 - len(lines), lines[0].shape[1]), F32)]
    return jnp.concatenate(lines, axis=0).T


def relay_kernel(with_stats, *refs):
    if with_stats:
        near, far, from_left, from_right, mine = refs[:5]
        near_out, far_out, kept, table_out = refs[-4:]
        depth = from_left.shape[0] - 16
        rows = 2 * depth // SIDE
        stats = [unpack_rows(part[depth:, :], 5) for part in (mine, from_left, from_right)]
        kept[...] = jnp.concatenate(stats[0] + stats[1] + stats[2] + [jnp.zeros((1, rows), F32)], axis=0)
        own, left, right = (line[0] for line in stats)
        lane = lax.broadcasted_iota(jnp.int32, own.shape, 1)
        other = jnp.where(lane < rows // 2, left, right)
        peak = jnp.maximum(own, other)
        table = columns_of([jnp.exp(own - peak), jnp.exp(other - peak)])
        table_out[...] = table
        near_out[SIDE * rows : SIDE * rows + 16, :] = from_left[depth : depth + 16, :]
    else:
        near, far, from_left, from_right, table = refs[:5]
        near_out, far_out = refs[-2:]
        table = table[...]
        depth = from_left.shape[0]
        rows = 2 * depth // SIDE
    half = rows // 2
    for z in range(SIDE):
        low, high = slice(z * rows, z * rows + half), slice(z * rows + half, (z + 1) * rows)
        part = slice(z * half, (z + 1) * half)
        value = table[:half, 0:1] * near[low, :].astype(F32) + table[:half, 1:2] * from_left[part, :].astype(F32)
        near_out[low, :] = value.astype(BF16)
        near_out[high, :] = near[high, :]
        value = table[half:, 0:1] * far[high, :].astype(F32) + table[half:, 1:2] * from_right[part, :].astype(F32)
        far_out[high, :] = value.astype(BF16)
        far_out[low, :] = far[low, :]


def relayed(near, far, from_left, from_right, last, first, behind=()):
    depth, width = near.shape
    rows = depth // SIDE
    outs = [
        jax.ShapeDtypeStruct((depth + (16 if first else 0), width), BF16),
        jax.ShapeDtypeStruct((depth, width), BF16),
    ]
    if first:
        outs.append(jax.ShapeDtypeStruct((16, rows), F32))
        outs.append(jax.ShapeDtypeStruct((rows, 128), F32))
    return pl.pallas_call(
        functools.partial(relay_kernel, first),
        out_shape=outs,
        in_specs=[VMEM] * 5 + [ANY] * len(behind),
        out_specs=[VMEM] * len(outs),
        compiler_params=params(),
        cost_estimate=cost(depth * width, depth * width),
        name="relay_targets",
    )(near, far, from_left, from_right, last, *behind)


def merge_kernel(with_stats, place, given, *refs):
    parts = refs[:3]
    if with_stats:
        outs, kept = refs[-1 - SIDE : -1], refs[-1]
        rows = outs[0].shape[0] - 16
        lines = [[given[5 * i + j : 5 * i + j + 1] for j in range(5)] for i in range(3)]
        lines.append(unpack_rows(parts[1][SIDE * rows :, :], 5))
        stats, _ = joined(lines)
        packed = pack_rows(stats)
        for out in outs:
            out[rows : rows + 16, :] = packed
        own, left, right, across = (line[0] for line in lines)
        lane = lax.broadcasted_iota(jnp.int32, own.shape, 1)
        low = lane < rows // 2
        left = jnp.where(low, jnp.maximum(left, across), left)
        right = jnp.where(low, right, jnp.maximum(right, across))
        table = columns_of([jnp.exp(base - stats[0]) for base in (own, left, right)])
        kept[...] = table
    else:
        table, outs = given[...], refs[-SIDE:]
        rows = outs[0].shape[0]
    for step in range(SIDE):
        at = pl.ds(pl.multiple_of(lax.rem(place[1] + step, SIDE) * rows, rows), rows)
        value = table[:, 0:1] * parts[0][at, :].astype(F32)
        for d in range(1, 3):
            value += table[:, d : d + 1] * parts[d][at, :].astype(F32)
        outs[step][0:rows, :] = value.astype(BF16)


def merged(place, given, parts, rows, first, behind=()):
    width = parts[0].shape[1]
    outs = [jax.ShapeDtypeStruct((rows + (16 if first else 0), width), BF16)] * SIDE
    if first:
        outs = outs + [jax.ShapeDtypeStruct((rows, 128), F32)]
    return pl.pallas_call(
        functools.partial(merge_kernel, first),
        out_shape=outs,
        in_specs=[SMEM] + [VMEM] * 4 + [ANY] * len(behind),
        out_specs=[VMEM] * len(outs),
        compiler_params=params(),
        cost_estimate=cost(rows * width, rows * width),
        name="merge_targets",
    )(place, given, *parts, *behind)


def gradient_kernel(offset, with_stats, place, logits, *refs):
    if with_stats:
        parts, (grad, loss, kept) = refs[:SIDE], refs[-3:]
        rows = logits.shape[0]
        stats, factors = joined([unpack_rows(part[rows:, :], 5) for part in parts])
        _, mass, total, peak, smass = stats
        total = total / mass
        floored = jnp.maximum(total, 1.0)
        share = total / floored
        scales = [factor / mass / floored for factor in factors]
        table = columns_of(scales + [share / smass, peak, peak + jnp.log(smass)])
        kept[...] = table
    else:
        table, loss, parts, grad = refs[0][...], refs[1], refs[2 : 2 + SIDE], refs[-1]
    rows, width = logits.shape[0], parts[0].shape[1]
    share, peak, norm = (table[:, c : c + 1] for c in range(4, 7))
    terms = jnp.zeros((rows, width), F32)
    for step in range(SIDE):
        block = lax.rem(place[1] + SIDE - step, SIDE)
        scores = logits[:, pl.ds(pl.multiple_of(block * 512 + offset, 128), width)]
        target = parts[step][0:rows, :].astype(F32) * table[:, step : step + 1]
        positive = target > 0
        entropy = jnp.where(positive, target * jnp.log(jnp.where(positive, target, 1.0)), 0.0)
        terms += entropy - target * (scores - norm)
        value = share * jnp.exp(scores - peak) - target
        at = pl.ds(pl.multiple_of(block * width, width), width)
        grad[at, :] = value.T.astype(BF16)
    sum_of_terms = jnp.sum(terms.T, axis=0, keepdims=True)
    if with_stats:
        loss[...] = jnp.broadcast_to(sum_of_terms, loss.shape)
    else:
        grad[SIDE * width :, :] = pack_rows([sum_of_terms + loss[0:1]])


def gradients(offset, place, logits, parts, before=(), behind=()):
    rows, width = logits.shape[0], parts[0].shape[1]
    first = not before
    outs = [jax.ShapeDtypeStruct((SIDE * width + (0 if first else 16), rows), BF16)]
    if first:
        outs.append(jax.ShapeDtypeStruct((8, rows), F32))
        outs.append(jax.ShapeDtypeStruct((rows, 128), F32))
    return pl.pallas_call(
        functools.partial(gradient_kernel, offset, first),
        out_shape=outs,
        in_specs=[SMEM] + [VMEM] * (1 + SIDE + len(before)) + [ANY] * len(behind),
        out_specs=[VMEM] * len(outs),
        compiler_params=params(),
        cost_estimate=cost(rows * width, rows * width),
        name="logit_grad",
    )(place, logits, *before, *parts, *behind)


def both_cores(core, mine, other, depth, out):
    rows = mine.shape[1]
    out[:, pl.ds(pl.multiple_of(core * rows, rows), rows)] = mine[0:depth, :]
    out[:, pl.ds(pl.multiple_of((1 - core) * rows, rows), rows)] = other[0:depth, :]


def stage_kernel(place, unembed, *refs):
    stage, sems = refs[-2:]
    first = place[3] == 0
    copies = []
    for major in range(SIDE):
        for minor in range(SIDE):
            index = major * SIDE + minor
            owner = jnp.where(first, index, minor * SIDE + major)
            start = pl.multiple_of(owner * 256 + place[3] * 128, 128)
            copies.append(
                pltpu.make_async_copy(
                    unembed.at[pl.ds(start, 128), :],
                    stage.at[pl.ds(index * 128, 128), :],
                    sems.at[index],
                )
            )
    for copy in copies:
        copy.start()
    for copy in copies:
        copy.wait()


def staged(place, unembed, behind):
    depth, cols = unembed.shape
    return pl.pallas_call(
        stage_kernel,
        out_shape=jax.ShapeDtypeStruct((depth // 2, cols), BF16),
        in_specs=[SMEM, pl.BlockSpec(memory_space=pltpu.HBM)] + [ANY] * len(behind),
        out_specs=VMEM,
        scratch_shapes=[pltpu.SemaphoreType.DMA((SIDE * SIDE,))],
        compiler_params=params(42),
        cost_estimate=cost(0, depth * cols),
        name="stage_unembed",
    )(place, unembed, *behind)


def columns_at(stage, rows, chunk, width):
    parts = [stage[rows, (2 * b + chunk) * width : (2 * b + chunk + 1) * width] for b in range(SIDE)]
    return jnp.concatenate(parts, axis=1)


def early_kernel(place, stage, mine, other, out, both):
    depth = both.shape[0]
    both_cores(place[3], mine, other, depth, both)
    for step in range(SIDE):
        rows = slice(step * 512, step * 512 + 512)
        out[rows, :] = jnp.dot(
            columns_at(stage, rows, 0, depth // SIDE), both[...], preferred_element_type=F32
        )


def early_hidden(place, stage, mine, other):
    depth = stage.shape[0]
    width, rows = mine.shape
    return pl.pallas_call(
        early_kernel,
        out_shape=jax.ShapeDtypeStruct((depth, 2 * rows), F32),
        in_specs=[SMEM] + [VMEM] * 3,
        out_specs=VMEM,
        scratch_shapes=[pltpu.VMEM((width, 2 * rows), BF16)],
        compiler_params=params(),
        cost_estimate=cost(4 * depth * width * rows, 4 * depth * width + 8 * depth * rows),
        name="early_hidden",
    )(place, stage, mine, other)


def late_kernel(place, stage, mine, other, early, *refs):
    outs, both = refs[:SIDE], refs[SIDE]
    depth = both.shape[0]
    rows = mine.shape[1]
    both_cores(place[3], mine, other, depth, both)
    for step in range(SIDE):
        at = pl.ds(pl.multiple_of(lax.rem(place[4] + step, SIDE) * 512, 512), 512)
        result = jnp.dot(
            columns_at(stage, at, 1, depth // SIDE), both[...], preferred_element_type=F32
        )
        outs[step][0:512, :] = (early[at, :] + result).astype(BF16)
        for part, core in ((mine, place[3]), (other, 1 - place[3])):
            lanes = pl.ds(pl.multiple_of(core * rows, rows), rows)
            outs[step][512:528, lanes] = part[depth : depth + 16, :]


def late_hidden(place, stage, mine, other, early):
    depth, width = stage.shape
    width, rows = width // 2, early.shape[1]
    return pl.pallas_call(
        late_kernel,
        out_shape=[jax.ShapeDtypeStruct((528, rows), BF16)] * SIDE,
        in_specs=[SMEM] + [VMEM] * 4,
        out_specs=[VMEM] * SIDE,
        scratch_shapes=[pltpu.VMEM((width, rows), BF16)],
        compiler_params=params(),
        cost_estimate=cost(2 * depth * width * rows, 2 * depth * width + 6 * depth * rows),
        name="late_hidden",
    )(place, stage, mine, other, early)


def packed_loss(index, parts, at, ordered):
    for step in range(SIDE):
        ordered[lax.rem(index + SIDE - step, SIDE)] = unpack_rows(parts[step][at : at + 16, :], 1)[0]
    return ((ordered[0] + ordered[1]) + ordered[2]) + ordered[3]


def middle_kernel(place, *refs):
    parts, outs, ordered = refs[:SIDE], refs[SIDE : 2 * SIDE], refs[2 * SIDE]
    packed = pack_rows([packed_loss(place[4], parts, 512, ordered)])
    for step in range(SIDE):
        at = pl.ds(pl.multiple_of(lax.rem(place[5] + step, SIDE) * 128, 128), 128)
        value = parts[0][at, :].astype(F32)
        for part in parts[1:]:
            value += part[at, :].astype(F32)
        outs[step][0:128, :] = value.astype(BF16)
        outs[step][128:144, :] = packed


def middle(place, parts):
    rows = parts[0].shape[1]
    return pl.pallas_call(
        middle_kernel,
        out_shape=[jax.ShapeDtypeStruct((144, rows), BF16)] * SIDE,
        in_specs=[SMEM] + [VMEM] * SIDE,
        out_specs=[VMEM] * SIDE,
        scratch_shapes=[pltpu.VMEM((SIDE, 1, rows), F32)],
        compiler_params=params(),
        cost_estimate=cost(4 * 512 * rows, 10 * 512 * rows),
        name="merge_grads",
    )(place, *parts)


def total_kernel(place, *refs):
    parts = refs[:SIDE]
    keep, give, loss, ordered = refs[SIDE:]
    rows = keep.shape[1]
    mine = pl.ds(pl.multiple_of(place[3] * rows, rows), rows)
    other = pl.ds(pl.multiple_of((1 - place[3]) * rows, rows), rows)
    ordered[4] = packed_loss(place[5], parts, 128, ordered)
    loss[...] = jnp.broadcast_to(ordered[4, :, mine], loss.shape)
    for lanes, out in ((other, give), (mine, keep)):
        value = parts[0][0:128, lanes].astype(F32)
        for part in parts[1:]:
            value += part[0:128, lanes].astype(F32)
        out[...] = value.astype(BF16)


def totals(place, parts):
    rows = parts[0].shape[1] // 2
    half = jax.ShapeDtypeStruct((128, rows), BF16)
    return pl.pallas_call(
        total_kernel,
        out_shape=[half, half, jax.ShapeDtypeStruct((8, rows), F32)],
        in_specs=[SMEM] + [VMEM] * SIDE,
        out_specs=[VMEM] * 3,
        scratch_shapes=[pltpu.VMEM((SIDE + 1, 1, 2 * rows), F32)],
        compiler_params=params(),
        cost_estimate=cost(8 * 128 * rows, 20 * 128 * rows),
        name="sum_grads",
    )(place, *parts)


def turn_kernel(place, keep, given, grad):
    mine = pl.ds(pl.multiple_of(place[3] * 128, 128), 128)
    other = pl.ds(pl.multiple_of((1 - place[3]) * 128, 128), 128)
    grad[:, mine] = keep[...].astype(F32).T.astype(BF16)
    grad[:, other] = given[...].astype(F32).T.astype(BF16)


def turned(place, keep, given):
    rows = keep.shape[1]
    return pl.pallas_call(
        turn_kernel,
        out_shape=jax.ShapeDtypeStruct((rows, 256), BF16),
        in_specs=[SMEM, VMEM, VMEM],
        out_specs=VMEM,
        compiler_params=params(),
        cost_estimate=cost(0, 4 * 256 * rows),
        name="turn_grads",
    )(place, keep, given)


def spread(parts, axis):
    return [parts[0]] + [send(parts[step], axis, step) for step in (1, 2, 3)]


def crossed(parts, first):
    def target(y, z, core, step):
        if (core == 0) == first:
            y = (y + step) % SIDE
        else:
            z = (z + step) % SIDE
        return (y * SIDE + z) * 2 + core

    places = [(y, z, core) for y in range(SIDE) for z in range(SIDE) for core in range(2)]
    received = [parts[0]]
    for step in (1, 2, 3):
        pairs = [(i, target(*at, step)) for i, at in enumerate(places)]
        received.append(lax.ppermute(parts[step], ("vy", "vz", "tc"), pairs))
    return received


def shards(teacher_logits, student_hidden, student_unembed, tile_weights, tile_pairs, tile_count):
    y, z, x, core = (lax.axis_index(name) for name in ("vy", "vz", "tx", "tc"))
    crossing = [jnp.where(core == 0, y, z), jnp.where(core == 0, z, y)]
    place = jnp.stack([y, z, x, core] + crossing).astype(jnp.int32)
    rows = teacher_logits.shape[0]
    teacher = teacher_logits.astype(F32)
    peak = jnp.max(teacher, axis=1)
    shifted = jnp.exp(teacher - peak[:, None])
    mass = jnp.sum(shifted, axis=1)
    probs = shifted.astype(BF16)

    logits = jnp.dot(student_hidden, student_unembed, preferred_element_type=F32)
    speak = jnp.max(logits, axis=1)
    smass = jnp.sum(jnp.exp(logits - speak[:, None]), axis=1)

    blank = jnp.zeros_like(peak)
    before = jnp.stack([peak, mass, blank, speak, smass, blank, blank, blank])

    width = tile_weights.shape[2] // 2
    piece = prepared(tile_weights, width)
    mine = [piece, *gated(spread([piece] * SIDE, "tx")[1:], [mass, smass])]
    other = [swap(piece) for piece in mine]

    piece = sliced(tile_weights, width, width, [mine[1]])
    right, left = send(piece, "tx", 1), send(piece, "tx", 3)
    parts = products(place, tile_pairs, tile_count, probs, mine, other, before, [piece])
    top, low = halves(right, left, [parts[0]])
    own, near, far, to_right, to_left = parts
    left_part, right_part = send(to_right, "vy", 1), send(to_left, "vy", 3)
    near, far, given, factors = relayed(near, far, left_part, right_part, to_right, True, [right, left])
    pieces = [piece, right, send(top, "tx", 1), send(low, "tx", 3), left]
    near, far = send(near, "vy", 1), send(far, "vy", 3)
    mine = packed_pieces(pieces, [near, far])
    later = products(place, tile_pairs, tile_count, probs, [mine], [swap(mine)])

    *parts, scales = merged(place, given, [own, near, far], rows, True, [later[0]])
    own, near, far, to_right, to_left = later
    left_part, right_part = send(to_right, "vy", 1), send(to_left, "vy", 3)
    near, far = relayed(near, far, left_part, right_part, factors, False)
    later = [own, send(near, "vy", 1), send(far, "vy", 3)]
    stage = staged(place, student_unembed, [parts[0]])
    grad, *before = gradients(0, place, logits, spread(parts, "vz"), (), later[1:] + [stage])
    early = early_hidden(place, stage, grad, swap(grad))
    before = [before[1], before[0]]
    parts = merged(place, scales, later, rows, False)
    (grad,) = gradients(width, place, logits, spread(parts, "vz"), before, [early])

    parts = late_hidden(place, stage, grad, swap(grad), early)
    parts = middle(place, crossed(parts, True))
    keep, give, loss = totals(place, crossed(parts, False))
    return turned(place, keep, swap(give)), loss[0]


def solution(mesh):
    grid = Mesh(mesh.devices.reshape(SIDE, SIDE, SIDE, 2), ("vy", "vz", "tx", "tc"))
    vocab, tokens = ("vy", "vz"), ("tx", "tc")
    return jax.shard_map(
        shards,
        mesh=grid,
        in_specs=(
            P(tokens, vocab),
            P(tokens, None),
            P(None, vocab),
            P(vocab, tokens, None),
            P(vocab, None),
            P(vocab),
        ),
        out_specs=(P(tokens, vocab), P(tokens)),
        check_vma=False,
    )
```

```python
import functools

import jax
import jax.numpy as jnp
from jax import lax
from jax.experimental import pallas as pl
from jax.experimental.pallas import tpu as pltpu
from jax.sharding import Mesh
from jax.sharding import PartitionSpec as P

F32 = jnp.float32
BF16 = jnp.bfloat16
SIDE = 4
VMEM = pl.BlockSpec(memory_space=pltpu.VMEM)
SMEM = pl.BlockSpec(memory_space=pltpu.SMEM)
ANY = pl.BlockSpec(memory_space=pl.ANY)
MIB = 1024 * 1024


def params(mib=16):
    return pltpu.CompilerParams(vmem_limit_bytes=mib * MIB)


def cost(flops, moved, transcendentals=0):
    return pl.CostEstimate(flops=flops, bytes_accessed=moved, transcendentals=transcendentals)


def send(value, axis, step):
    return lax.ppermute(value, axis, [(i, (i + step) % SIDE) for i in range(SIDE)])


def swap(value):
    return lax.ppermute(value, "tc", [(0, 1), (1, 0)])


def thirds(value):
    high = value.astype(BF16).astype(F32)
    rest = value - high
    middle = rest.astype(BF16).astype(F32)
    return high, middle, rest - middle


def prepare_kernel(weights, piece):
    slots, shard_rows, _ = weights.shape
    width = piece.shape[1]
    rows = slots * shard_rows
    piece[0:rows, :] = weights[:, :, 0:width].reshape(rows, width)
    sums = jnp.sum(weights[...].astype(F32), axis=2, keepdims=True).reshape(rows, 1)
    line = jnp.broadcast_to(sums, (rows, 128)).T[0:1]
    lines = jnp.concatenate(list(thirds(line)) + [jnp.zeros((5, rows), F32)], axis=0)
    extra = jnp.concatenate([lines[:, i * 128 : (i + 1) * 128] for i in range(8)], axis=0)
    if width > 128:
        extra = jnp.concatenate([extra, jnp.zeros((64, width - 128), F32)], axis=1)
    piece[rows : rows + 64, :] = extra.astype(BF16)


def prepared(weights, width):
    slots, shard_rows, _ = weights.shape
    return pl.pallas_call(
        prepare_kernel,
        out_shape=jax.ShapeDtypeStruct((slots * shard_rows + 64, width), BF16),
        in_specs=[VMEM],
        out_specs=VMEM,
        compiler_params=params(),
        cost_estimate=cost(2 * weights.size, 3 * weights.size),
        name="prepare_weights",
    )(weights)


def slice_kernel(offset, weights, *refs):
    piece = refs[-1]
    piece[...] = weights[:, :, offset : offset + piece.shape[1]].reshape(piece.shape)


def sliced(weights, offset, width, behind):
    slots, shard_rows, _ = weights.shape
    return pl.pallas_call(
        functools.partial(slice_kernel, offset),
        out_shape=jax.ShapeDtypeStruct((slots * shard_rows, width), BF16),
        in_specs=[VMEM] + [ANY] * len(behind),
        out_specs=VMEM,
        compiler_params=params(),
        cost_estimate=cost(0, 3 * weights.size),
        name="slice_weights",
    )(weights, *behind)


def gate_kernel(*refs):
    pass


def gated(parts, behind):
    return pl.pallas_call(
        gate_kernel,
        out_shape=[jax.ShapeDtypeStruct(part.shape, part.dtype) for part in parts],
        in_specs=[ANY] * (len(parts) + len(behind)),
        out_specs=[ANY] * len(parts),
        input_output_aliases={i: i for i in range(len(parts))},
        compiler_params=params(),
        cost_estimate=cost(0, 0),
        name="gate",
    )(*parts, *behind)


def pack_kernel(number, *refs):
    out = refs[-1]
    at = 0
    for part in refs[:number]:
        out[at : at + part.shape[0], :] = part[...]
        at += part.shape[0]


def packed_pieces(parts, behind):
    depth = sum(part.shape[0] for part in parts)
    width = parts[0].shape[1]
    return pl.pallas_call(
        functools.partial(pack_kernel, len(parts)),
        out_shape=jax.ShapeDtypeStruct((depth, width), BF16),
        in_specs=[VMEM] * len(parts) + [ANY] * len(behind),
        out_specs=VMEM,
        compiler_params=params(),
        cost_estimate=cost(0, 4 * depth * width),
        name="pack_weights",
    )(*parts, *behind)


def halves_kernel(right, left, *refs):
    top, low = refs[-2:]
    top[...] = right[...]
    low[...] = left[...]


def halves(right, left, behind):
    depth, width = right.shape
    shape = (depth // 2, width)
    return pl.pallas_call(
        halves_kernel,
        grid=(1,),
        out_shape=[jax.ShapeDtypeStruct(shape, BF16)] * 2,
        in_specs=[
            pl.BlockSpec(shape, lambda i: (0, 0)),
            pl.BlockSpec(shape, lambda i: (1, 0)),
        ]
        + [ANY] * len(behind),
        out_specs=[pl.BlockSpec(shape, lambda i: (0, 0))] * 2,
        compiler_params=params(),
        cost_estimate=cost(0, 4 * depth * width),
        name="take_halves",
    )(right, left, *behind)


def product_kernel(number, with_stats, place, pairs, count, source, *rest):
    probs, sem, rest = rest[-2], rest[-1], rest[:-2]
    copy = pltpu.make_async_copy(source, probs, sem)
    copy.start()
    mine, other, rest = rest[:number], rest[number : 2 * number], rest[2 * number :]
    if with_stats:
        before, rest = rest[0], rest[1:]
    first = len(rest) - (SIDE + 5 if with_stats else SIDE + 3)
    outs, rest = rest[first : first + SIDE + 1], rest[first + SIDE + 1 :]
    weights, total = rest[:2]
    block = weights.shape[0] * 64
    width = weights.shape[2]
    rows = probs.shape[0]
    vocab_y = place[0]
    first_block = (vocab_y * SIDE + place[1]) * (probs.shape[1] // block)
    total[...] = jnp.zeros_like(total)
    depth = weights.shape[1]
    for step in range(SIDE):
        at = lax.rem(place[2] + SIDE - step, SIDE) * 2
        for parts, core in ((mine, place[3]), (other, 1 - place[3])):
            if number == 1:
                weights[at + core] = parts[0][step * depth : step * depth + depth, :]
            else:
                weights[at + core] = parts[step][...]
    if with_stats:
        sums, line = rest[2:]
        line[...] = jnp.zeros_like(line)
        lane = lax.broadcasted_iota(jnp.int32, (64, 128), 1)
        for pair in range(SIDE):
            even = weights[2 * pair, 1024:1088, 0:128].astype(F32)
            odd = weights[2 * pair + 1, 1024:1088, 0:128].astype(F32)
            lanes = slice(pair * 128, pair * 128 + 128)
            sums[0, :, lanes] = jnp.where(lane < 64, even, pltpu.roll(odd, 64, 1))
            sums[1, :, lanes] = jnp.where(lane < 64, pltpu.roll(even, 64, 1), odd)

    def tile(slot, carry):
        teacher = pairs[slot, 0] - first_block
        owner = pairs[slot, 1] // SIDE
        columns = probs[:, pl.ds(pl.multiple_of(teacher * block, block), block)]
        matrix = weights[:, pl.ds(pl.multiple_of(slot * 64, 64), 64), :].reshape(block, width)
        total[owner] += jnp.dot(columns, matrix, preferred_element_type=F32)
        if with_stats:
            row_sums = sums[lax.rem(slot, 2), pl.ds(pl.multiple_of(slot // 2 * 8, 8), 8), :]
            line[...] += lax.dot_general(
                row_sums.astype(BF16), columns, (((1,), (1,)), ((), ())), preferred_element_type=F32
            )
        return carry

    copy.wait()
    lax.fori_loop(0, count[0], tile, 0)
    half = rows // 2
    for step in range(SIDE):
        start = lax.rem(vocab_y + step, SIDE) * SIDE
        for z in range(SIDE):
            value = total[start + z].astype(BF16)
            if step == 2:
                outs[3][z * half : z * half + half, :] = value[:half]
                outs[4][z * half : z * half + half, :] = value[half:]
            else:
                outs[step - step // 3][z * rows : z * rows + rows, :] = value
    if with_stats:
        sent = line[0:1] + line[1:2] + line[2:3]
        packed = pack_rows([before[0:1], before[1:2], sent, before[3:4], before[4:5]])
        for out in outs[3:]:
            out[SIDE * half : SIDE * half + 16, :] = packed


def products(place, pairs, count, probs, mine, other, before=None, behind=()):
    rows = probs.shape[0]
    depth, width = sum(part.shape[0] for part in mine) // SIDE, mine[0].shape[1]
    extra = [] if before is None else [before]
    scratch = [
        pltpu.VMEM((2 * SIDE, depth, width), BF16),
        pltpu.VMEM((SIDE * SIDE, rows, width), F32),
    ]
    if extra:
        scratch += [pltpu.VMEM((2, 64, 512), F32), pltpu.VMEM((8, rows), F32)]
    return pl.pallas_call(
        functools.partial(product_kernel, len(mine), bool(extra)),
        out_shape=[jax.ShapeDtypeStruct((SIDE * rows, width), BF16)] * 3
        + [jax.ShapeDtypeStruct((SIDE * rows // 2 + 16 * len(extra), width), BF16)] * 2,
        in_specs=[SMEM, SMEM, SMEM, ANY]
        + [VMEM] * (2 * len(mine) + len(extra))
        + [ANY] * len(behind),
        out_specs=[VMEM] * (SIDE + 1),
        scratch_shapes=scratch + [pltpu.VMEM(probs.shape, BF16), pltpu.SemaphoreType.DMA(())],
        compiler_params=params(24),
        cost_estimate=cost(
            16 * 2 * rows * 512 * width, 2 * probs.size + 16 * depth * width + 32 * rows * width
        ),
        name="tile_products",
    )(place, pairs, count, probs, *mine, *other, *extra, *behind)


def pack_rows(lines):
    rows = [part for line in lines for part in thirds(line)]
    rows.append(jnp.zeros((16 - len(rows), rows[0].shape[1]), F32))
    return jnp.concatenate(rows, axis=0).astype(BF16)


def unpack_rows(packed, number):
    packed = packed.astype(F32)
    return [
        packed[3 * i : 3 * i + 1] + packed[3 * i + 1 : 3 * i + 2] + packed[3 * i + 2 : 3 * i + 3]
        for i in range(number)
    ]


def joined(stats):
    peak = functools.reduce(jnp.maximum, [line[0] for line in stats])
    speak = functools.reduce(jnp.maximum, [line[3] for line in stats])
    factors = [jnp.exp(line[0] - peak) for line in stats]
    mass = sum(line[1] * factor for line, factor in zip(stats, factors))
    total = sum(line[2] * factor for line, factor in zip(stats, factors))
    smass = sum(line[4] * jnp.exp(line[3] - speak) for line in stats)
    return (peak, mass, total, speak, smass), factors


def columns_of(lines):
    lines = list(lines) + [jnp.zeros((128 - len(lines), lines[0].shape[1]), F32)]
    return jnp.concatenate(lines, axis=0).T


def relay_kernel(with_stats, *refs):
    if with_stats:
        near, far, from_left, from_right, mine = refs[:5]
        near_out, far_out, kept, table_out = refs[-4:]
        depth = from_left.shape[0] - 16
        rows = 2 * depth // SIDE
        stats = [unpack_rows(part[depth:, :], 5) for part in (mine, from_left, from_right)]
        kept[...] = jnp.concatenate(stats[0] + stats[1] + stats[2] + [jnp.zeros((1, rows), F32)], axis=0)
        own, left, right = (line[0] for line in stats)
        lane = lax.broadcasted_iota(jnp.int32, own.shape, 1)
        other = jnp.where(lane < rows // 2, left, right)
        peak = jnp.maximum(own, other)
        table = columns_of([jnp.exp(own - peak), jnp.exp(other - peak)])
        table_out[...] = table
        near_out[SIDE * rows : SIDE * rows + 16, :] = from_left[depth : depth + 16, :]
    else:
        near, far, from_left, from_right, table = refs[:5]
        near_out, far_out = refs[-2:]
        table = table[...]
        depth = from_left.shape[0]
        rows = 2 * depth // SIDE
    half = rows // 2
    for z in range(SIDE):
        low, high = slice(z * rows, z * rows + half), slice(z * rows + half, (z + 1) * rows)
        part = slice(z * half, (z + 1) * half)
        value = table[:half, 0:1] * near[low, :].astype(F32) + table[:half, 1:2] * from_left[part, :].astype(F32)
        near_out[low, :] = value.astype(BF16)
        near_out[high, :] = near[high, :]
        value = table[half:, 0:1] * far[high, :].astype(F32) + table[half:, 1:2] * from_right[part, :].astype(F32)
        far_out[high, :] = value.astype(BF16)
        far_out[low, :] = far[low, :]


def relayed(near, far, from_left, from_right, last, first, behind=()):
    depth, width = near.shape
    rows = depth // SIDE
    outs = [
        jax.ShapeDtypeStruct((depth + (16 if first else 0), width), BF16),
        jax.ShapeDtypeStruct((depth, width), BF16),
    ]
    if first:
        outs.append(jax.ShapeDtypeStruct((16, rows), F32))
        outs.append(jax.ShapeDtypeStruct((rows, 128), F32))
    return pl.pallas_call(
        functools.partial(relay_kernel, first),
        out_shape=outs,
        in_specs=[VMEM] * 5 + [ANY] * len(behind),
        out_specs=[VMEM] * len(outs),
        compiler_params=params(),
        cost_estimate=cost(depth * width, depth * width),
        name="relay_targets",
    )(near, far, from_left, from_right, last, *behind)


def merge_kernel(with_stats, place, given, *refs):
    parts = refs[:3]
    if with_stats:
        outs, kept = refs[-1 - SIDE : -1], refs[-1]
        rows = outs[0].shape[0] - 16
        lines = [[given[5 * i + j : 5 * i + j + 1] for j in range(5)] for i in range(3)]
        lines.append(unpack_rows(parts[1][SIDE * rows :, :], 5))
        stats, _ = joined(lines)
        packed = pack_rows(stats)
        for out in outs:
            out[rows : rows + 16, :] = packed
        own, left, right, across = (line[0] for line in lines)
        lane = lax.broadcasted_iota(jnp.int32, own.shape, 1)
        low = lane < rows // 2
        left = jnp.where(low, jnp.maximum(left, across), left)
        right = jnp.where(low, right, jnp.maximum(right, across))
        table = columns_of([jnp.exp(base - stats[0]) for base in (own, left, right)])
        kept[...] = table
    else:
        table, outs = given[...], refs[-SIDE:]
        rows = outs[0].shape[0]
    for step in range(SIDE):
        at = pl.ds(pl.multiple_of(lax.rem(place[1] + step, SIDE) * rows, rows), rows)
        value = table[:, 0:1] * parts[0][at, :].astype(F32)
        for d in range(1, 3):
            value += table[:, d : d + 1] * parts[d][at, :].astype(F32)
        outs[step][0:rows, :] = value.astype(BF16)


def merged(place, given, parts, rows, first, behind=()):
    width = parts[0].shape[1]
    outs = [jax.ShapeDtypeStruct((rows + (16 if first else 0), width), BF16)] * SIDE
    if first:
        outs = outs + [jax.ShapeDtypeStruct((rows, 128), F32)]
    return pl.pallas_call(
        functools.partial(merge_kernel, first),
        out_shape=outs,
        in_specs=[SMEM] + [VMEM] * 4 + [ANY] * len(behind),
        out_specs=[VMEM] * len(outs),
        compiler_params=params(),
        cost_estimate=cost(rows * width, rows * width),
        name="merge_targets",
    )(place, given, *parts, *behind)


def gradient_kernel(offset, with_stats, place, logits, *refs):
    if with_stats:
        parts, (grad, loss, kept) = refs[:SIDE], refs[-3:]
        rows = logits.shape[0]
        stats, factors = joined([unpack_rows(part[rows:, :], 5) for part in parts])
        _, mass, total, peak, smass = stats
        total = total / mass
        floored = jnp.maximum(total, 1.0)
        share = total / floored
        scales = [factor / mass / floored for factor in factors]
        table = columns_of(scales + [share / smass, peak, peak + jnp.log(smass)])
        kept[...] = table
    else:
        table, loss, earlier = refs[0][...], refs[1], refs[2]
        parts, grad = refs[3 : 3 + SIDE], refs[-1]
    rows, width = logits.shape[0], parts[0].shape[1]
    share, peak, norm = (table[:, c : c + 1] for c in range(4, 7))
    terms = jnp.zeros((rows, width), F32)
    for step in range(SIDE):
        block = lax.rem(place[1] + SIDE - step, SIDE)
        scores = logits[:, pl.ds(pl.multiple_of(block * 512 + offset, 128), width)]
        target = parts[step][0:rows, :].astype(F32) * table[:, step : step + 1]
        positive = target > 0
        entropy = jnp.where(positive, target * jnp.log(jnp.where(positive, target, 1.0)), 0.0)
        terms += entropy - target * (scores - norm)
        value = share * jnp.exp(scores - peak) - target
        if with_stats:
            at = pl.ds(pl.multiple_of(block * width, width), width)
        else:
            at = pl.ds(pl.multiple_of(block * 512 + offset, width), width)
        grad[at, :] = value.T.astype(BF16)
    sum_of_terms = jnp.sum(terms.T, axis=0, keepdims=True)
    if with_stats:
        loss[...] = jnp.broadcast_to(sum_of_terms, loss.shape)
    else:
        grad[SIDE * 512 :, :] = pack_rows([sum_of_terms + loss[0:1]])
        for block in range(SIDE):
            grad[block * 512 : block * 512 + offset, :] = earlier[block * offset : (block + 1) * offset, :]


def gradients(offset, place, logits, parts, before=(), behind=()):
    rows, width = logits.shape[0], parts[0].shape[1]
    first = not before
    outs = [jax.ShapeDtypeStruct((SIDE * width if first else SIDE * 512 + 16, rows), BF16)]
    if first:
        outs.append(jax.ShapeDtypeStruct((8, rows), F32))
        outs.append(jax.ShapeDtypeStruct((rows, 128), F32))
    return pl.pallas_call(
        functools.partial(gradient_kernel, offset, first),
        out_shape=outs,
        in_specs=[SMEM] + [VMEM] * (1 + SIDE + len(before)) + [ANY] * len(behind),
        out_specs=[VMEM] * len(outs),
        compiler_params=params(),
        cost_estimate=cost(rows * width, rows * width),
        name="logit_grad",
    )(place, logits, *before, *parts, *behind)


def stage_kernel(place, unembed, *refs):
    stage, sems = refs[-2:]
    first = place[3] == 0
    copies = []
    for major in range(SIDE):
        for minor in range(SIDE):
            index = major * SIDE + minor
            owner = jnp.where(first, index, minor * SIDE + major)
            start = pl.multiple_of(owner * 256 + place[3] * 128, 128)
            copies.append(
                pltpu.make_async_copy(
                    unembed.at[pl.ds(start, 128), :],
                    stage.at[pl.ds(index * 128, 128), :],
                    sems.at[index],
                )
            )
    for copy in copies:
        copy.start()
    for copy in copies:
        copy.wait()


def staged(place, unembed, behind):
    depth, cols = unembed.shape
    return pl.pallas_call(
        stage_kernel,
        out_shape=jax.ShapeDtypeStruct((depth // 2, cols), BF16),
        in_specs=[SMEM, pl.BlockSpec(memory_space=pltpu.HBM)] + [ANY] * len(behind),
        out_specs=VMEM,
        scratch_shapes=[pltpu.SemaphoreType.DMA((SIDE * SIDE,))],
        compiler_params=params(42),
        cost_estimate=cost(0, depth * cols),
        name="stage_unembed",
    )(place, unembed, *behind)


def own_kernel(stage, mine, out):
    depth = stage.shape[1]
    for step in range(SIDE):
        rows = slice(step * 512, step * 512 + 512)
        result = jnp.dot(stage[rows, :], mine[0:depth, :], preferred_element_type=F32)
        out[rows, :] = result.astype(BF16)


def own_hidden(stage, mine):
    depth, rows = stage.shape[0], mine.shape[1]
    return pl.pallas_call(
        own_kernel,
        out_shape=jax.ShapeDtypeStruct((depth, rows), BF16),
        in_specs=[VMEM, VMEM],
        out_specs=VMEM,
        compiler_params=params(),
        cost_estimate=cost(2 * stage.size * rows, 2 * stage.size),
        name="own_hidden",
    )(stage, mine)


def other_kernel(steps, place, stage, mine, other, own, *refs):
    outs = refs[-len(steps) :]
    depth = stage.shape[1]
    rows = mine.shape[1]
    lanes = pl.ds(pl.multiple_of(place[3] * rows, rows), rows)
    other_lanes = pl.ds(pl.multiple_of((1 - place[3]) * rows, rows), rows)
    for out, step in zip(outs, steps):
        at = pl.ds(pl.multiple_of(lax.rem(place[4] + step, SIDE) * 512, 512), 512)
        result = jnp.dot(stage[at, :], other[0:depth, :], preferred_element_type=F32)
        out[0:512, other_lanes] = result.astype(BF16)
        out[0:512, lanes] = own[at, :]
        out[512:528, lanes] = mine[depth : depth + 16, :]
        out[512:528, other_lanes] = other[depth : depth + 16, :]


def other_hidden(steps, place, stage, mine, other, own, behind=()):
    rows = mine.shape[1]
    return pl.pallas_call(
        functools.partial(other_kernel, steps),
        out_shape=[jax.ShapeDtypeStruct((528, 2 * rows), BF16)] * len(steps),
        in_specs=[SMEM] + [VMEM] * 4 + [ANY] * len(behind),
        out_specs=[VMEM] * len(steps),
        compiler_params=params(),
        cost_estimate=cost(len(steps) * stage.size * rows // 2, 2 * stage.size),
        name="other_hidden",
    )(place, stage, mine, other, own, *behind)


def packed_loss(index, parts, at, ordered):
    for step in range(SIDE):
        ordered[lax.rem(index + SIDE - step, SIDE)] = unpack_rows(parts[step][at : at + 16, :], 1)[0]
    return ((ordered[0] + ordered[1]) + ordered[2]) + ordered[3]


def middle_kernel(place, *refs):
    parts, outs, ordered = refs[:SIDE], refs[SIDE : 2 * SIDE], refs[2 * SIDE]
    packed = pack_rows([packed_loss(place[4], parts, 512, ordered)])
    for step in range(SIDE):
        at = pl.ds(pl.multiple_of(lax.rem(place[5] + step, SIDE) * 128, 128), 128)
        value = parts[0][at, :].astype(F32)
        for part in parts[1:]:
            value += part[at, :].astype(F32)
        outs[step][0:128, :] = value.astype(BF16)
        outs[step][128:144, :] = packed


def middle(place, parts):
    rows = parts[0].shape[1]
    return pl.pallas_call(
        middle_kernel,
        out_shape=[jax.ShapeDtypeStruct((144, rows), BF16)] * SIDE,
        in_specs=[SMEM] + [VMEM] * SIDE,
        out_specs=[VMEM] * SIDE,
        scratch_shapes=[pltpu.VMEM((SIDE, 1, rows), F32)],
        compiler_params=params(),
        cost_estimate=cost(4 * 512 * rows, 10 * 512 * rows),
        name="merge_grads",
    )(place, *parts)


def total_kernel(place, *refs):
    parts = refs[:SIDE]
    keep, give, loss, ordered = refs[SIDE:]
    rows = keep.shape[1]
    mine = pl.ds(pl.multiple_of(place[3] * rows, rows), rows)
    other = pl.ds(pl.multiple_of((1 - place[3]) * rows, rows), rows)
    ordered[4] = packed_loss(place[5], parts, 128, ordered)
    loss[...] = jnp.broadcast_to(ordered[4, :, mine], loss.shape)
    for lanes, out in ((other, give), (mine, keep)):
        value = parts[0][0:128, lanes].astype(F32)
        for part in parts[1:]:
            value += part[0:128, lanes].astype(F32)
        out[...] = value.astype(BF16)


def totals(place, parts):
    rows = parts[0].shape[1] // 2
    half = jax.ShapeDtypeStruct((128, rows), BF16)
    return pl.pallas_call(
        total_kernel,
        out_shape=[half, half, jax.ShapeDtypeStruct((8, rows), F32)],
        in_specs=[SMEM] + [VMEM] * SIDE,
        out_specs=[VMEM] * 3,
        scratch_shapes=[pltpu.VMEM((SIDE + 1, 1, 2 * rows), F32)],
        compiler_params=params(),
        cost_estimate=cost(8 * 128 * rows, 20 * 128 * rows),
        name="sum_grads",
    )(place, *parts)


def turn_kernel(place, keep, given, grad):
    mine = pl.ds(pl.multiple_of(place[3] * 128, 128), 128)
    other = pl.ds(pl.multiple_of((1 - place[3]) * 128, 128), 128)
    grad[:, mine] = keep[...].astype(F32).T.astype(BF16)
    grad[:, other] = given[...].astype(F32).T.astype(BF16)


def turned(place, keep, given):
    rows = keep.shape[1]
    return pl.pallas_call(
        turn_kernel,
        out_shape=jax.ShapeDtypeStruct((rows, 256), BF16),
        in_specs=[SMEM, VMEM, VMEM],
        out_specs=VMEM,
        compiler_params=params(),
        cost_estimate=cost(0, 4 * 256 * rows),
        name="turn_grads",
    )(place, keep, given)


def spread(parts, axis):
    return [parts[0]] + [send(parts[step], axis, step) for step in (1, 2, 3)]


def crossed(parts, first):
    def target(y, z, core, step):
        if (core == 0) == first:
            y = (y + step) % SIDE
        else:
            z = (z + step) % SIDE
        return (y * SIDE + z) * 2 + core

    places = [(y, z, core) for y in range(SIDE) for z in range(SIDE) for core in range(2)]
    received = [parts[0]]
    for step in (1, 2, 3):
        pairs = [(i, target(*at, step)) for i, at in enumerate(places)]
        received.append(lax.ppermute(parts[step], ("vy", "vz", "tc"), pairs))
    return received


def shards(teacher_logits, student_hidden, student_unembed, tile_weights, tile_pairs, tile_count):
    y, z, x, core = (lax.axis_index(name) for name in ("vy", "vz", "tx", "tc"))
    crossing = [jnp.where(core == 0, y, z), jnp.where(core == 0, z, y)]
    place = jnp.stack([y, z, x, core] + crossing).astype(jnp.int32)
    rows = teacher_logits.shape[0]
    teacher = teacher_logits.astype(F32)
    peak = jnp.max(teacher, axis=1)
    shifted = jnp.exp(teacher - peak[:, None])
    mass = jnp.sum(shifted, axis=1)
    probs = shifted.astype(BF16)

    logits = jnp.dot(student_hidden, student_unembed, preferred_element_type=F32)
    speak = jnp.max(logits, axis=1)
    smass = jnp.sum(jnp.exp(logits - speak[:, None]), axis=1)

    blank = jnp.zeros_like(peak)
    before = jnp.stack([peak, mass, blank, speak, smass, blank, blank, blank])

    width = tile_weights.shape[2] // 2
    piece = prepared(tile_weights, width)
    mine = [piece, *gated(spread([piece] * SIDE, "tx")[1:], [mass, smass])]
    other = [swap(piece) for piece in mine]

    piece = sliced(tile_weights, width, width, [mine[1]])
    right, left = send(piece, "tx", 1), send(piece, "tx", 3)
    parts = products(place, tile_pairs, tile_count, probs, mine, other, before, [piece])
    top, low = halves(right, left, [parts[0]])
    own, near, far, to_right, to_left = parts
    left_part, right_part = send(to_right, "vy", 1), send(to_left, "vy", 3)
    near, far, given, factors = relayed(near, far, left_part, right_part, to_right, True, [right, left])
    pieces = [piece, right, send(top, "tx", 1), send(low, "tx", 3), left]
    near, far = send(near, "vy", 1), send(far, "vy", 3)
    mine = packed_pieces(pieces, [near, far])
    later = products(place, tile_pairs, tile_count, probs, [mine], [swap(mine)])

    *parts, scales = merged(place, given, [own, near, far], rows, True, [later[0]])
    own, near, far, to_right, to_left = later
    left_part, right_part = send(to_right, "vy", 1), send(to_left, "vy", 3)
    stage = staged(place, student_unembed, [own])
    near, far = relayed(near, far, left_part, right_part, factors, False, [stage])
    later = [own, send(near, "vy", 1), send(far, "vy", 3)]
    grad, *before = gradients(0, place, logits, spread(parts, "vz"), (), later[1:])
    before = [before[1], before[0], grad]
    parts = merged(place, scales, later, rows, False)
    (mine,) = gradients(width, place, logits, spread(parts, "vz"), before)

    own = own_hidden(stage, mine)
    other = swap(mine)
    parts = other_hidden(range(SIDE), place, stage, mine, other, own)
    parts = middle(place, crossed(parts, True))
    keep, give, loss = totals(place, crossed(parts, False))
    return turned(place, keep, swap(give)), loss[0]


def solution(mesh):
    grid = Mesh(mesh.devices.reshape(SIDE, SIDE, SIDE, 2), ("vy", "vz", "tx", "tc"))
    vocab, tokens = ("vy", "vz"), ("tx", "tc")
    return jax.shard_map(
        shards,
        mesh=grid,
        in_specs=(
            P(tokens, vocab),
            P(tokens, None),
            P(None, vocab),
            P(vocab, tokens, None),
            P(vocab, None),
            P(vocab),
        ),
        out_specs=(P(tokens, vocab), P(tokens)),
        check_vma=False,
    )
```

```python
import functools

import jax
import jax.numpy as jnp
from jax import lax
from jax.experimental import pallas as pl
from jax.experimental.pallas import tpu as pltpu
from jax.sharding import Mesh
from jax.sharding import PartitionSpec as P

F32 = jnp.float32
BF16 = jnp.bfloat16
SIDE = 4
VMEM = pl.BlockSpec(memory_space=pltpu.VMEM)
SMEM = pl.BlockSpec(memory_space=pltpu.SMEM)
ANY = pl.BlockSpec(memory_space=pl.ANY)
MIB = 1024 * 1024


def params(mib=16):
    return pltpu.CompilerParams(vmem_limit_bytes=mib * MIB)


def cost(flops, moved, transcendentals=0):
    return pl.CostEstimate(flops=flops, bytes_accessed=moved, transcendentals=transcendentals)


def send(value, axis, step):
    return lax.ppermute(value, axis, [(i, (i + step) % SIDE) for i in range(SIDE)])


def swap(value):
    return lax.ppermute(value, "tc", [(0, 1), (1, 0)])


def thirds(value):
    high = value.astype(BF16).astype(F32)
    rest = value - high
    middle = rest.astype(BF16).astype(F32)
    return high, middle, rest - middle


def prepare_kernel(weights, piece):
    slots, shard_rows, _ = weights.shape
    width = piece.shape[1]
    rows = slots * shard_rows
    piece[0:rows, :] = weights[:, :, 0:width].reshape(rows, width)
    sums = jnp.sum(weights[...].astype(F32), axis=2, keepdims=True).reshape(rows, 1)
    line = jnp.broadcast_to(sums, (rows, 128)).T[0:1]
    lines = jnp.concatenate(list(thirds(line)) + [jnp.zeros((5, rows), F32)], axis=0)
    extra = jnp.concatenate([lines[:, i * 128 : (i + 1) * 128] for i in range(8)], axis=0)
    if width > 128:
        extra = jnp.concatenate([extra, jnp.zeros((64, width - 128), F32)], axis=1)
    piece[rows : rows + 64, :] = extra.astype(BF16)


def prepared(weights):
    slots, shard_rows, width = weights.shape
    return pl.pallas_call(
        prepare_kernel,
        out_shape=jax.ShapeDtypeStruct((slots * shard_rows + 64, width), BF16),
        in_specs=[VMEM],
        out_specs=VMEM,
        compiler_params=params(),
        cost_estimate=cost(2 * weights.size, 3 * weights.size),
        name="prepare_weights",
    )(weights)


def halves_kernel(right, left, *refs):
    top, low = refs[-2:]
    top[...] = right[0 : top.shape[0], :]
    low[...] = left[top.shape[0] :, :]


def halves(right, left, behind):
    depth, width = right.shape
    outs = [jax.ShapeDtypeStruct((rows, width), BF16) for rows in (512, depth - 512)]
    return pl.pallas_call(
        halves_kernel,
        out_shape=outs,
        in_specs=[VMEM, VMEM] + [ANY] * len(behind),
        out_specs=[VMEM, VMEM],
        compiler_params=params(),
        cost_estimate=cost(0, 4 * depth * width),
        name="take_halves",
    )(right, left, *behind)


def product_kernel(place, pairs, count, probs, before, *rest):
    pieces, outs = rest[:10], rest[10:15]
    across, total, sums, line, seen = rest[15:]
    mine = [pieces[0], pieces[1], across.at[0], pieces[2]]
    other = [pieces[5], pieces[6], across.at[1], pieces[7]]
    for core in range(2):
        across[core, 0:512] = pieces[5 * core + 3][...]
        across[core, 512:] = pieces[5 * core + 4][...]
    block = 512
    rows = probs.shape[0]
    half = rows // 2
    vocab_y = place[0]
    first_block = (vocab_y * SIDE + place[1]) * (probs.shape[1] // block)
    core_0 = place[3] == 0

    def in_order(step, at):
        one, two = mine[step][at, :], other[step][at, :]
        return jnp.where(core_0, one, two), jnp.where(core_0, two, one)

    line[...] = jnp.zeros_like(line)
    lane = lax.broadcasted_iota(jnp.int32, (64, 128), 1)
    for step in range(SIDE):
        even, odd = in_order(step, slice(1024, 1088))
        even, odd = even[:, 0:128].astype(F32), odd[:, 0:128].astype(F32)
        x = lax.rem(place[2] + SIDE - step, SIDE)
        lanes = pl.ds(pl.multiple_of(x * 128, 128), 128)
        sums[0, :, lanes] = jnp.where(lane < 64, even, pltpu.roll(odd, 64, 1))
        sums[1, :, lanes] = jnp.where(lane < 64, pltpu.roll(even, 64, 1), odd)
    for owner in range(SIDE * SIDE):
        seen[owner] = 0

    def tile(slot, carry):
        teacher = pairs[slot, 0] - first_block
        owner = pairs[slot, 1] // SIDE
        at = pl.ds(pl.multiple_of(slot * 64, 64), 64)
        matrix, columns = [], []
        for step in range(SIDE):
            matrix.extend(in_order(step, at))
            x = lax.rem(place[2] + SIDE - step, SIDE)
            columns.append(probs[:, pl.ds(pl.multiple_of(teacher * block + x * 128, 128), 128)])
        product = jnp.dot(
            jnp.concatenate(columns, axis=1), jnp.concatenate(matrix, axis=0), preferred_element_type=F32
        )
        row_sums = sums[lax.rem(slot, 2), pl.ds(pl.multiple_of(slot // 2 * 8, 8), 8), :]
        line[...] += lax.dot_general(
            row_sums.astype(BF16),
            probs[:, pl.ds(pl.multiple_of(teacher * block, block), block)],
            (((1,), (1,)), ((), ())),
            preferred_element_type=F32,
        )
        fresh = seen[owner] == 0

        @pl.when(fresh)
        def _():
            total[owner] = product

        @pl.when(jnp.logical_not(fresh))
        def _():
            total[owner] += product

        seen[owner] = 1
        return carry

    lax.fori_loop(0, count[0], tile, 0)
    for step in range(SIDE):
        start = lax.rem(vocab_y + step, SIDE) * SIDE
        for z in range(SIDE):
            used = seen[start + z] == 1

            def put(value):
                if step == 2:
                    outs[3][z * half : z * half + half, :] = value[:half]
                    outs[4][z * half : z * half + half, :] = value[half:]
                else:
                    outs[step - step // 3][z * rows : z * rows + rows, :] = value

            @pl.when(used)
            def _():
                put(total[start + z].astype(BF16))

            @pl.when(jnp.logical_not(used))
            def _():
                put(jnp.zeros(total.shape[1:], BF16))

    sent = line[0:1] + line[1:2] + line[2:3]
    packed = pack_rows([before[0:1], before[1:2], sent, before[3:4], before[4:5]])
    for out in outs[3:]:
        put_rows(out, SIDE * half, packed)


def put_rows(out, at, packed):
    wide = jnp.zeros((16, out.shape[1] - packed.shape[1]), BF16)
    out[at : at + 16, :] = jnp.concatenate([packed, wide], axis=1)


def products(place, pairs, count, probs, before, pieces):
    rows = probs.shape[0]
    depth, width = pieces[0].shape
    return pl.pallas_call(
        product_kernel,
        out_shape=[jax.ShapeDtypeStruct((SIDE * rows, width), BF16)] * 3
        + [jax.ShapeDtypeStruct((SIDE * rows // 2 + 16, width), BF16)] * 2,
        in_specs=[SMEM, SMEM, SMEM] + [VMEM] * (2 + len(pieces)),
        out_specs=[VMEM] * (SIDE + 1),
        scratch_shapes=[
            pltpu.VMEM((2, depth, width), BF16),
            pltpu.VMEM((SIDE * SIDE, rows, width), F32),
            pltpu.VMEM((2, 64, 512), F32),
            pltpu.VMEM((8, rows), F32),
            pltpu.SMEM((SIDE * SIDE,), jnp.int32),
        ],
        compiler_params=params(20),
        cost_estimate=cost(
            16 * 2 * rows * 512 * width, 2 * probs.size + 16 * depth * width + 32 * rows * width
        ),
        name="tile_products",
    )(place, pairs, count, probs, before, *pieces)


def pack_rows(lines):
    rows = [part for line in lines for part in thirds(line)]
    rows.append(jnp.zeros((16 - len(rows), rows[0].shape[1]), F32))
    return jnp.concatenate(rows, axis=0).astype(BF16)


def unpack_rows(packed, number):
    packed = packed.astype(F32)
    return [
        packed[3 * i : 3 * i + 1] + packed[3 * i + 1 : 3 * i + 2] + packed[3 * i + 2 : 3 * i + 3]
        for i in range(number)
    ]


def joined(stats):
    peak = functools.reduce(jnp.maximum, [line[0] for line in stats])
    speak = functools.reduce(jnp.maximum, [line[3] for line in stats])
    factors = [jnp.exp(line[0] - peak) for line in stats]
    mass = sum(line[1] * factor for line, factor in zip(stats, factors))
    total = sum(line[2] * factor for line, factor in zip(stats, factors))
    smass = sum(line[4] * jnp.exp(line[3] - speak) for line in stats)
    return (peak, mass, total, speak, smass), factors


def columns_of(lines):
    lines = list(lines) + [jnp.zeros((128 - len(lines), lines[0].shape[1]), F32)]
    return jnp.concatenate(lines, axis=0).T


def relay_kernel(near, far, from_left, from_right, mine, *refs):
    near_out, far_out, kept = refs[-3:]
    depth = from_left.shape[0] - 16
    half = depth // SIDE
    rows = 2 * half
    stats = [unpack_rows(part[depth:, 0:rows], 5) for part in (mine, from_left, from_right)]
    kept[...] = jnp.concatenate(stats[0] + stats[1] + stats[2] + [jnp.zeros((1, rows), F32)], axis=0)
    own, left, right = (line[0] for line in stats)
    lane = lax.broadcasted_iota(jnp.int32, own.shape, 1)
    other = jnp.where(lane < half, left, right)
    peak = jnp.maximum(own, other)
    table = columns_of([jnp.exp(own - peak), jnp.exp(other - peak)])
    near_out[SIDE * rows : SIDE * rows + 16, :] = from_left[depth : depth + 16, :]
    for z in range(SIDE):
        low, high = slice(z * rows, z * rows + half), slice(z * rows + half, (z + 1) * rows)
        part = slice(z * half, (z + 1) * half)
        value = table[:half, 0:1] * near[low, :].astype(F32) + table[:half, 1:2] * from_left[part, :].astype(F32)
        near_out[low, :] = value.astype(BF16)
        near_out[high, :] = near[high, :]
        value = table[half:, 0:1] * far[high, :].astype(F32) + table[half:, 1:2] * from_right[part, :].astype(F32)
        far_out[high, :] = value.astype(BF16)
        far_out[low, :] = far[low, :]


def relayed(near, far, from_left, from_right, last, behind):
    depth, width = near.shape
    rows = depth // SIDE
    return pl.pallas_call(
        relay_kernel,
        out_shape=[
            jax.ShapeDtypeStruct((depth + 16, width), BF16),
            jax.ShapeDtypeStruct((depth, width), BF16),
            jax.ShapeDtypeStruct((16, rows), F32),
        ],
        in_specs=[VMEM] * 5 + [ANY] * len(behind),
        out_specs=[VMEM] * 3,
        compiler_params=params(),
        cost_estimate=cost(depth * width, 8 * depth * width),
        name="relay_targets",
    )(near, far, from_left, from_right, last, *behind)


def merge_kernel(place, given, *refs):
    parts, outs = refs[:3], refs[3:]
    rows = outs[0].shape[0] - 16
    lines = [[given[5 * i + j : 5 * i + j + 1] for j in range(5)] for i in range(3)]
    lines.append(unpack_rows(parts[1][SIDE * rows :, 0:rows], 5))
    stats, _ = joined(lines)
    packed = pack_rows(stats)
    own, left, right, across = (line[0] for line in lines)
    lane = lax.broadcasted_iota(jnp.int32, own.shape, 1)
    low = lane < rows // 2
    left = jnp.where(low, jnp.maximum(left, across), left)
    right = jnp.where(low, right, jnp.maximum(right, across))
    table = columns_of([jnp.exp(base - stats[0]) for base in (own, left, right)])
    for step in range(SIDE):
        at = pl.ds(pl.multiple_of(lax.rem(place[1] + step, SIDE) * rows, rows), rows)
        value = table[:, 0:1] * parts[0][at, :].astype(F32)
        for d in range(1, 3):
            value += table[:, d : d + 1] * parts[d][at, :].astype(F32)
        outs[step][0:rows, :] = value.astype(BF16)
        put_rows(outs[step], rows, packed)


def merged(place, given, parts, rows):
    width = parts[0].shape[1]
    return pl.pallas_call(
        merge_kernel,
        out_shape=[jax.ShapeDtypeStruct((rows + 16, width), BF16)] * SIDE,
        in_specs=[SMEM] + [VMEM] * 4,
        out_specs=[VMEM] * SIDE,
        compiler_params=params(),
        cost_estimate=cost(32 * rows * width, 40 * rows * width),
        name="merge_targets",
    )(place, given, *parts)


def gradient_kernel(place, logits, *refs):
    parts, grad = refs[:SIDE], refs[SIDE]
    rows, width = logits.shape[0], parts[0].shape[1]
    stats, factors = joined([unpack_rows(part[rows:, 0:rows], 5) for part in parts])
    _, mass, total, peak, smass = stats
    total = total / mass
    floored = jnp.maximum(total, 1.0)
    scales = [factor / mass / floored for factor in factors]
    table = columns_of(scales + [total / floored / smass, peak, peak + jnp.log(smass)])
    share, peak, norm = (table[:, c : c + 1] for c in range(4, 7))
    terms = jnp.zeros((rows, width), F32)
    for step in range(SIDE):
        block = lax.rem(place[1] + SIDE - step, SIDE)
        at = pl.ds(pl.multiple_of(block * width, width), width)
        scores = logits[:, at]
        target = parts[step][0:rows, :].astype(F32) * table[:, step : step + 1]
        positive = target > 0
        entropy = jnp.where(positive, target * jnp.log(jnp.where(positive, target, 1.0)), 0.0)
        terms += entropy - target * (scores - norm)
        value = share * jnp.exp(scores - peak) - target
        grad[at, :] = value.T.astype(BF16)
    grad[SIDE * width :, :] = pack_rows([jnp.sum(terms.T, axis=0, keepdims=True)])


def gradients(place, logits, parts):
    rows, cols = logits.shape
    return pl.pallas_call(
        gradient_kernel,
        out_shape=jax.ShapeDtypeStruct((cols + 16, rows), BF16),
        in_specs=[SMEM] + [VMEM] * (1 + SIDE),
        out_specs=VMEM,
        compiler_params=params(),
        cost_estimate=cost(60 * rows * cols, 8 * rows * cols, 2 * rows * cols),
        name="logit_grad",
    )(place, logits, *parts)


def stage_kernel(place, unembed, *refs):
    stage, sems = refs[-2:]
    first = place[3] == 0
    copies = []
    for major in range(SIDE):
        for minor in range(SIDE):
            index = major * SIDE + minor
            owner = jnp.where(first, index, minor * SIDE + major)
            start = pl.multiple_of(owner * 256 + place[3] * 128, 128)
            copies.append(
                pltpu.make_async_copy(
                    unembed.at[pl.ds(start, 128), :],
                    stage.at[pl.ds(index * 128, 128), :],
                    sems.at[index],
                )
            )
    for copy in copies:
        copy.start()
    for copy in copies:
        copy.wait()


def staged(place, unembed, behind):
    depth, cols = unembed.shape
    return pl.pallas_call(
        stage_kernel,
        out_shape=jax.ShapeDtypeStruct((depth // 2, cols), BF16),
        in_specs=[SMEM, pl.BlockSpec(memory_space=pltpu.HBM)] + [ANY] * len(behind),
        out_specs=VMEM,
        scratch_shapes=[pltpu.SemaphoreType.DMA((SIDE * SIDE,))],
        compiler_params=params(42),
        cost_estimate=cost(0, depth * cols),
        name="stage_unembed",
    )(place, unembed, *behind)


def own_kernel(stage, mine, out):
    depth = stage.shape[1]
    for step in range(SIDE):
        rows = slice(step * 512, step * 512 + 512)
        result = jnp.dot(stage[rows, :], mine[0:depth, :], preferred_element_type=F32)
        out[rows, :] = result.astype(BF16)


def own_hidden(stage, mine):
    depth, rows = stage.shape[0], mine.shape[1]
    return pl.pallas_call(
        own_kernel,
        out_shape=jax.ShapeDtypeStruct((depth, rows), BF16),
        in_specs=[VMEM, VMEM],
        out_specs=VMEM,
        compiler_params=params(),
        cost_estimate=cost(2 * stage.size * rows, 2 * stage.size),
        name="own_hidden",
    )(stage, mine)


def other_kernel(steps, place, stage, mine, other, own, *refs):
    outs = refs[-len(steps) :]
    depth = stage.shape[1]
    rows = mine.shape[1]
    lanes = pl.ds(pl.multiple_of(place[3] * rows, rows), rows)
    other_lanes = pl.ds(pl.multiple_of((1 - place[3]) * rows, rows), rows)
    for out, step in zip(outs, steps):
        at = pl.ds(pl.multiple_of(lax.rem(place[4] + step, SIDE) * 512, 512), 512)
        result = jnp.dot(stage[at, :], other[0:depth, :], preferred_element_type=F32)
        out[0:512, other_lanes] = result.astype(BF16)
        out[0:512, lanes] = own[at, :]
        out[512:528, lanes] = mine[depth : depth + 16, :]
        out[512:528, other_lanes] = other[depth : depth + 16, :]


def other_hidden(steps, place, stage, mine, other, own, behind=()):
    rows = mine.shape[1]
    return pl.pallas_call(
        functools.partial(other_kernel, steps),
        out_shape=[jax.ShapeDtypeStruct((528, 2 * rows), BF16)] * len(steps),
        in_specs=[SMEM] + [VMEM] * 4 + [ANY] * len(behind),
        out_specs=[VMEM] * len(steps),
        compiler_params=params(),
        cost_estimate=cost(len(steps) * stage.size * rows // 2, 2 * stage.size),
        name="other_hidden",
    )(place, stage, mine, other, own, *behind)


def packed_loss(index, parts, at, ordered):
    for step in range(SIDE):
        ordered[lax.rem(index + SIDE - step, SIDE)] = unpack_rows(parts[step][at : at + 16, :], 1)[0]
    return ((ordered[0] + ordered[1]) + ordered[2]) + ordered[3]


def middle_kernel(place, *refs):
    parts, outs, ordered = refs[:SIDE], refs[SIDE : 2 * SIDE], refs[2 * SIDE]
    packed = pack_rows([packed_loss(place[4], parts, 512, ordered)])
    for step in range(SIDE):
        at = pl.ds(pl.multiple_of(lax.rem(place[5] + step, SIDE) * 128, 128), 128)
        value = parts[0][at, :].astype(F32)
        for part in parts[1:]:
            value += part[at, :].astype(F32)
        outs[step][0:128, :] = value.astype(BF16)
        outs[step][128:144, :] = packed


def middle(place, parts):
    rows = parts[0].shape[1]
    return pl.pallas_call(
        middle_kernel,
        out_shape=[jax.ShapeDtypeStruct((144, rows), BF16)] * SIDE,
        in_specs=[SMEM] + [VMEM] * SIDE,
        out_specs=[VMEM] * SIDE,
        scratch_shapes=[pltpu.VMEM((SIDE, 1, rows), F32)],
        compiler_params=params(),
        cost_estimate=cost(4 * 512 * rows, 10 * 512 * rows),
        name="merge_grads",
    )(place, *parts)


def total_kernel(place, *refs):
    parts = refs[:SIDE]
    keep, give, loss, ordered = refs[SIDE:]
    rows = keep.shape[1]
    mine = pl.ds(pl.multiple_of(place[3] * rows, rows), rows)
    other = pl.ds(pl.multiple_of((1 - place[3]) * rows, rows), rows)
    ordered[4] = packed_loss(place[5], parts, 128, ordered)
    loss[...] = jnp.broadcast_to(ordered[4, :, mine], loss.shape)
    for lanes, out in ((other, give), (mine, keep)):
        value = parts[0][0:128, lanes].astype(F32)
        for part in parts[1:]:
            value += part[0:128, lanes].astype(F32)
        out[...] = value.astype(BF16)


def totals(place, parts):
    rows = parts[0].shape[1] // 2
    half = jax.ShapeDtypeStruct((128, rows), BF16)
    return pl.pallas_call(
        total_kernel,
        out_shape=[half, half, jax.ShapeDtypeStruct((8, rows), F32)],
        in_specs=[SMEM] + [VMEM] * SIDE,
        out_specs=[VMEM] * 3,
        scratch_shapes=[pltpu.VMEM((SIDE + 1, 1, 2 * rows), F32)],
        compiler_params=params(),
        cost_estimate=cost(8 * 128 * rows, 20 * 128 * rows),
        name="sum_grads",
    )(place, *parts)


def turn_kernel(place, keep, given, grad):
    mine = pl.ds(pl.multiple_of(place[3] * 128, 128), 128)
    other = pl.ds(pl.multiple_of((1 - place[3]) * 128, 128), 128)
    grad[:, mine] = keep[...].astype(F32).T.astype(BF16)
    grad[:, other] = given[...].astype(F32).T.astype(BF16)


def turned(place, keep, given):
    rows = keep.shape[1]
    return pl.pallas_call(
        turn_kernel,
        out_shape=jax.ShapeDtypeStruct((rows, 256), BF16),
        in_specs=[SMEM, VMEM, VMEM],
        out_specs=VMEM,
        compiler_params=params(),
        cost_estimate=cost(0, 4 * 256 * rows),
        name="turn_grads",
    )(place, keep, given)


def spread(parts, axis):
    return [parts[0]] + [send(parts[step], axis, step) for step in (1, 2, 3)]


def crossed(parts, first):
    def target(y, z, core, step):
        if (core == 0) == first:
            y = (y + step) % SIDE
        else:
            z = (z + step) % SIDE
        return (y * SIDE + z) * 2 + core

    places = [(y, z, core) for y in range(SIDE) for z in range(SIDE) for core in range(2)]
    received = [parts[0]]
    for step in (1, 2, 3):
        pairs = [(i, target(*at, step)) for i, at in enumerate(places)]
        received.append(lax.ppermute(parts[step], ("vy", "vz", "tc"), pairs))
    return received


def shards(teacher_logits, student_hidden, student_unembed, tile_weights, tile_pairs, tile_count):
    y, z, x, core = (lax.axis_index(name) for name in ("vy", "vz", "tx", "tc"))
    crossing = [jnp.where(core == 0, y, z), jnp.where(core == 0, z, y)]
    place = jnp.stack([y, z, x, core] + crossing).astype(jnp.int32)
    rows = teacher_logits.shape[0]
    teacher = teacher_logits.astype(F32)
    peak = jnp.max(teacher, axis=1)
    shifted = jnp.exp(teacher - peak[:, None])
    mass = jnp.sum(shifted, axis=1)
    probs = shifted.astype(BF16)

    logits = jnp.dot(student_hidden, student_unembed, preferred_element_type=F32)
    speak = jnp.max(logits, axis=1)
    smass = jnp.sum(jnp.exp(logits - speak[:, None]), axis=1)

    blank = jnp.zeros_like(peak)
    before = jnp.stack([peak, mass, blank, speak, smass, blank, blank, blank])

    piece = prepared(tile_weights)
    right, left = send(piece, "tx", 1), send(piece, "tx", 3)
    top, low = halves(right, left, [mass, smass])
    pieces = [piece, right, left, send(top, "tx", 1), send(low, "tx", 3)]
    pieces = pieces + [swap(piece) for piece in pieces]

    own, near, far, to_right, to_left = products(
        place, tile_pairs, tile_count, probs, before, pieces
    )
    stage = staged(place, student_unembed, [own])
    left_part, right_part = send(to_right, "vy", 1), send(to_left, "vy", 3)
    near, far, given = relayed(near, far, left_part, right_part, to_right, [stage])
    parts = merged(place, given, [own, send(near, "vy", 1), send(far, "vy", 3)], rows)
    mine = gradients(place, logits, spread(parts, "vz"))

    own = own_hidden(stage, mine)
    other = swap(mine)
    parts = other_hidden(range(SIDE), place, stage, mine, other, own)
    parts = middle(place, crossed(parts, True))
    keep, give, loss = totals(place, crossed(parts, False))
    return turned(place, keep, swap(give)), loss[0]


def solution(mesh):
    grid = Mesh(mesh.devices.reshape(SIDE, SIDE, SIDE, 2), ("vy", "vz", "tx", "tc"))
    vocab, tokens = ("vy", "vz"), ("tx", "tc")
    return jax.shard_map(
        shards,
        mesh=grid,
        in_specs=(
            P(tokens, vocab),
            P(tokens, None),
            P(None, vocab),
            P(vocab, tokens, None),
            P(vocab, None),
            P(vocab),
        ),
        out_specs=(P(tokens, vocab), P(tokens)),
        check_vma=False,
    )
```

```python
import functools

import jax
import jax.numpy as jnp
from jax import lax
from jax.experimental import pallas as pl
from jax.experimental.pallas import tpu as pltpu
from jax.sharding import Mesh
from jax.sharding import PartitionSpec as P

F32 = jnp.float32
BF16 = jnp.bfloat16
SIDE = 4
VMEM = pl.BlockSpec(memory_space=pltpu.VMEM)
SMEM = pl.BlockSpec(memory_space=pltpu.SMEM)
ANY = pl.BlockSpec(memory_space=pl.ANY)
MIB = 1024 * 1024


def params(mib=16):
    return pltpu.CompilerParams(vmem_limit_bytes=mib * MIB)


def cost(flops, moved, transcendentals=0):
    return pl.CostEstimate(flops=flops, bytes_accessed=moved, transcendentals=transcendentals)


def send(value, axis, step):
    return lax.ppermute(value, axis, [(i, (i + step) % SIDE) for i in range(SIDE)])


def swap(value):
    return lax.ppermute(value, "tc", [(0, 1), (1, 0)])


def thirds(value):
    high = value.astype(BF16).astype(F32)
    rest = value - high
    middle = rest.astype(BF16).astype(F32)
    return high, middle, rest - middle


def slice_kernel(weights, *refs):
    piece = refs[-1]
    piece[...] = weights[...].reshape(piece.shape)


def sliced(weights, index, behind=()):
    slots, shard_rows, cols = weights.shape
    width = cols // 2
    return pl.pallas_call(
        slice_kernel,
        grid=(1,),
        out_shape=jax.ShapeDtypeStruct((slots * shard_rows, width), BF16),
        in_specs=[pl.BlockSpec((slots, shard_rows, width), lambda i: (0, 0, index))]
        + [ANY] * len(behind),
        out_specs=pl.BlockSpec((slots * shard_rows, width), lambda i: (0, 0)),
        compiler_params=params(),
        cost_estimate=cost(0, 2 * weights.size),
        name="slice_weights",
    )(weights, *behind)


def gate_kernel(*refs):
    pass


def gated(parts, behind):
    return pl.pallas_call(
        gate_kernel,
        out_shape=[jax.ShapeDtypeStruct(part.shape, part.dtype) for part in parts],
        in_specs=[ANY] * (len(parts) + len(behind)),
        out_specs=[ANY] * len(parts),
        input_output_aliases={i: i for i in range(len(parts))},
        compiler_params=params(),
        cost_estimate=cost(0, 0),
        name="gate",
    )(*parts, *behind)


def pack_kernel(number, *refs):
    out = refs[-1]
    at = 0
    for part in refs[:number]:
        out[at : at + part.shape[0], :] = part[...]
        at += part.shape[0]


def packed_pieces(parts, behind):
    depth = sum(part.shape[0] for part in parts)
    width = parts[0].shape[1]
    return pl.pallas_call(
        functools.partial(pack_kernel, len(parts)),
        out_shape=jax.ShapeDtypeStruct((depth, width), BF16),
        in_specs=[VMEM] * len(parts) + [ANY] * len(behind),
        out_specs=VMEM,
        compiler_params=params(),
        cost_estimate=cost(0, 4 * depth * width),
        name="pack_weights",
    )(*parts, *behind)


def halves_kernel(right, left, *refs):
    top, low = refs[-2:]
    top[...] = right[...]
    low[...] = left[...]


def halves(right, left, behind):
    depth, width = right.shape
    shape = (depth // 2, width)
    return pl.pallas_call(
        halves_kernel,
        grid=(1,),
        out_shape=[jax.ShapeDtypeStruct(shape, BF16)] * 2,
        in_specs=[
            pl.BlockSpec(shape, lambda i: (0, 0)),
            pl.BlockSpec(shape, lambda i: (1, 0)),
        ]
        + [ANY] * len(behind),
        out_specs=[pl.BlockSpec(shape, lambda i: (0, 0))] * 2,
        compiler_params=params(),
        cost_estimate=cost(0, 4 * depth * width),
        name="take_halves",
    )(right, left, *behind)


def product_kernel(number, later, place, pairs, count, probs, before, *rest):
    pieces, (across, total, seen) = rest[:number], rest[-3:]
    outs = rest[-9:-4] if not later else rest[-8:-3]
    half_number = number // 2
    mine, other = list(pieces[:half_number]), list(pieces[half_number:])
    if half_number == 5:
        for core, parts in enumerate((mine, other)):
            across[core, 0:512] = parts[3][...]
            across[core, 512:1024] = parts[4][...]
            parts[2:] = [across.at[core], parts[2]]
    block = 512
    rows, width = probs.shape[0], total.shape[2]
    half = rows // 2
    vocab_y = place[0]
    first_block = (vocab_y * SIDE + place[1]) * (probs.shape[1] // block)
    core_0 = place[3] == 0
    for owner in range(SIDE * SIDE):
        seen[owner] = 0

    def tile(slot, carry):
        teacher = pairs[slot, 0] - first_block
        owner = pairs[slot, 1] // SIDE
        at = pl.ds(pl.multiple_of(slot * 64, 64), 64)
        matrix, columns = [], []
        for step in range(SIDE):
            one, two = mine[step][at, :], other[step][at, :]
            matrix += [jnp.where(core_0, one, two), jnp.where(core_0, two, one)]
            x = lax.rem(place[2] + SIDE - step, SIDE)
            columns.append(probs[:, pl.ds(pl.multiple_of(teacher * block + x * 128, 128), 128)])
        product = jnp.dot(
            jnp.concatenate(columns, axis=1), jnp.concatenate(matrix, axis=0), preferred_element_type=F32
        )
        fresh = seen[owner] == 0

        @pl.when(fresh)
        def _():
            total[owner] = product

        @pl.when(jnp.logical_not(fresh))
        def _():
            total[owner] += product

        seen[owner] = 1
        return carry

    lax.fori_loop(0, count[0], tile, 0)
    summed = total.at[SIDE * SIDE]
    summed[...] = jnp.zeros(summed.shape, F32)
    for step in range(SIDE):
        start = lax.rem(vocab_y + step, SIDE) * SIDE
        for z in range(SIDE):
            used = seen[start + z] == 1

            def put(value):
                if step == 2:
                    outs[3][z * half : z * half + half, :] = value[:half]
                    outs[4][z * half : z * half + half, :] = value[half:]
                else:
                    outs[step - step // 3][z * rows : z * rows + rows, :] = value

            @pl.when(used)
            def _():
                value = total[start + z]
                summed[...] += value
                put(value.astype(BF16))

            @pl.when(jnp.logical_not(used))
            def _():
                put(jnp.zeros((rows, width), BF16))

    line = jnp.sum(summed[...].T, axis=0, keepdims=True)
    if later:
        packed = pack_rows([line + before[0:1]])
    else:
        rest[-4][...] = jnp.broadcast_to(line, rest[-4].shape)
        packed = pack_rows([before[i : i + 1] for i in range(4)])
    for out in outs[3:]:
        out[SIDE * half : SIDE * half + 16, :] = packed


def products(place, pairs, count, probs, before, mine, other, later, behind=()):
    rows = probs.shape[0]
    depth, width = mine[0].shape
    pieces = [*mine, *other]
    outs = [jax.ShapeDtypeStruct((SIDE * rows, width), BF16)] * 3
    outs += [jax.ShapeDtypeStruct((SIDE * rows // 2 + 16, width), BF16)] * 2
    if not later:
        outs.append(jax.ShapeDtypeStruct((8, rows), F32))
    return pl.pallas_call(
        functools.partial(product_kernel, len(pieces), later),
        out_shape=outs,
        in_specs=[SMEM, SMEM, SMEM] + [VMEM] * (2 + len(pieces)) + [ANY] * len(behind),
        out_specs=[VMEM] * len(outs),
        scratch_shapes=[
            pltpu.VMEM((2, depth if later else 16, width), BF16),
            pltpu.VMEM((SIDE * SIDE + 1, rows, width), F32),
            pltpu.SMEM((SIDE * SIDE,), jnp.int32),
        ],
        compiler_params=params(12),
        cost_estimate=cost(
            16 * 2 * rows * 512 * width, 2 * probs.size + 16 * depth * width + 32 * rows * width
        ),
        name="tile_products",
    )(place, pairs, count, probs, before, *pieces, *behind)


def pack_rows(lines):
    rows = [part for line in lines for part in thirds(line)]
    rows.append(jnp.zeros((16 - len(rows), rows[0].shape[1]), F32))
    return jnp.concatenate(rows, axis=0).astype(BF16)


def unpack_rows(packed, number):
    packed = packed.astype(F32)
    return [
        packed[3 * i : 3 * i + 1] + packed[3 * i + 1 : 3 * i + 2] + packed[3 * i + 2 : 3 * i + 3]
        for i in range(number)
    ]


def joined(stats):
    peak = functools.reduce(jnp.maximum, [line[0] for line in stats])
    speak = functools.reduce(jnp.maximum, [line[2] for line in stats])
    factors = [jnp.exp(line[0] - peak) for line in stats]
    mass = sum(line[1] * factor for line, factor in zip(stats, factors))
    smass = sum(line[3] * jnp.exp(line[2] - speak) for line in stats)
    return (peak, mass, speak, smass), factors


def columns_of(lines):
    lines = list(lines) + [jnp.zeros((128 - len(lines), lines[0].shape[1]), F32)]
    return jnp.concatenate(lines, axis=0).T


def relay_kernel(later, near, far, from_left, from_right, mine, *refs):
    depth = from_left.shape[0] - 16
    half = depth // SIDE
    rows = 2 * half
    number = 1 if later else 4
    stats = [unpack_rows(part[depth:, :], number) for part in (mine, from_left, from_right)]
    lines = stats[0] + stats[1] + stats[2]
    lines.append(jnp.zeros((16 - len(lines), rows), F32))
    if later:
        table = refs[0][...]
        near_out, far_out, kept = refs[-3:]
    else:
        near_out, far_out, kept, table_out = refs[-4:]
        own, left, right = (line[0] for line in stats)
        lane = lax.broadcasted_iota(jnp.int32, own.shape, 1)
        other = jnp.where(lane < half, left, right)
        peak = jnp.maximum(own, other)
        table = columns_of([jnp.exp(own - peak), jnp.exp(other - peak)])
        table_out[...] = table
    kept[...] = jnp.concatenate(lines, axis=0)
    near_out[SIDE * rows : SIDE * rows + 16, :] = from_left[depth : depth + 16, :]
    for z in range(SIDE):
        low, high = slice(z * rows, z * rows + half), slice(z * rows + half, (z + 1) * rows)
        part = slice(z * half, (z + 1) * half)
        value = table[:half, 0:1] * near[low, :].astype(F32) + table[:half, 1:2] * from_left[part, :].astype(F32)
        near_out[low, :] = value.astype(BF16)
        near_out[high, :] = near[high, :]
        value = table[half:, 0:1] * far[high, :].astype(F32) + table[half:, 1:2] * from_right[part, :].astype(F32)
        far_out[high, :] = value.astype(BF16)
        far_out[low, :] = far[low, :]


def relayed(near, far, from_left, from_right, mine, tables, behind=()):
    depth, width = near.shape
    rows = depth // SIDE
    outs = [
        jax.ShapeDtypeStruct((depth + 16, width), BF16),
        jax.ShapeDtypeStruct((depth, width), BF16),
        jax.ShapeDtypeStruct((16, rows), F32),
    ]
    if not tables:
        outs.append(jax.ShapeDtypeStruct((rows, 128), F32))
    return pl.pallas_call(
        functools.partial(relay_kernel, bool(tables)),
        out_shape=outs,
        in_specs=[VMEM] * (5 + len(tables)) + [ANY] * len(behind),
        out_specs=[VMEM] * len(outs),
        compiler_params=params(),
        cost_estimate=cost(depth * width, depth * width),
        name="relay_targets",
    )(near, far, from_left, from_right, mine, *tables, *behind)


def merge_kernel(later, place, given, *refs):
    parts = refs[:3]
    width = parts[0].shape[1]
    rows = parts[0].shape[0] // SIDE
    sent = parts[1][SIDE * rows :, :]
    if later:
        table, factors, outs = refs[3][...], refs[4], refs[-SIDE:]
        lines = [given[i : i + 1] for i in range(3)] + unpack_rows(sent, 1)
        packed = pack_rows([sum(line * factors[i : i + 1] for i, line in enumerate(lines))])
    else:
        outs = refs[-2 - SIDE : -2]
        lines = [[given[4 * i + j : 4 * i + j + 1] for j in range(4)] for i in range(3)]
        lines.append(unpack_rows(sent, 4))
        stats, factors = joined(lines)
        packed = pack_rows(stats)
        own, left, right, across = (line[0] for line in lines)
        lane = lax.broadcasted_iota(jnp.int32, own.shape, 1)
        low = lane < rows // 2
        left = jnp.where(low, jnp.maximum(left, across), left)
        right = jnp.where(low, right, jnp.maximum(right, across))
        table = columns_of([jnp.exp(base - stats[0]) for base in (own, left, right)])
        refs[-2][...] = table
        refs[-1][...] = jnp.concatenate(factors + [jnp.zeros((4, rows), F32)], axis=0)
    for step in range(SIDE):
        at = pl.ds(pl.multiple_of(lax.rem(place[1] + step, SIDE) * rows, rows), rows)
        value = table[:, 0:1] * parts[0][at, :].astype(F32)
        for d in range(1, 3):
            value += table[:, d : d + 1] * parts[d][at, :].astype(F32)
        outs[step][0:rows, :] = value.astype(BF16)
        outs[step][rows : rows + 16, :] = packed


def merged(place, given, parts, tables, behind=()):
    width = parts[0].shape[1]
    rows = parts[0].shape[0] // SIDE
    outs = [jax.ShapeDtypeStruct((rows + 16, width), BF16)] * SIDE
    if not tables:
        outs += [jax.ShapeDtypeStruct((rows, 128), F32), jax.ShapeDtypeStruct((8, rows), F32)]
    return pl.pallas_call(
        functools.partial(merge_kernel, bool(tables)),
        out_shape=outs,
        in_specs=[SMEM] + [VMEM] * (4 + len(tables)) + [ANY] * len(behind),
        out_specs=[VMEM] * len(outs),
        compiler_params=params(),
        cost_estimate=cost(rows * width, rows * width),
        name="merge_targets",
    )(place, given, *parts, *tables, *behind)


def gradient_kernel(place, logits, *refs):
    chunks, grad = (refs[:SIDE], refs[SIDE : 2 * SIDE]), refs[2 * SIDE]
    rows, width = logits.shape[0], refs[0].shape[1]
    stats, factors = joined([unpack_rows(part[rows:, :], 4) for part in chunks[0]])
    _, mass, peak, smass = stats
    total = sum(
        unpack_rows(part[rows:, :], 1)[0] * factor for part, factor in zip(chunks[1], factors)
    )
    total = total / mass
    floored = jnp.maximum(total, 1.0)
    scales = [factor / mass / floored for factor in factors]
    table = columns_of(scales + [total / floored / smass, peak, peak + jnp.log(smass)])
    share, peak, norm = (table[:, c : c + 1] for c in range(4, 7))
    terms = jnp.zeros((rows, width), F32)
    for step in range(SIDE):
        block = lax.rem(place[1] + SIDE - step, SIDE)
        for chunk, parts in enumerate(chunks):
            at = pl.ds(pl.multiple_of(block * 512 + chunk * width, width), width)
            scores = logits[:, at]
            target = parts[step][0:rows, :].astype(F32) * table[:, step : step + 1]
            positive = target > 0
            entropy = jnp.where(positive, target * jnp.log(jnp.where(positive, target, 1.0)), 0.0)
            terms += entropy - target * (scores - norm)
            value = share * jnp.exp(scores - peak) - target
            grad[at, :] = value.T.astype(BF16)
    grad[SIDE * 512 :, :] = pack_rows([jnp.sum(terms.T, axis=0, keepdims=True)])


def gradients(place, logits, parts):
    rows, cols = logits.shape
    return pl.pallas_call(
        gradient_kernel,
        out_shape=jax.ShapeDtypeStruct((cols + 16, rows), BF16),
        in_specs=[SMEM] + [VMEM] * (1 + 2 * SIDE),
        out_specs=VMEM,
        compiler_params=params(),
        cost_estimate=cost(60 * rows * cols, 8 * rows * cols, 2 * rows * cols),
        name="logit_grad",
    )(place, logits, *parts)


def stage_kernel(place, unembed, *refs):
    stage, sems = refs[-2:]
    first = place[3] == 0
    copies = []
    for major in range(SIDE):
        for minor in range(SIDE):
            index = major * SIDE + minor
            owner = jnp.where(first, index, minor * SIDE + major)
            start = pl.multiple_of(owner * 256 + place[3] * 128, 128)
            copies.append(
                pltpu.make_async_copy(
                    unembed.at[pl.ds(start, 128), :],
                    stage.at[pl.ds(index * 128, 128), :],
                    sems.at[index],
                )
            )
    for copy in copies:
        copy.start()
    for copy in copies:
        copy.wait()


def staged(place, unembed, behind):
    depth, cols = unembed.shape
    return pl.pallas_call(
        stage_kernel,
        out_shape=jax.ShapeDtypeStruct((depth // 2, cols), BF16),
        in_specs=[SMEM, pl.BlockSpec(memory_space=pltpu.HBM)] + [ANY] * len(behind),
        out_specs=VMEM,
        scratch_shapes=[pltpu.SemaphoreType.DMA((SIDE * SIDE,))],
        compiler_params=params(42),
        cost_estimate=cost(0, depth * cols),
        name="stage_unembed",
    )(place, unembed, *behind)


def own_kernel(stage, mine, out):
    depth = stage.shape[1]
    for step in range(SIDE):
        rows = slice(step * 512, step * 512 + 512)
        result = jnp.dot(stage[rows, :], mine[0:depth, :], preferred_element_type=F32)
        out[rows, :] = result.astype(BF16)


def own_hidden(stage, mine):
    depth, rows = stage.shape[0], mine.shape[1]
    return pl.pallas_call(
        own_kernel,
        out_shape=jax.ShapeDtypeStruct((depth, rows), BF16),
        in_specs=[VMEM, VMEM],
        out_specs=VMEM,
        compiler_params=params(),
        cost_estimate=cost(2 * stage.size * rows, 2 * stage.size),
        name="own_hidden",
    )(stage, mine)


def other_kernel(steps, place, stage, mine, other, own, *refs):
    outs = refs[-len(steps) :]
    depth = stage.shape[1]
    rows = mine.shape[1]
    lanes = pl.ds(pl.multiple_of(place[3] * rows, rows), rows)
    other_lanes = pl.ds(pl.multiple_of((1 - place[3]) * rows, rows), rows)
    for out, step in zip(outs, steps):
        at = pl.ds(pl.multiple_of(lax.rem(place[4] + step, SIDE) * 512, 512), 512)
        result = jnp.dot(stage[at, :], other[0:depth, :], preferred_element_type=F32)
        out[0:512, other_lanes] = result.astype(BF16)
        out[0:512, lanes] = own[at, :]
        out[512:528, lanes] = mine[depth : depth + 16, :]
        out[512:528, other_lanes] = other[depth : depth + 16, :]


def other_hidden(steps, place, stage, mine, other, own, behind=()):
    rows = mine.shape[1]
    return pl.pallas_call(
        functools.partial(other_kernel, steps),
        out_shape=[jax.ShapeDtypeStruct((528, 2 * rows), BF16)] * len(steps),
        in_specs=[SMEM] + [VMEM] * 4 + [ANY] * len(behind),
        out_specs=[VMEM] * len(steps),
        compiler_params=params(),
        cost_estimate=cost(len(steps) * stage.size * rows // 2, 2 * stage.size),
        name="other_hidden",
    )(place, stage, mine, other, own, *behind)


def packed_loss(index, parts, at, ordered):
    for step in range(SIDE):
        ordered[lax.rem(index + SIDE - step, SIDE)] = unpack_rows(parts[step][at : at + 16, :], 1)[0]
    return ((ordered[0] + ordered[1]) + ordered[2]) + ordered[3]


def middle_kernel(place, *refs):
    parts, outs, ordered = refs[:SIDE], refs[SIDE : 2 * SIDE], refs[2 * SIDE]
    packed = pack_rows([packed_loss(place[4], parts, 512, ordered)])
    for step in range(SIDE):
        at = pl.ds(pl.multiple_of(lax.rem(place[5] + step, SIDE) * 128, 128), 128)
        value = parts[0][at, :].astype(F32)
        for part in parts[1:]:
            value += part[at, :].astype(F32)
        outs[step][0:128, :] = value.astype(BF16)
        outs[step][128:144, :] = packed


def middle(place, parts):
    rows = parts[0].shape[1]
    return pl.pallas_call(
        middle_kernel,
        out_shape=[jax.ShapeDtypeStruct((144, rows), BF16)] * SIDE,
        in_specs=[SMEM] + [VMEM] * SIDE,
        out_specs=[VMEM] * SIDE,
        scratch_shapes=[pltpu.VMEM((SIDE, 1, rows), F32)],
        compiler_params=params(),
        cost_estimate=cost(4 * 512 * rows, 10 * 512 * rows),
        name="merge_grads",
    )(place, *parts)


def total_kernel(place, *refs):
    parts = refs[:SIDE]
    keep, give, loss, ordered = refs[SIDE:]
    rows = keep.shape[1]
    mine = pl.ds(pl.multiple_of(place[3] * rows, rows), rows)
    other = pl.ds(pl.multiple_of((1 - place[3]) * rows, rows), rows)
    ordered[4] = packed_loss(place[5], parts, 128, ordered)
    loss[...] = jnp.broadcast_to(ordered[4, :, mine], loss.shape)
    for lanes, out in ((other, give), (mine, keep)):
        value = parts[0][0:128, lanes].astype(F32)
        for part in parts[1:]:
            value += part[0:128, lanes].astype(F32)
        out[...] = value.astype(BF16)


def totals(place, parts):
    rows = parts[0].shape[1] // 2
    half = jax.ShapeDtypeStruct((128, rows), BF16)
    return pl.pallas_call(
        total_kernel,
        out_shape=[half, half, jax.ShapeDtypeStruct((8, rows), F32)],
        in_specs=[SMEM] + [VMEM] * SIDE,
        out_specs=[VMEM] * 3,
        scratch_shapes=[pltpu.VMEM((SIDE + 1, 1, 2 * rows), F32)],
        compiler_params=params(),
        cost_estimate=cost(8 * 128 * rows, 20 * 128 * rows),
        name="sum_grads",
    )(place, *parts)


def turn_kernel(place, keep, given, grad):
    mine = pl.ds(pl.multiple_of(place[3] * 128, 128), 128)
    other = pl.ds(pl.multiple_of((1 - place[3]) * 128, 128), 128)
    grad[:, mine] = keep[...].astype(F32).T.astype(BF16)
    grad[:, other] = given[...].astype(F32).T.astype(BF16)


def turned(place, keep, given):
    rows = keep.shape[1]
    return pl.pallas_call(
        turn_kernel,
        out_shape=jax.ShapeDtypeStruct((rows, 256), BF16),
        in_specs=[SMEM, VMEM, VMEM],
        out_specs=VMEM,
        compiler_params=params(),
        cost_estimate=cost(0, 4 * 256 * rows),
        name="turn_grads",
    )(place, keep, given)


def spread(parts, axis):
    return [parts[0]] + [send(parts[step], axis, step) for step in (1, 2, 3)]


def crossed(parts, first):
    def target(y, z, core, step):
        if (core == 0) == first:
            y = (y + step) % SIDE
        else:
            z = (z + step) % SIDE
        return (y * SIDE + z) * 2 + core

    places = [(y, z, core) for y in range(SIDE) for z in range(SIDE) for core in range(2)]
    received = [parts[0]]
    for step in (1, 2, 3):
        pairs = [(i, target(*at, step)) for i, at in enumerate(places)]
        received.append(lax.ppermute(parts[step], ("vy", "vz", "tc"), pairs))
    return received


def shards(teacher_logits, student_hidden, student_unembed, tile_weights, tile_pairs, tile_count):
    y, z, x, core = (lax.axis_index(name) for name in ("vy", "vz", "tx", "tc"))
    crossing = [jnp.where(core == 0, y, z), jnp.where(core == 0, z, y)]
    place = jnp.stack([y, z, x, core] + crossing).astype(jnp.int32)
    rows = teacher_logits.shape[0]
    teacher = teacher_logits.astype(F32)
    peak = jnp.max(teacher, axis=1)
    shifted = jnp.exp(teacher - peak[:, None])
    mass = jnp.sum(shifted, axis=1)
    probs = shifted.astype(BF16)

    logits = jnp.dot(student_hidden, student_unembed, preferred_element_type=F32)
    speak = jnp.max(logits, axis=1)
    smass = jnp.sum(jnp.exp(logits - speak[:, None]), axis=1)

    before = jnp.stack([peak, mass, speak, smass] * 2)

    piece = sliced(tile_weights, 0)
    mine = [piece, *gated(spread([piece] * SIDE, "tx")[1:], [mass, smass])]
    other = [swap(piece) for piece in mine]

    piece = sliced(tile_weights, 1, [mine[1]])
    right, left = send(piece, "tx", 1), send(piece, "tx", 3)
    *parts, total = products(
        place, tile_pairs, tile_count, probs, before, mine, other, False, [piece]
    )
    top, low = halves(right, left, [parts[0]])
    own, near, far, to_right, to_left = parts
    left_part, right_part = send(to_right, "vy", 1), send(to_left, "vy", 3)
    near, far, given, table = relayed(near, far, left_part, right_part, to_right, [], [right, left])
    near, far = send(near, "vy", 1), send(far, "vy", 3)
    top, low = gated([send(top, "tx", 1), send(low, "tx", 3)], [near, far])
    mine = [piece, right, left, top, low]
    later = products(
        place, tile_pairs, tile_count, probs, total, mine, [swap(piece) for piece in mine], True
    )

    *first, scales, factors = merged(place, given, [own, near, far], [], [later[0]])
    own, near, far, to_right, to_left = later
    left_part, right_part = send(to_right, "vy", 1), send(to_left, "vy", 3)
    stage = staged(place, student_unembed, [own])
    near, far, given = relayed(near, far, left_part, right_part, to_right, [table], [stage])
    parts = [own, send(near, "vy", 1), send(far, "vy", 3)]
    first = spread(first, "vz")
    second = merged(place, given, parts, [scales, factors])
    mine = gradients(place, logits, first + spread(second, "vz"))

    own = own_hidden(stage, mine)
    other = swap(mine)
    parts = other_hidden(range(SIDE), place, stage, mine, other, own)
    parts = middle(place, crossed(parts, True))
    keep, give, loss = totals(place, crossed(parts, False))
    return turned(place, keep, swap(give)), loss[0]


def solution(mesh):
    grid = Mesh(mesh.devices.reshape(SIDE, SIDE, SIDE, 2), ("vy", "vz", "tx", "tc"))
    vocab, tokens = ("vy", "vz"), ("tx", "tc")
    return jax.shard_map(
        shards,
        mesh=grid,
        in_specs=(
            P(tokens, vocab),
            P(tokens, None),
            P(None, vocab),
            P(vocab, tokens, None),
            P(vocab, None),
            P(vocab),
        ),
        out_specs=(P(tokens, vocab), P(tokens)),
        check_vma=False,
    )
```

```python
import functools

import jax
import jax.numpy as jnp
from jax import lax
from jax.experimental import pallas as pl
from jax.experimental.pallas import tpu as pltpu
from jax.sharding import Mesh
from jax.sharding import PartitionSpec as P

F32 = jnp.float32
BF16 = jnp.bfloat16
SIDE = 4
VMEM = pl.BlockSpec(memory_space=pltpu.VMEM)
SMEM = pl.BlockSpec(memory_space=pltpu.SMEM)
ANY = pl.BlockSpec(memory_space=pl.ANY)
MIB = 1024 * 1024


def params(mib=16):
    return pltpu.CompilerParams(vmem_limit_bytes=mib * MIB)


def cost(flops, moved, transcendentals=0):
    return pl.CostEstimate(flops=flops, bytes_accessed=moved, transcendentals=transcendentals)


def send(value, axis, step):
    return lax.ppermute(value, axis, [(i, (i + step) % SIDE) for i in range(SIDE)])


def swap(value):
    return lax.ppermute(value, "tc", [(0, 1), (1, 0)])


def thirds(value):
    high = value.astype(BF16).astype(F32)
    rest = value - high
    middle = rest.astype(BF16).astype(F32)
    return high, middle, rest - middle


def slice_kernel(weights, *refs):
    piece = refs[-1]
    piece[...] = weights[...].reshape(piece.shape)


def sliced(weights, index, behind=()):
    slots, shard_rows, cols = weights.shape
    width = cols // 2
    return pl.pallas_call(
        slice_kernel,
        grid=(1,),
        out_shape=jax.ShapeDtypeStruct((slots * shard_rows, width), BF16),
        in_specs=[pl.BlockSpec((slots, shard_rows, width), lambda i: (0, 0, index))]
        + [ANY] * len(behind),
        out_specs=pl.BlockSpec((slots * shard_rows, width), lambda i: (0, 0)),
        compiler_params=params(),
        cost_estimate=cost(0, 2 * weights.size),
        name="slice_weights",
    )(weights, *behind)


def gate_kernel(*refs):
    pass


def gated(parts, behind):
    return pl.pallas_call(
        gate_kernel,
        out_shape=[jax.ShapeDtypeStruct(part.shape, part.dtype) for part in parts],
        in_specs=[ANY] * (len(parts) + len(behind)),
        out_specs=[ANY] * len(parts),
        input_output_aliases={i: i for i in range(len(parts))},
        compiler_params=params(),
        cost_estimate=cost(0, 0),
        name="gate",
    )(*parts, *behind)


def hold_kernel(source, out):
    out[...] = source[...]


def held(value):
    return pl.pallas_call(
        hold_kernel,
        out_shape=jax.ShapeDtypeStruct(value.shape, value.dtype),
        in_specs=[VMEM],
        out_specs=VMEM,
        compiler_params=params(),
        cost_estimate=cost(0, 4 * value.size),
        name="hold_probs",
    )(value)


def halves_kernel(right, left, *refs):
    top, low = refs[-2:]
    top[...] = right[...]
    low[...] = left[...]


def halves(right, left, behind):
    depth, width = right.shape
    shape = (depth // 2, width)
    return pl.pallas_call(
        halves_kernel,
        grid=(1,),
        out_shape=[jax.ShapeDtypeStruct(shape, BF16)] * 2,
        in_specs=[
            pl.BlockSpec(shape, lambda i: (0, 0)),
            pl.BlockSpec(shape, lambda i: (1, 0)),
        ]
        + [ANY] * len(behind),
        out_specs=[pl.BlockSpec(shape, lambda i: (0, 0))] * 2,
        compiler_params=params(),
        cost_estimate=cost(0, 4 * depth * width),
        name="take_halves",
    )(right, left, *behind)


def product_kernel(number, later, place, pairs, count, probs, before, *rest):
    pieces, (weights, total) = rest[:number], rest[-2:]
    outs = rest[-7:-2] if later else rest[-9:-4]
    block = 512
    rows, width = probs.shape[0], total.shape[2]
    half = rows // 2
    vocab_y = place[0]
    first_block = (vocab_y * SIDE + place[1]) * (probs.shape[1] // block)
    total[...] = jnp.zeros_like(total)
    starts = ((0, 0), (1, 0), (3, 0), (2, 0), (2, 512)) if number == 10 else ((0, 0), (1, 0), (2, 0), (3, 0))
    for core, parts in ((place[3], pieces[: number // 2]), (1 - place[3], pieces[number // 2 :])):
        for part, (step, start) in zip(parts, starts):
            x = lax.rem(place[2] + SIDE - step, SIDE)
            weights[x * 2 + core, start : start + part.shape[0]] = part[...]

    def tiles(group, carry):
        for member in range(4):
            slot = group * 4 + member
            teacher = pairs[slot, 0] - first_block
            owner = pairs[slot, 1] // SIDE
            columns = probs[:, pl.ds(pl.multiple_of(teacher * block, block), block)]
            matrix = weights[:, pl.ds(pl.multiple_of(slot * 64, 64), 64), :].reshape(block, width)
            product = jnp.dot(columns, matrix, preferred_element_type=F32)
            if member:
                product = jnp.where(slot < count[0], product, 0.0)
            total[owner] += product
        return carry

    lax.fori_loop(0, (count[0] + 3) // 4, tiles, 0)
    summed = jnp.zeros((rows, width), F32)
    for step in range(SIDE):
        start = lax.rem(vocab_y + step, SIDE) * SIDE
        for z in range(SIDE):
            value = total[start + z]
            summed += value
            value = value.astype(BF16)
            if step == 2:
                outs[3][z * half : z * half + half, :] = value[:half]
                outs[4][z * half : z * half + half, :] = value[half:]
            else:
                outs[step - step // 3][z * rows : z * rows + rows, :] = value
    line = jnp.sum(summed.T, axis=0, keepdims=True)
    if later:
        packed = pack_rows([line + before[0:1]])
    else:
        rest[-4][...] = jnp.broadcast_to(line, rest[-4].shape)
        rest[-3][...] = probs[...]
        packed = pack_rows([before[i : i + 1] for i in range(4)])
    for out in outs[3:]:
        out[SIDE * half : SIDE * half + 16, :] = packed


def products(place, pairs, count, probs, before, mine, other, later, behind=()):
    rows = probs.shape[0]
    depth, width = mine[0].shape
    pieces = [*mine, *other]
    outs = [jax.ShapeDtypeStruct((SIDE * rows, width), BF16)] * 3
    outs += [jax.ShapeDtypeStruct((SIDE * rows // 2 + 16, width), BF16)] * 2
    if not later:
        outs += [jax.ShapeDtypeStruct((8, rows), F32), jax.ShapeDtypeStruct(probs.shape, BF16)]
    return pl.pallas_call(
        functools.partial(product_kernel, len(pieces), later),
        out_shape=outs,
        in_specs=[SMEM, SMEM, SMEM] + [VMEM] * (2 + len(pieces)) + [ANY] * len(behind),
        out_specs=[VMEM] * len(outs),
        scratch_shapes=[
            pltpu.VMEM((2 * SIDE, depth, width), BF16),
            pltpu.VMEM((SIDE * SIDE, rows, width), F32),
        ],
        compiler_params=params(14),
        cost_estimate=cost(
            16 * 2 * rows * 512 * width, 2 * probs.size + 16 * depth * width + 32 * rows * width
        ),
        name="tile_products",
    )(place, pairs, count, probs, before, *pieces, *behind)


def pack_rows(lines):
    rows = [part for line in lines for part in thirds(line)]
    rows.append(jnp.zeros((16 - len(rows), rows[0].shape[1]), F32))
    return jnp.concatenate(rows, axis=0).astype(BF16)


def unpack_rows(packed, number):
    packed = packed.astype(F32)
    return [
        packed[3 * i : 3 * i + 1] + packed[3 * i + 1 : 3 * i + 2] + packed[3 * i + 2 : 3 * i + 3]
        for i in range(number)
    ]


def joined(stats):
    peak = functools.reduce(jnp.maximum, [line[0] for line in stats])
    speak = functools.reduce(jnp.maximum, [line[2] for line in stats])
    factors = [jnp.exp(line[0] - peak) for line in stats]
    mass = sum(line[1] * factor for line, factor in zip(stats, factors))
    smass = sum(line[3] * jnp.exp(line[2] - speak) for line in stats)
    return (peak, mass, speak, smass), factors


def columns_of(lines):
    lines = list(lines) + [jnp.zeros((128 - len(lines), lines[0].shape[1]), F32)]
    return jnp.concatenate(lines, axis=0).T


def relay_kernel(later, near, far, from_left, from_right, mine, *refs):
    depth = from_left.shape[0] - 16
    half = depth // SIDE
    rows = 2 * half
    number = 1 if later else 4
    stats = [unpack_rows(part[depth:, :], number) for part in (mine, from_left, from_right)]
    lines = stats[0] + stats[1] + stats[2]
    lines.append(jnp.zeros((16 - len(lines), rows), F32))
    if later:
        table = refs[0][...]
        near_out, far_out, kept = refs[-3:]
    else:
        near_out, far_out, kept, table_out = refs[-4:]
        own, left, right = (line[0] for line in stats)
        lane = lax.broadcasted_iota(jnp.int32, own.shape, 1)
        other = jnp.where(lane < half, left, right)
        peak = jnp.maximum(own, other)
        table = columns_of([jnp.exp(own - peak), jnp.exp(other - peak)])
        table_out[...] = table
    kept[...] = jnp.concatenate(lines, axis=0)
    near_out[SIDE * rows : SIDE * rows + 16, :] = from_left[depth : depth + 16, :]
    for z in range(SIDE):
        low, high = slice(z * rows, z * rows + half), slice(z * rows + half, (z + 1) * rows)
        part = slice(z * half, (z + 1) * half)
        value = table[:half, 0:1] * near[low, :].astype(F32) + table[:half, 1:2] * from_left[part, :].astype(F32)
        near_out[low, :] = value.astype(BF16)
        near_out[high, :] = near[high, :]
        value = table[half:, 0:1] * far[high, :].astype(F32) + table[half:, 1:2] * from_right[part, :].astype(F32)
        far_out[high, :] = value.astype(BF16)
        far_out[low, :] = far[low, :]


def relayed(near, far, from_left, from_right, mine, tables, behind=()):
    depth, width = near.shape
    rows = depth // SIDE
    outs = [
        jax.ShapeDtypeStruct((depth + 16, width), BF16),
        jax.ShapeDtypeStruct((depth, width), BF16),
        jax.ShapeDtypeStruct((16, rows), F32),
    ]
    if not tables:
        outs.append(jax.ShapeDtypeStruct((rows, 128), F32))
    return pl.pallas_call(
        functools.partial(relay_kernel, bool(tables)),
        out_shape=outs,
        in_specs=[VMEM] * (5 + len(tables)) + [ANY] * len(behind),
        out_specs=[VMEM] * len(outs),
        compiler_params=params(),
        cost_estimate=cost(depth * width, depth * width),
        name="relay_targets",
    )(near, far, from_left, from_right, mine, *tables, *behind)


def merge_kernel(later, place, given, *refs):
    parts = refs[:3]
    width = parts[0].shape[1]
    rows = parts[0].shape[0] // SIDE
    sent = parts[1][SIDE * rows :, :]
    if later:
        table, factors, outs = refs[3][...], refs[4], refs[-SIDE:]
        lines = [given[i : i + 1] for i in range(3)] + unpack_rows(sent, 1)
        packed = pack_rows([sum(line * factors[i : i + 1] for i, line in enumerate(lines))])
    else:
        outs = refs[-2 - SIDE : -2]
        lines = [[given[4 * i + j : 4 * i + j + 1] for j in range(4)] for i in range(3)]
        lines.append(unpack_rows(sent, 4))
        stats, factors = joined(lines)
        packed = pack_rows(stats)
        own, left, right, across = (line[0] for line in lines)
        lane = lax.broadcasted_iota(jnp.int32, own.shape, 1)
        low = lane < rows // 2
        left = jnp.where(low, jnp.maximum(left, across), left)
        right = jnp.where(low, right, jnp.maximum(right, across))
        table = columns_of([jnp.exp(base - stats[0]) for base in (own, left, right)])
        refs[-2][...] = table
        refs[-1][...] = jnp.concatenate(factors + [jnp.zeros((4, rows), F32)], axis=0)
    for step in range(SIDE):
        at = pl.ds(pl.multiple_of(lax.rem(place[1] + step, SIDE) * rows, rows), rows)
        value = table[:, 0:1] * parts[0][at, :].astype(F32)
        for d in range(1, 3):
            value += table[:, d : d + 1] * parts[d][at, :].astype(F32)
        outs[step][0:rows, :] = value.astype(BF16)
        outs[step][rows : rows + 16, :] = packed


def merged(place, given, parts, tables, behind=()):
    width = parts[0].shape[1]
    rows = parts[0].shape[0] // SIDE
    outs = [jax.ShapeDtypeStruct((rows + 16, width), BF16)] * SIDE
    if not tables:
        outs += [jax.ShapeDtypeStruct((rows, 128), F32), jax.ShapeDtypeStruct((8, rows), F32)]
    return pl.pallas_call(
        functools.partial(merge_kernel, bool(tables)),
        out_shape=outs,
        in_specs=[SMEM] + [VMEM] * (4 + len(tables)) + [ANY] * len(behind),
        out_specs=[VMEM] * len(outs),
        compiler_params=params(),
        cost_estimate=cost(rows * width, rows * width),
        name="merge_targets",
    )(place, given, *parts, *tables, *behind)


def gradient_kernel(place, logits, *refs):
    chunks, grad = (refs[:SIDE], refs[SIDE : 2 * SIDE]), refs[2 * SIDE]
    rows, width = logits.shape[0], refs[0].shape[1]
    stats, factors = joined([unpack_rows(part[rows:, :], 4) for part in chunks[0]])
    _, mass, peak, smass = stats
    total = sum(
        unpack_rows(part[rows:, :], 1)[0] * factor for part, factor in zip(chunks[1], factors)
    )
    total = total / mass
    floored = jnp.maximum(total, 1.0)
    scales = [factor / mass / floored for factor in factors]
    table = columns_of(scales + [total / floored / smass, peak, peak + jnp.log(smass)])
    share, peak, norm = (table[:, c : c + 1] for c in range(4, 7))
    terms = jnp.zeros((rows, width), F32)
    for step in range(SIDE):
        block = lax.rem(place[1] + SIDE - step, SIDE)
        for chunk, parts in enumerate(chunks):
            at = pl.ds(pl.multiple_of(block * 512 + chunk * width, width), width)
            scores = logits[:, at]
            target = parts[step][0:rows, :].astype(F32) * table[:, step : step + 1]
            positive = target > 0
            entropy = jnp.where(positive, target * jnp.log(jnp.where(positive, target, 1.0)), 0.0)
            terms += entropy - target * (scores - norm)
            value = share * jnp.exp(scores - peak) - target
            grad[at, :] = value.T.astype(BF16)
    grad[SIDE * 512 :, :] = pack_rows([jnp.sum(terms.T, axis=0, keepdims=True)])


def gradients(place, logits, parts):
    rows, cols = logits.shape
    return pl.pallas_call(
        gradient_kernel,
        out_shape=jax.ShapeDtypeStruct((cols + 16, rows), BF16),
        in_specs=[SMEM] + [VMEM] * (1 + 2 * SIDE),
        out_specs=VMEM,
        compiler_params=params(),
        cost_estimate=cost(60 * rows * cols, 8 * rows * cols, 2 * rows * cols),
        name="logit_grad",
    )(place, logits, *parts)


def stage_kernel(place, unembed, *refs):
    stage, sems = refs[-2:]
    first = place[3] == 0
    copies = []
    for major in range(SIDE):
        for minor in range(SIDE):
            index = major * SIDE + minor
            owner = jnp.where(first, index, minor * SIDE + major)
            start = pl.multiple_of(owner * 256 + place[3] * 128, 128)
            copies.append(
                pltpu.make_async_copy(
                    unembed.at[pl.ds(start, 128), :],
                    stage.at[pl.ds(index * 128, 128), :],
                    sems.at[index],
                )
            )
    for copy in copies:
        copy.start()
    for copy in copies:
        copy.wait()


def staged(place, unembed, behind):
    depth, cols = unembed.shape
    return pl.pallas_call(
        stage_kernel,
        out_shape=jax.ShapeDtypeStruct((depth // 2, cols), BF16),
        in_specs=[SMEM, pl.BlockSpec(memory_space=pltpu.HBM)] + [ANY] * len(behind),
        out_specs=VMEM,
        scratch_shapes=[pltpu.SemaphoreType.DMA((SIDE * SIDE,))],
        compiler_params=params(42),
        cost_estimate=cost(0, depth * cols),
        name="stage_unembed",
    )(place, unembed, *behind)


def own_kernel(stage, mine, out):
    depth = stage.shape[1]
    for step in range(SIDE):
        rows = slice(step * 512, step * 512 + 512)
        result = jnp.dot(stage[rows, :], mine[0:depth, :], preferred_element_type=F32)
        out[rows, :] = result.astype(BF16)


def own_hidden(stage, mine):
    depth, rows = stage.shape[0], mine.shape[1]
    return pl.pallas_call(
        own_kernel,
        out_shape=jax.ShapeDtypeStruct((depth, rows), BF16),
        in_specs=[VMEM, VMEM],
        out_specs=VMEM,
        compiler_params=params(),
        cost_estimate=cost(2 * stage.size * rows, 2 * stage.size),
        name="own_hidden",
    )(stage, mine)


def other_kernel(steps, place, stage, mine, other, own, *refs):
    outs = refs[-len(steps) :]
    depth = stage.shape[1]
    rows = mine.shape[1]
    lanes = pl.ds(pl.multiple_of(place[3] * rows, rows), rows)
    other_lanes = pl.ds(pl.multiple_of((1 - place[3]) * rows, rows), rows)
    for out, step in zip(outs, steps):
        at = pl.ds(pl.multiple_of(lax.rem(place[4] + step, SIDE) * 512, 512), 512)
        result = jnp.dot(stage[at, :], other[0:depth, :], preferred_element_type=F32)
        out[0:512, other_lanes] = result.astype(BF16)
        out[0:512, lanes] = own[at, :]
        out[512:528, lanes] = mine[depth : depth + 16, :]
        out[512:528, other_lanes] = other[depth : depth + 16, :]


def other_hidden(steps, place, stage, mine, other, own, behind=()):
    rows = mine.shape[1]
    return pl.pallas_call(
        functools.partial(other_kernel, steps),
        out_shape=[jax.ShapeDtypeStruct((528, 2 * rows), BF16)] * len(steps),
        in_specs=[SMEM] + [VMEM] * 4 + [ANY] * len(behind),
        out_specs=[VMEM] * len(steps),
        compiler_params=params(),
        cost_estimate=cost(len(steps) * stage.size * rows // 2, 2 * stage.size),
        name="other_hidden",
    )(place, stage, mine, other, own, *behind)


def packed_loss(index, parts, at, ordered):
    for step in range(SIDE):
        ordered[lax.rem(index + SIDE - step, SIDE)] = unpack_rows(parts[step][at : at + 16, :], 1)[0]
    return ((ordered[0] + ordered[1]) + ordered[2]) + ordered[3]


def middle_kernel(place, *refs):
    parts, outs, ordered = refs[:SIDE], refs[SIDE : 2 * SIDE], refs[2 * SIDE]
    packed = pack_rows([packed_loss(place[4], parts, 512, ordered)])
    for step in range(SIDE):
        at = pl.ds(pl.multiple_of(lax.rem(place[5] + step, SIDE) * 128, 128), 128)
        value = parts[0][at, :].astype(F32)
        for part in parts[1:]:
            value += part[at, :].astype(F32)
        outs[step][0:128, :] = value.astype(BF16)
        outs[step][128:144, :] = packed


def middle(place, parts):
    rows = parts[0].shape[1]
    return pl.pallas_call(
        middle_kernel,
        out_shape=[jax.ShapeDtypeStruct((144, rows), BF16)] * SIDE,
        in_specs=[SMEM] + [VMEM] * SIDE,
        out_specs=[VMEM] * SIDE,
        scratch_shapes=[pltpu.VMEM((SIDE, 1, rows), F32)],
        compiler_params=params(),
        cost_estimate=cost(4 * 512 * rows, 10 * 512 * rows),
        name="merge_grads",
    )(place, *parts)


def total_kernel(place, *refs):
    parts = refs[:SIDE]
    keep, give, loss, ordered = refs[SIDE:]
    rows = keep.shape[1]
    mine = pl.ds(pl.multiple_of(place[3] * rows, rows), rows)
    other = pl.ds(pl.multiple_of((1 - place[3]) * rows, rows), rows)
    ordered[4] = packed_loss(place[5], parts, 128, ordered)
    loss[...] = jnp.broadcast_to(ordered[4, :, mine], loss.shape)
    for lanes, out in ((other, give), (mine, keep)):
        value = parts[0][0:128, lanes].astype(F32)
        for part in parts[1:]:
            value += part[0:128, lanes].astype(F32)
        out[...] = value.astype(BF16)


def totals(place, parts):
    rows = parts[0].shape[1] // 2
    half = jax.ShapeDtypeStruct((128, rows), BF16)
    return pl.pallas_call(
        total_kernel,
        out_shape=[half, half, jax.ShapeDtypeStruct((8, rows), F32)],
        in_specs=[SMEM] + [VMEM] * SIDE,
        out_specs=[VMEM] * 3,
        scratch_shapes=[pltpu.VMEM((SIDE + 1, 1, 2 * rows), F32)],
        compiler_params=params(),
        cost_estimate=cost(8 * 128 * rows, 20 * 128 * rows),
        name="sum_grads",
    )(place, *parts)


def turn_kernel(place, keep, given, grad):
    mine = pl.ds(pl.multiple_of(place[3] * 128, 128), 128)
    other = pl.ds(pl.multiple_of((1 - place[3]) * 128, 128), 128)
    grad[:, mine] = keep[...].astype(F32).T.astype(BF16)
    grad[:, other] = given[...].astype(F32).T.astype(BF16)


def turned(place, keep, given):
    rows = keep.shape[1]
    return pl.pallas_call(
        turn_kernel,
        out_shape=jax.ShapeDtypeStruct((rows, 256), BF16),
        in_specs=[SMEM, VMEM, VMEM],
        out_specs=VMEM,
        compiler_params=params(),
        cost_estimate=cost(0, 4 * 256 * rows),
        name="turn_grads",
    )(place, keep, given)


def spread(parts, axis):
    return [parts[0]] + [send(parts[step], axis, step) for step in (1, 2, 3)]


def crossed(parts, first):
    def target(y, z, core, step):
        if (core == 0) == first:
            y = (y + step) % SIDE
        else:
            z = (z + step) % SIDE
        return (y * SIDE + z) * 2 + core

    places = [(y, z, core) for y in range(SIDE) for z in range(SIDE) for core in range(2)]
    received = [parts[0]]
    for step in (1, 2, 3):
        pairs = [(i, target(*at, step)) for i, at in enumerate(places)]
        received.append(lax.ppermute(parts[step], ("vy", "vz", "tc"), pairs))
    return received


def shards(teacher_logits, student_hidden, student_unembed, tile_weights, tile_pairs, tile_count):
    y, z, x, core = (lax.axis_index(name) for name in ("vy", "vz", "tx", "tc"))
    crossing = [jnp.where(core == 0, y, z), jnp.where(core == 0, z, y)]
    place = jnp.stack([y, z, x, core] + crossing).astype(jnp.int32)
    rows = teacher_logits.shape[0]
    teacher = teacher_logits.astype(F32)
    peak = jnp.max(teacher, axis=1)
    shifted = jnp.exp(teacher - peak[:, None])
    mass = jnp.sum(shifted, axis=1)
    probs = shifted.astype(BF16)

    logits = jnp.dot(student_hidden, student_unembed, preferred_element_type=F32)
    speak = jnp.max(logits, axis=1)
    smass = jnp.sum(jnp.exp(logits - speak[:, None]), axis=1)

    before = jnp.stack([peak, mass, speak, smass] * 2)

    piece = sliced(tile_weights, 0)
    probs = held(probs)
    mine = [piece, *gated(spread([piece] * SIDE, "tx")[1:], [mass, smass, probs])]
    other = [swap(piece) for piece in mine]

    piece = sliced(tile_weights, 1, [mine[1]])
    right, left = send(piece, "tx", 1), send(piece, "tx", 3)
    *parts, total, probs = products(
        place, tile_pairs, tile_count, probs, before, mine, other, False, [piece]
    )
    top, low = halves(right, left, [parts[0]])
    own, near, far, to_right, to_left = parts
    left_part, right_part = send(to_right, "vy", 1), send(to_left, "vy", 3)
    near, far, given, table = relayed(near, far, left_part, right_part, to_right, [], [right, left])
    near, far = send(near, "vy", 1), send(far, "vy", 3)
    top, low = gated([send(top, "tx", 1), send(low, "tx", 3)], [near, far])
    mine = [piece, right, left, top, low]
    later = products(
        place, tile_pairs, tile_count, probs, total, mine, [swap(piece) for piece in mine], True
    )

    *first, scales, factors = merged(place, given, [own, near, far], [], [later[0]])
    own, near, far, to_right, to_left = later
    left_part, right_part = send(to_right, "vy", 1), send(to_left, "vy", 3)
    stage = staged(place, student_unembed, [own])
    near, far, given = relayed(near, far, left_part, right_part, to_right, [table], [stage])
    parts = [own, send(near, "vy", 1), send(far, "vy", 3)]
    first = spread(first, "vz")
    second = merged(place, given, parts, [scales, factors])
    mine = gradients(place, logits, first + spread(second, "vz"))

    own = own_hidden(stage, mine)
    other = swap(mine)
    parts = other_hidden(range(SIDE), place, stage, mine, other, own)
    parts = middle(place, crossed(parts, True))
    keep, give, loss = totals(place, crossed(parts, False))
    return turned(place, keep, swap(give)), loss[0]


def solution(mesh):
    grid = Mesh(mesh.devices.reshape(SIDE, SIDE, SIDE, 2), ("vy", "vz", "tx", "tc"))
    vocab, tokens = ("vy", "vz"), ("tx", "tc")
    return jax.shard_map(
        shards,
        mesh=grid,
        in_specs=(
            P(tokens, vocab),
            P(tokens, None),
            P(None, vocab),
            P(vocab, tokens, None),
            P(vocab, None),
            P(vocab),
        ),
        out_specs=(P(tokens, vocab), P(tokens)),
        check_vma=False,
    )
```

```python
import functools

import jax
import jax.numpy as jnp
from jax import lax
from jax.experimental import pallas as pl
from jax.experimental.pallas import tpu as pltpu
from jax.sharding import Mesh
from jax.sharding import PartitionSpec as P

F32 = jnp.float32
BF16 = jnp.bfloat16
SIDE = 4
VMEM = pl.BlockSpec(memory_space=pltpu.VMEM)
SMEM = pl.BlockSpec(memory_space=pltpu.SMEM)
ANY = pl.BlockSpec(memory_space=pl.ANY)
MIB = 1024 * 1024


def params(mib=16):
    return pltpu.CompilerParams(vmem_limit_bytes=mib * MIB)


def cost(flops, moved, transcendentals=0):
    return pl.CostEstimate(flops=flops, bytes_accessed=moved, transcendentals=transcendentals)


def send(value, axis, step):
    return lax.ppermute(value, axis, [(i, (i + step) % SIDE) for i in range(SIDE)])


def swap(value):
    return lax.ppermute(value, "tc", [(0, 1), (1, 0)])


def thirds(value):
    high = value.astype(BF16).astype(F32)
    rest = value - high
    middle = rest.astype(BF16).astype(F32)
    return high, middle, rest - middle


def slice_kernel(weights, *refs):
    piece = refs[-1]
    piece[...] = weights[...].reshape(piece.shape)


def sliced(weights, index, behind=()):
    slots, shard_rows, cols = weights.shape
    width = cols // 2
    return pl.pallas_call(
        slice_kernel,
        grid=(1,),
        out_shape=jax.ShapeDtypeStruct((slots * shard_rows, width), BF16),
        in_specs=[pl.BlockSpec((slots, shard_rows, width), lambda i: (0, 0, index))]
        + [ANY] * len(behind),
        out_specs=pl.BlockSpec((slots * shard_rows, width), lambda i: (0, 0)),
        compiler_params=params(),
        cost_estimate=cost(0, 2 * weights.size),
        name="slice_weights",
    )(weights, *behind)


def gate_kernel(*refs):
    pass


def gated(parts, behind):
    return pl.pallas_call(
        gate_kernel,
        out_shape=[jax.ShapeDtypeStruct(part.shape, part.dtype) for part in parts],
        in_specs=[ANY] * (len(parts) + len(behind)),
        out_specs=[ANY] * len(parts),
        input_output_aliases={i: i for i in range(len(parts))},
        compiler_params=params(),
        cost_estimate=cost(0, 0),
        name="gate",
    )(*parts, *behind)


def hold_kernel(source, out):
    out[...] = source[...]


def held(value):
    return pl.pallas_call(
        hold_kernel,
        out_shape=jax.ShapeDtypeStruct(value.shape, value.dtype),
        in_specs=[VMEM],
        out_specs=VMEM,
        compiler_params=params(),
        cost_estimate=cost(0, 4 * value.size),
        name="hold_probs",
    )(value)


def halves_kernel(right, left, *refs):
    top, low = refs[-2:]
    top[...] = right[...]
    low[...] = left[...]


def halves(right, left, behind):
    depth, width = right.shape
    shape = (depth // 2, width)
    return pl.pallas_call(
        halves_kernel,
        grid=(1,),
        out_shape=[jax.ShapeDtypeStruct(shape, BF16)] * 2,
        in_specs=[
            pl.BlockSpec(shape, lambda i: (0, 0)),
            pl.BlockSpec(shape, lambda i: (1, 0)),
        ]
        + [ANY] * len(behind),
        out_specs=[pl.BlockSpec(shape, lambda i: (0, 0))] * 2,
        compiler_params=params(),
        cost_estimate=cost(0, 4 * depth * width),
        name="take_halves",
    )(right, left, *behind)


def product_kernel(number, later, place, pairs, count, probs, before, *rest):
    pieces, (weights, total) = rest[:number], rest[-2:]
    outs = rest[-7:-2] if later else rest[-9:-4]
    block = 512
    rows, width = probs.shape[0], total.shape[2]
    half = rows // 2
    vocab_y = place[0]
    first_block = (vocab_y * SIDE + place[1]) * (probs.shape[1] // block)
    total[...] = jnp.zeros_like(total)
    starts = ((0, 0), (1, 0), (3, 0), (2, 0), (2, 512)) if number == 10 else ((0, 0), (1, 0), (2, 0), (3, 0))
    for core, parts in ((place[3], pieces[: number // 2]), (1 - place[3], pieces[number // 2 :])):
        for part, (step, start) in zip(parts, starts):
            x = lax.rem(place[2] + SIDE - step, SIDE)
            weights[x * 2 + core, start : start + part.shape[0]] = part[...]

    def tiles(group, carry):
        for member in range(4):
            slot = group * 4 + member
            teacher = pairs[slot, 0] - first_block
            owner = pairs[slot, 1] // SIDE
            columns = probs[:, pl.ds(pl.multiple_of(teacher * block, block), block)]
            matrix = weights[:, pl.ds(pl.multiple_of(slot * 64, 64), 64), :].reshape(block, width)
            product = jnp.dot(columns, matrix, preferred_element_type=F32)
            if member:
                product = jnp.where(slot < count[0], product, 0.0)
            total[owner] += product
        return carry

    lax.fori_loop(0, (count[0] + 3) // 4, tiles, 0)
    summed = jnp.zeros((rows, width), F32)
    for step in range(SIDE):
        start = lax.rem(vocab_y + step, SIDE) * SIDE
        for z in range(SIDE):
            value = total[start + z]
            summed += value
            value = value.astype(BF16)
            if step == 2:
                outs[3][z * half : z * half + half, :] = value[:half]
                outs[4][z * half : z * half + half, :] = value[half:]
            else:
                outs[step - step // 3][z * rows : z * rows + rows, :] = value
    line = jnp.sum(summed.T, axis=0, keepdims=True)
    if later:
        packed = pack_rows([line + before[0:1]])
    else:
        rest[-4][...] = jnp.broadcast_to(line, rest[-4].shape)
        rest[-3][...] = probs[...]
        packed = pack_rows([before[i : i + 1] for i in range(4)])
    for out in outs[3:]:
        out[SIDE * half : SIDE * half + 16, :] = packed


def products(place, pairs, count, probs, before, mine, other, later, behind=()):
    rows = probs.shape[0]
    depth, width = mine[0].shape
    pieces = [*mine, *other]
    outs = [jax.ShapeDtypeStruct((SIDE * rows, width), BF16)] * 3
    outs += [jax.ShapeDtypeStruct((SIDE * rows // 2 + 16, width), BF16)] * 2
    if not later:
        outs += [jax.ShapeDtypeStruct((8, rows), F32), jax.ShapeDtypeStruct(probs.shape, BF16)]
    return pl.pallas_call(
        functools.partial(product_kernel, len(pieces), later),
        out_shape=outs,
        in_specs=[SMEM, SMEM, SMEM] + [VMEM] * (2 + len(pieces)) + [ANY] * len(behind),
        out_specs=[VMEM] * len(outs),
        scratch_shapes=[
            pltpu.VMEM((2 * SIDE, depth, width), BF16),
            pltpu.VMEM((SIDE * SIDE, rows, width), F32),
        ],
        compiler_params=params(14),
        cost_estimate=cost(
            16 * 2 * rows * 512 * width, 2 * probs.size + 16 * depth * width + 32 * rows * width
        ),
        name="tile_products",
    )(place, pairs, count, probs, before, *pieces, *behind)


def pack_rows(lines):
    rows = [part for line in lines for part in thirds(line)]
    rows.append(jnp.zeros((16 - len(rows), rows[0].shape[1]), F32))
    return jnp.concatenate(rows, axis=0).astype(BF16)


def unpack_rows(packed, number):
    packed = packed.astype(F32)
    return [
        packed[3 * i : 3 * i + 1] + packed[3 * i + 1 : 3 * i + 2] + packed[3 * i + 2 : 3 * i + 3]
        for i in range(number)
    ]


def joined(stats):
    peak = functools.reduce(jnp.maximum, [line[0] for line in stats])
    speak = functools.reduce(jnp.maximum, [line[2] for line in stats])
    factors = [jnp.exp(line[0] - peak) for line in stats]
    mass = sum(line[1] * factor for line, factor in zip(stats, factors))
    smass = sum(line[3] * jnp.exp(line[2] - speak) for line in stats)
    return (peak, mass, speak, smass), factors


def columns_of(lines):
    lines = list(lines) + [jnp.zeros((128 - len(lines), lines[0].shape[1]), F32)]
    return jnp.concatenate(lines, axis=0).T


def relay_kernel(later, near, far, from_left, from_right, mine, *refs):
    depth = from_left.shape[0] - 16
    half = depth // SIDE
    rows = 2 * half
    number = 1 if later else 4
    stats = [unpack_rows(part[depth:, :], number) for part in (mine, from_left, from_right)]
    lines = stats[0] + stats[1] + stats[2]
    lines.append(jnp.zeros((16 - len(lines), rows), F32))
    if later:
        table = refs[0][...]
        near_out, far_out, kept = refs[-3:]
    else:
        near_out, far_out, kept, table_out = refs[-4:]
        own, left, right = (line[0] for line in stats)
        lane = lax.broadcasted_iota(jnp.int32, own.shape, 1)
        other = jnp.where(lane < half, left, right)
        peak = jnp.maximum(own, other)
        table = columns_of([jnp.exp(own - peak), jnp.exp(other - peak)])
        table_out[...] = table
    kept[...] = jnp.concatenate(lines, axis=0)
    near_out[SIDE * rows : SIDE * rows + 16, :] = from_left[depth : depth + 16, :]
    for z in range(SIDE):
        low, high = slice(z * rows, z * rows + half), slice(z * rows + half, (z + 1) * rows)
        part = slice(z * half, (z + 1) * half)
        value = table[:half, 0:1] * near[low, :].astype(F32) + table[:half, 1:2] * from_left[part, :].astype(F32)
        near_out[low, :] = value.astype(BF16)
        near_out[high, :] = near[high, :]
        value = table[half:, 0:1] * far[high, :].astype(F32) + table[half:, 1:2] * from_right[part, :].astype(F32)
        far_out[high, :] = value.astype(BF16)
        far_out[low, :] = far[low, :]


def relayed(near, far, from_left, from_right, mine, tables, behind=()):
    depth, width = near.shape
    rows = depth // SIDE
    outs = [
        jax.ShapeDtypeStruct((depth + 16, width), BF16),
        jax.ShapeDtypeStruct((depth, width), BF16),
        jax.ShapeDtypeStruct((16, rows), F32),
    ]
    if not tables:
        outs.append(jax.ShapeDtypeStruct((rows, 128), F32))
    return pl.pallas_call(
        functools.partial(relay_kernel, bool(tables)),
        out_shape=outs,
        in_specs=[VMEM] * (5 + len(tables)) + [ANY] * len(behind),
        out_specs=[VMEM] * len(outs),
        compiler_params=params(),
        cost_estimate=cost(depth * width, depth * width),
        name="relay_targets",
    )(near, far, from_left, from_right, mine, *tables, *behind)


def merge_kernel(later, place, given, *refs):
    parts = refs[:3]
    width = parts[0].shape[1]
    rows = parts[0].shape[0] // SIDE
    sent = parts[1][SIDE * rows :, :]
    if later:
        table, factors, outs = refs[3][...], refs[4], refs[-SIDE:]
        lines = [given[i : i + 1] for i in range(3)] + unpack_rows(sent, 1)
        packed = pack_rows([sum(line * factors[i : i + 1] for i, line in enumerate(lines))])
    else:
        outs = refs[-2 - SIDE : -2]
        lines = [[given[4 * i + j : 4 * i + j + 1] for j in range(4)] for i in range(3)]
        lines.append(unpack_rows(sent, 4))
        stats, factors = joined(lines)
        packed = pack_rows(stats)
        own, left, right, across = (line[0] for line in lines)
        lane = lax.broadcasted_iota(jnp.int32, own.shape, 1)
        low = lane < rows // 2
        left = jnp.where(low, jnp.maximum(left, across), left)
        right = jnp.where(low, right, jnp.maximum(right, across))
        table = columns_of([jnp.exp(base - stats[0]) for base in (own, left, right)])
        refs[-2][...] = table
        refs[-1][...] = jnp.concatenate(factors + [jnp.zeros((4, rows), F32)], axis=0)
    for step in range(SIDE):
        at = pl.ds(pl.multiple_of(lax.rem(place[1] + step, SIDE) * rows, rows), rows)
        value = table[:, 0:1] * parts[0][at, :].astype(F32)
        for d in range(1, 3):
            value += table[:, d : d + 1] * parts[d][at, :].astype(F32)
        outs[step][0:rows, :] = value.astype(BF16)
        outs[step][rows : rows + 16, :] = packed


def merged(place, given, parts, tables, behind=()):
    width = parts[0].shape[1]
    rows = parts[0].shape[0] // SIDE
    outs = [jax.ShapeDtypeStruct((rows + 16, width), BF16)] * SIDE
    if not tables:
        outs += [jax.ShapeDtypeStruct((rows, 128), F32), jax.ShapeDtypeStruct((8, rows), F32)]
    return pl.pallas_call(
        functools.partial(merge_kernel, bool(tables)),
        out_shape=outs,
        in_specs=[SMEM] + [VMEM] * (4 + len(tables)) + [ANY] * len(behind),
        out_specs=[VMEM] * len(outs),
        compiler_params=params(),
        cost_estimate=cost(rows * width, rows * width),
        name="merge_targets",
    )(place, given, *parts, *tables, *behind)


def gradient_kernel(place, logits, *refs):
    chunks, grad = (refs[:SIDE], refs[SIDE : 2 * SIDE]), refs[2 * SIDE]
    rows, width = logits.shape[0], refs[0].shape[1]
    stats, factors = joined([unpack_rows(part[rows:, :], 4) for part in chunks[0]])
    _, mass, peak, smass = stats
    total = sum(
        unpack_rows(part[rows:, :], 1)[0] * factor for part, factor in zip(chunks[1], factors)
    )
    total = total / mass
    floored = jnp.maximum(total, 1.0)
    scales = [factor / mass / floored for factor in factors]
    table = columns_of(scales + [total / floored / smass, peak, peak + jnp.log(smass)])
    share, peak, norm = (table[:, c : c + 1] for c in range(4, 7))
    terms = jnp.zeros((rows, width), F32)
    for step in range(SIDE):
        block = lax.rem(place[1] + SIDE - step, SIDE)
        for chunk, parts in enumerate(chunks):
            at = pl.ds(pl.multiple_of(block * 512 + chunk * width, width), width)
            scores = logits[:, at]
            target = parts[step][0:rows, :].astype(F32) * table[:, step : step + 1]
            positive = target > 0
            entropy = jnp.where(positive, target * jnp.log(jnp.where(positive, target, 1.0)), 0.0)
            terms += entropy - target * (scores - norm)
            value = share * jnp.exp(scores - peak) - target
            grad[at, :] = value.T.astype(BF16)
    grad[SIDE * 512 :, :] = pack_rows([jnp.sum(terms.T, axis=0, keepdims=True)])


def gradients(place, logits, parts):
    rows, cols = logits.shape
    return pl.pallas_call(
        gradient_kernel,
        out_shape=jax.ShapeDtypeStruct((cols + 16, rows), BF16),
        in_specs=[SMEM] + [VMEM] * (1 + 2 * SIDE),
        out_specs=VMEM,
        compiler_params=params(),
        cost_estimate=cost(60 * rows * cols, 8 * rows * cols, 2 * rows * cols),
        name="logit_grad",
    )(place, logits, *parts)


def stage_kernel(place, unembed, *refs):
    stage, sems = refs[-2:]
    first = place[3] == 0
    copies = []
    for major in range(SIDE):
        for minor in range(SIDE):
            index = major * SIDE + minor
            owner = jnp.where(first, index, minor * SIDE + major)
            start = pl.multiple_of(owner * 256 + place[3] * 128, 128)
            copies.append(
                pltpu.make_async_copy(
                    unembed.at[pl.ds(start, 128), :],
                    stage.at[pl.ds(index * 128, 128), :],
                    sems.at[index],
                )
            )
    for copy in copies:
        copy.start()
    for copy in copies:
        copy.wait()


def staged(place, unembed, behind):
    depth, cols = unembed.shape
    return pl.pallas_call(
        stage_kernel,
        out_shape=jax.ShapeDtypeStruct((depth // 2, cols), BF16),
        in_specs=[SMEM, pl.BlockSpec(memory_space=pltpu.HBM)] + [ANY] * len(behind),
        out_specs=VMEM,
        scratch_shapes=[pltpu.SemaphoreType.DMA((SIDE * SIDE,))],
        compiler_params=params(42),
        cost_estimate=cost(0, depth * cols),
        name="stage_unembed",
    )(place, unembed, *behind)


def own_kernel(stage, mine, out):
    depth = stage.shape[1]
    for step in range(SIDE):
        rows = slice(step * 512, step * 512 + 512)
        result = jnp.dot(stage[rows, :], mine[0:depth, :], preferred_element_type=F32)
        out[rows, :] = result.astype(BF16)


def own_hidden(stage, mine):
    depth, rows = stage.shape[0], mine.shape[1]
    return pl.pallas_call(
        own_kernel,
        out_shape=jax.ShapeDtypeStruct((depth, rows), BF16),
        in_specs=[VMEM, VMEM],
        out_specs=VMEM,
        compiler_params=params(),
        cost_estimate=cost(2 * stage.size * rows, 2 * stage.size),
        name="own_hidden",
    )(stage, mine)


def other_kernel(far_only, place, stage, mine, other, own, *refs):
    depth = stage.shape[1]
    rows = mine.shape[1]
    lanes = pl.ds(pl.multiple_of(place[3] * rows, rows), rows)
    other_lanes = pl.ds(pl.multiple_of((1 - place[3]) * rows, rows), rows)
    for index, step in enumerate((2,) if far_only else (0, 1, 3)):
        at = pl.ds(pl.multiple_of(lax.rem(place[4] + step, SIDE) * 512, 512), 512)
        result = jnp.dot(stage[at, :], other[0:depth, :], preferred_element_type=F32).astype(BF16)
        if far_only:
            for half, out in enumerate(refs[-2:]):
                out[0:256, other_lanes] = result[half * 256 : half * 256 + 256]
                out[256:272, lanes] = mine[depth : depth + 16, :]
                out[256:272, other_lanes] = other[depth : depth + 16, :]
                at = pl.multiple_of(lax.rem(place[4] + step, SIDE) * 512 + half * 256, 256)
                out[0:256, lanes] = own[pl.ds(at, 256), :]
        else:
            out = refs[index - 3]
            out[:, other_lanes] = result
            out[:, lanes] = own[at, :]


def other_hidden(far_only, place, stage, mine, other, own, behind=()):
    rows = mine.shape[1]
    shapes = [(272, 2 * rows)] * 2 if far_only else [(512, 2 * rows)] * 3
    return pl.pallas_call(
        functools.partial(other_kernel, far_only),
        out_shape=[jax.ShapeDtypeStruct(shape, BF16) for shape in shapes],
        in_specs=[SMEM] + [VMEM] * 4 + [ANY] * len(behind),
        out_specs=[VMEM] * len(shapes),
        compiler_params=params(),
        cost_estimate=cost((1 if far_only else 3) * stage.size * rows // 2, 2 * stage.size),
        name="other_hidden",
    )(place, stage, mine, other, own, *behind)


def pass_kernel(near, far, from_left, from_right, near_out, far_out):
    near_out[0:256, :] = (near[0:256, :].astype(F32) + from_left[0:256, :].astype(F32)).astype(BF16)
    near_out[256:512, :] = near[256:512, :]
    near_out[512:528, :] = from_left[256:272, :]
    far_out[0:256, :] = far[0:256, :]
    far_out[256:512, :] = (far[256:512, :].astype(F32) + from_right[0:256, :].astype(F32)).astype(BF16)


def passed(near, far, from_left, from_right):
    rows = near.shape[1]
    return pl.pallas_call(
        pass_kernel,
        out_shape=[jax.ShapeDtypeStruct((528, rows), BF16), jax.ShapeDtypeStruct((512, rows), BF16)],
        in_specs=[VMEM] * 4,
        out_specs=[VMEM] * 2,
        compiler_params=params(),
        cost_estimate=cost(512 * rows, 10 * 512 * rows),
        name="pass_grads",
    )(near, far, from_left, from_right)


def ordered_loss(index, pieces, ordered):
    for step, piece in pieces:
        ordered[lax.rem(index + step, SIDE)] = unpack_rows(piece, 1)[0]
    return ((ordered[0] + ordered[1]) + ordered[2]) + ordered[3]


def middle_kernel(place, own, left, right, mine, from_left, from_right, *refs):
    outs, ordered = refs[:SIDE], refs[SIDE]
    pieces = [
        (0, mine[256:272, :]),
        (3, from_left[256:272, :]),
        (1, from_right[256:272, :]),
        (2, left[512:528, :]),
    ]
    packed = pack_rows([ordered_loss(place[4], pieces, ordered)])
    for step in range(SIDE):
        at = pl.ds(pl.multiple_of(lax.rem(place[5] + step, SIDE) * 128, 128), 128)
        value = own[at, :].astype(F32) + left[at, :].astype(F32) + right[at, :].astype(F32)
        outs[step][0:128, :] = value.astype(BF16)
        outs[step][128:144, :] = packed


def middle(place, own, left, right, mine, from_left, from_right):
    rows = own.shape[1]
    return pl.pallas_call(
        middle_kernel,
        out_shape=[jax.ShapeDtypeStruct((144, rows), BF16)] * SIDE,
        in_specs=[SMEM] + [VMEM] * 6,
        out_specs=[VMEM] * SIDE,
        scratch_shapes=[pltpu.VMEM((SIDE, 1, rows), F32)],
        compiler_params=params(),
        cost_estimate=cost(4 * 512 * rows, 10 * 512 * rows),
        name="merge_grads",
    )(place, own, left, right, mine, from_left, from_right)


def total_kernel(place, *refs):
    parts = refs[:SIDE]
    keep, give, loss, ordered = refs[SIDE:]
    rows = keep.shape[1]
    mine = pl.ds(pl.multiple_of(place[3] * rows, rows), rows)
    other = pl.ds(pl.multiple_of((1 - place[3]) * rows, rows), rows)
    pieces = [((SIDE - step) % SIDE, part[128:144, :]) for step, part in enumerate(parts)]
    ordered[4] = ordered_loss(place[5], pieces, ordered)
    loss[...] = jnp.broadcast_to(ordered[4, :, mine], loss.shape)
    for lanes, out in ((other, give), (mine, keep)):
        value = parts[0][0:128, lanes].astype(F32)
        for part in parts[1:]:
            value += part[0:128, lanes].astype(F32)
        out[...] = value.astype(BF16)


def totals(place, parts):
    rows = parts[0].shape[1] // 2
    half = jax.ShapeDtypeStruct((128, rows), BF16)
    return pl.pallas_call(
        total_kernel,
        out_shape=[half, half, jax.ShapeDtypeStruct((8, rows), F32)],
        in_specs=[SMEM] + [VMEM] * SIDE,
        out_specs=[VMEM] * 3,
        scratch_shapes=[pltpu.VMEM((SIDE + 1, 1, 2 * rows), F32)],
        compiler_params=params(),
        cost_estimate=cost(8 * 128 * rows, 20 * 128 * rows),
        name="sum_grads",
    )(place, *parts)


def turn_kernel(place, keep, given, grad):
    mine = pl.ds(pl.multiple_of(place[3] * 128, 128), 128)
    other = pl.ds(pl.multiple_of((1 - place[3]) * 128, 128), 128)
    grad[:, mine] = keep[...].astype(F32).T.astype(BF16)
    grad[:, other] = given[...].astype(F32).T.astype(BF16)


def turned(place, keep, given):
    rows = keep.shape[1]
    return pl.pallas_call(
        turn_kernel,
        out_shape=jax.ShapeDtypeStruct((rows, 256), BF16),
        in_specs=[SMEM, VMEM, VMEM],
        out_specs=VMEM,
        compiler_params=params(),
        cost_estimate=cost(0, 4 * 256 * rows),
        name="turn_grads",
    )(place, keep, given)


def spread(parts, axis):
    return [parts[0]] + [send(parts[step], axis, step) for step in (1, 2, 3)]


def cross(value, step, first):
    def target(y, z, core):
        if (core == 0) == first:
            y = (y + step) % SIDE
        else:
            z = (z + step) % SIDE
        return (y * SIDE + z) * 2 + core

    places = [(y, z, core) for y in range(SIDE) for z in range(SIDE) for core in range(2)]
    pairs = [(i, target(*at)) for i, at in enumerate(places)]
    return lax.ppermute(value, ("vy", "vz", "tc"), pairs)


def shards(teacher_logits, student_hidden, student_unembed, tile_weights, tile_pairs, tile_count):
    y, z, x, core = (lax.axis_index(name) for name in ("vy", "vz", "tx", "tc"))
    crossing = [jnp.where(core == 0, y, z), jnp.where(core == 0, z, y)]
    place = jnp.stack([y, z, x, core] + crossing).astype(jnp.int32)
    rows = teacher_logits.shape[0]
    teacher = teacher_logits.astype(F32)
    peak = jnp.max(teacher, axis=1)
    shifted = jnp.exp(teacher - peak[:, None])
    mass = jnp.sum(shifted, axis=1)
    probs = shifted.astype(BF16)

    logits = jnp.dot(student_hidden, student_unembed, preferred_element_type=F32)
    speak = jnp.max(logits, axis=1)
    smass = jnp.sum(jnp.exp(logits - speak[:, None]), axis=1)

    before = jnp.stack([peak, mass, speak, smass] * 2)

    piece = tile_weights[:, :, : tile_weights.shape[2] // 2].reshape(-1, tile_weights.shape[2] // 2)
    probs = held(probs)
    mine = [piece, *gated(spread([piece] * SIDE, "tx")[1:], [mass, smass, probs])]
    other = [swap(piece) for piece in mine]

    piece = sliced(tile_weights, 1, [mine[1]])
    right, left = send(piece, "tx", 1), send(piece, "tx", 3)
    *parts, total, probs = products(
        place, tile_pairs, tile_count, probs, before, mine, other, False, [piece]
    )
    top, low = halves(right, left, [parts[0]])
    own, near, far, to_right, to_left = parts
    left_part, right_part = send(to_right, "vy", 1), send(to_left, "vy", 3)
    near, far, given, table = relayed(near, far, left_part, right_part, to_right, [], [right, left])
    near, far = send(near, "vy", 1), send(far, "vy", 3)
    top, low = gated([send(top, "tx", 1), send(low, "tx", 3)], [near, far])
    mine = [piece, right, left, top, low]
    later = products(
        place, tile_pairs, tile_count, probs, total, mine, [swap(piece) for piece in mine], True
    )

    *first, scales, factors = merged(place, given, [own, near, far], [], [later[0]])
    own, near, far, to_right, to_left = later
    left_part, right_part = send(to_right, "vy", 1), send(to_left, "vy", 3)
    stage = staged(place, student_unembed, [own])
    near, far, given = relayed(near, far, left_part, right_part, to_right, [table], [stage])
    parts = [own, send(near, "vy", 1), send(far, "vy", 3)]
    first = spread(first, "vz")
    second = merged(place, given, parts, [scales, factors])
    mine = gradients(place, logits, first + spread(second, "vz"))

    own = own_hidden(stage, mine)
    other = swap(mine)
    to_right, to_left = other_hidden(True, place, stage, mine, other, own)
    from_left, from_right = cross(to_right, 1, True), cross(to_left, 3, True)
    here, near, far = other_hidden(False, place, stage, mine, other, own, [to_right])
    near, far = passed(near, far, from_left, from_right)
    near, far = cross(near, 1, True), cross(far, 3, True)
    parts = middle(place, here, near, far, to_right, from_left, from_right)
    parts = [parts[0], *(cross(parts[step], step, False) for step in (1, 2, 3))]
    keep, give, loss = totals(place, parts)
    return turned(place, keep, swap(give)), loss[0]


def solution(mesh):
    grid = Mesh(mesh.devices.reshape(SIDE, SIDE, SIDE, 2), ("vy", "vz", "tx", "tc"))
    vocab, tokens = ("vy", "vz"), ("tx", "tc")
    return jax.shard_map(
        shards,
        mesh=grid,
        in_specs=(
            P(tokens, vocab),
            P(tokens, None),
            P(None, vocab),
            P(vocab, tokens, None),
            P(vocab, None),
            P(vocab),
        ),
        out_specs=(P(tokens, vocab), P(tokens)),
        check_vma=False,
    )
```

```python
import functools

import jax
import jax.numpy as jnp
from jax import lax
from jax.experimental import pallas as pl
from jax.experimental.pallas import tpu as pltpu
from jax.sharding import Mesh
from jax.sharding import PartitionSpec as P

F32 = jnp.float32
BF16 = jnp.bfloat16
SIDE = 4
VMEM = pl.BlockSpec(memory_space=pltpu.VMEM)
SMEM = pl.BlockSpec(memory_space=pltpu.SMEM)
ANY = pl.BlockSpec(memory_space=pl.ANY)
MIB = 1024 * 1024


def params(mib=16):
    return pltpu.CompilerParams(vmem_limit_bytes=mib * MIB)


def cost(flops, moved, transcendentals=0):
    return pl.CostEstimate(flops=flops, bytes_accessed=moved, transcendentals=transcendentals)


def send(value, axis, step):
    return lax.ppermute(value, axis, [(i, (i + step) % SIDE) for i in range(SIDE)])


def swap(value):
    return lax.ppermute(value, "tc", [(0, 1), (1, 0)])


def turn(value):
    pairs = [(x * 2 + core, (x + 1 - 2 * core) % SIDE * 2 + core) for x in range(SIDE) for core in (0, 1)]
    return lax.ppermute(value, ("tx", "tc"), pairs)


def thirds(value):
    high = value.astype(BF16).astype(F32)
    rest = value - high
    middle = rest.astype(BF16).astype(F32)
    return high, middle, rest - middle


def slice_kernel(weights, *refs):
    piece = refs[-1]
    piece[...] = weights[...].reshape(piece.shape)


def sliced(weights, index, behind=()):
    slots, shard_rows, cols = weights.shape
    width = cols // 2
    return pl.pallas_call(
        slice_kernel,
        grid=(1,),
        out_shape=jax.ShapeDtypeStruct((slots * shard_rows, width), BF16),
        in_specs=[pl.BlockSpec((slots, shard_rows, width), lambda i: (0, 0, index))]
        + [ANY] * len(behind),
        out_specs=pl.BlockSpec((slots * shard_rows, width), lambda i: (0, 0)),
        compiler_params=params(),
        cost_estimate=cost(0, 2 * weights.size),
        name="slice_weights",
    )(weights, *behind)


def gate_kernel(*refs):
    pass


def gated(parts, behind):
    return pl.pallas_call(
        gate_kernel,
        out_shape=[jax.ShapeDtypeStruct(part.shape, part.dtype) for part in parts],
        in_specs=[ANY] * (len(parts) + len(behind)),
        out_specs=[ANY] * len(parts),
        input_output_aliases={i: i for i in range(len(parts))},
        compiler_params=params(),
        cost_estimate=cost(0, 0),
        name="gate",
    )(*parts, *behind)


def hold_kernel(source, out):
    out[...] = source[...]


def held(value):
    return pl.pallas_call(
        hold_kernel,
        out_shape=jax.ShapeDtypeStruct(value.shape, value.dtype),
        in_specs=[VMEM],
        out_specs=VMEM,
        compiler_params=params(),
        cost_estimate=cost(0, 4 * value.size),
        name="hold_probs",
    )(value)


def product_kernel(number, later, place, pairs, count, probs, before, *rest):
    pieces, (weights, total) = rest[:number], rest[-2:]
    outs = rest[-7:-2] if later else rest[-9:-4]
    block = 512
    rows, width = probs.shape[0], total.shape[2]
    half = rows // 2
    vocab_y = place[0]
    first_block = (vocab_y * SIDE + place[1]) * (probs.shape[1] // block)
    total[...] = jnp.zeros_like(total)
    for core, parts in ((place[3], pieces[:SIDE]), (1 - place[3], pieces[SIDE:])):
        for step, part in enumerate(parts):
            x = lax.rem(place[2] + step + (SIDE - 2 * step) * (1 - core), SIDE)
            weights[x * 2 + core] = part[...]

    def tiles(group, carry):
        for member in range(4):
            slot = group * 4 + member
            teacher = pairs[slot, 0] - first_block
            owner = pairs[slot, 1] // SIDE
            columns = probs[:, pl.ds(pl.multiple_of(teacher * block, block), block)]
            matrix = weights[:, pl.ds(pl.multiple_of(slot * 64, 64), 64), :].reshape(block, width)
            product = jnp.dot(columns, matrix, preferred_element_type=F32)
            if member:
                product = jnp.where(slot < count[0], product, 0.0)
            total[owner] += product
        return carry

    lax.fori_loop(0, (count[0] + 3) // 4, tiles, 0)
    summed = jnp.zeros((rows, width), F32)
    for step in range(SIDE):
        start = lax.rem(vocab_y + step, SIDE) * SIDE
        for z in range(SIDE):
            value = total[start + z]
            summed += value
            value = value.astype(BF16)
            if step == 2:
                outs[3][z * half : z * half + half, :] = value[:half]
                outs[4][z * half : z * half + half, :] = value[half:]
            else:
                outs[step - step // 3][z * rows : z * rows + rows, :] = value
    line = jnp.sum(summed.T, axis=0, keepdims=True)
    if later:
        packed = pack_rows([line + before[0:1]])
    else:
        rest[-4][...] = jnp.broadcast_to(line, rest[-4].shape)
        rest[-3][...] = probs[...]
        packed = pack_rows([before[i : i + 1] for i in range(4)])
    for out in outs[3:]:
        out[SIDE * half : SIDE * half + 16, :] = packed


def products(place, pairs, count, probs, before, mine, other, later, behind=()):
    rows = probs.shape[0]
    depth, width = mine[0].shape
    pieces = [*mine, *other]
    outs = [jax.ShapeDtypeStruct((SIDE * rows, width), BF16)] * 3
    outs += [jax.ShapeDtypeStruct((SIDE * rows // 2 + 16, width), BF16)] * 2
    if not later:
        outs += [jax.ShapeDtypeStruct((8, rows), F32), jax.ShapeDtypeStruct(probs.shape, BF16)]
    return pl.pallas_call(
        functools.partial(product_kernel, len(pieces), later),
        out_shape=outs,
        in_specs=[SMEM, SMEM, SMEM] + [VMEM] * (2 + len(pieces)) + [ANY] * len(behind),
        out_specs=[VMEM] * len(outs),
        scratch_shapes=[
            pltpu.VMEM((2 * SIDE, depth, width), BF16),
            pltpu.VMEM((SIDE * SIDE, rows, width), F32),
        ],
        compiler_params=params(14),
        cost_estimate=cost(
            16 * 2 * rows * 512 * width, 2 * probs.size + 16 * depth * width + 32 * rows * width
        ),
        name="tile_products",
    )(place, pairs, count, probs, before, *pieces, *behind)


def pack_rows(lines):
    rows = [part for line in lines for part in thirds(line)]
    rows.append(jnp.zeros((16 - len(rows), rows[0].shape[1]), F32))
    return jnp.concatenate(rows, axis=0).astype(BF16)


def unpack_rows(packed, number):
    packed = packed.astype(F32)
    return [
        packed[3 * i : 3 * i + 1] + packed[3 * i + 1 : 3 * i + 2] + packed[3 * i + 2 : 3 * i + 3]
        for i in range(number)
    ]


def joined(stats):
    peak = functools.reduce(jnp.maximum, [line[0] for line in stats])
    speak = functools.reduce(jnp.maximum, [line[2] for line in stats])
    factors = [jnp.exp(line[0] - peak) for line in stats]
    mass = sum(line[1] * factor for line, factor in zip(stats, factors))
    smass = sum(line[3] * jnp.exp(line[2] - speak) for line in stats)
    return (peak, mass, speak, smass), factors


def columns_of(lines):
    lines = list(lines) + [jnp.zeros((128 - len(lines), lines[0].shape[1]), F32)]
    return jnp.concatenate(lines, axis=0).T


def relay_kernel(later, near, far, from_left, from_right, mine, *refs):
    depth = from_left.shape[0] - 16
    half = depth // SIDE
    rows = 2 * half
    number = 1 if later else 4
    stats = [unpack_rows(part[depth:, :], number) for part in (mine, from_left, from_right)]
    lines = stats[0] + stats[1] + stats[2]
    lines.append(jnp.zeros((16 - len(lines), rows), F32))
    if later:
        table = refs[0][...]
        near_out, far_out, kept = refs[-3:]
    else:
        near_out, far_out, kept, table_out = refs[-4:]
        own, left, right = (line[0] for line in stats)
        lane = lax.broadcasted_iota(jnp.int32, own.shape, 1)
        other = jnp.where(lane < half, left, right)
        peak = jnp.maximum(own, other)
        table = columns_of([jnp.exp(own - peak), jnp.exp(other - peak)])
        table_out[...] = table
    kept[...] = jnp.concatenate(lines, axis=0)
    near_out[SIDE * rows : SIDE * rows + 16, :] = from_left[depth : depth + 16, :]
    for z in range(SIDE):
        low, high = slice(z * rows, z * rows + half), slice(z * rows + half, (z + 1) * rows)
        part = slice(z * half, (z + 1) * half)
        value = table[:half, 0:1] * near[low, :].astype(F32) + table[:half, 1:2] * from_left[part, :].astype(F32)
        near_out[low, :] = value.astype(BF16)
        near_out[high, :] = near[high, :]
        value = table[half:, 0:1] * far[high, :].astype(F32) + table[half:, 1:2] * from_right[part, :].astype(F32)
        far_out[high, :] = value.astype(BF16)
        far_out[low, :] = far[low, :]


def relayed(near, far, from_left, from_right, mine, tables, behind=()):
    depth, width = near.shape
    rows = depth // SIDE
    outs = [
        jax.ShapeDtypeStruct((depth + 16, width), BF16),
        jax.ShapeDtypeStruct((depth, width), BF16),
        jax.ShapeDtypeStruct((16, rows), F32),
    ]
    if not tables:
        outs.append(jax.ShapeDtypeStruct((rows, 128), F32))
    return pl.pallas_call(
        functools.partial(relay_kernel, bool(tables)),
        out_shape=outs,
        in_specs=[VMEM] * (5 + len(tables)) + [ANY] * len(behind),
        out_specs=[VMEM] * len(outs),
        compiler_params=params(),
        cost_estimate=cost(depth * width, depth * width),
        name="relay_targets",
    )(near, far, from_left, from_right, mine, *tables, *behind)


def merge_kernel(later, place, given, *refs):
    parts = refs[:3]
    width = parts[0].shape[1]
    rows = parts[0].shape[0] // SIDE
    sent = parts[1][SIDE * rows :, :]
    if later:
        table, factors, outs = refs[3][...], refs[4], refs[-SIDE:]
        lines = [given[i : i + 1] for i in range(3)] + unpack_rows(sent, 1)
        packed = pack_rows([sum(line * factors[i : i + 1] for i, line in enumerate(lines))])
    else:
        outs = refs[-2 - SIDE : -2]
        lines = [[given[4 * i + j : 4 * i + j + 1] for j in range(4)] for i in range(3)]
        lines.append(unpack_rows(sent, 4))
        stats, factors = joined(lines)
        packed = pack_rows(stats)
        own, left, right, across = (line[0] for line in lines)
        lane = lax.broadcasted_iota(jnp.int32, own.shape, 1)
        low = lane < rows // 2
        left = jnp.where(low, jnp.maximum(left, across), left)
        right = jnp.where(low, right, jnp.maximum(right, across))
        table = columns_of([jnp.exp(base - stats[0]) for base in (own, left, right)])
        refs[-2][...] = table
        refs[-1][...] = jnp.concatenate(factors + [jnp.zeros((4, rows), F32)], axis=0)
    for step in range(SIDE):
        at = pl.ds(pl.multiple_of(lax.rem(place[1] + step, SIDE) * rows, rows), rows)
        value = table[:, 0:1] * parts[0][at, :].astype(F32)
        for d in range(1, 3):
            value += table[:, d : d + 1] * parts[d][at, :].astype(F32)
        outs[step][0:rows, :] = value.astype(BF16)
        outs[step][rows : rows + 16, :] = packed


def merged(place, given, parts, tables, behind=()):
    width = parts[0].shape[1]
    rows = parts[0].shape[0] // SIDE
    outs = [jax.ShapeDtypeStruct((rows + 16, width), BF16)] * SIDE
    if not tables:
        outs += [jax.ShapeDtypeStruct((rows, 128), F32), jax.ShapeDtypeStruct((8, rows), F32)]
    return pl.pallas_call(
        functools.partial(merge_kernel, bool(tables)),
        out_shape=outs,
        in_specs=[SMEM] + [VMEM] * (4 + len(tables)) + [ANY] * len(behind),
        out_specs=[VMEM] * len(outs),
        compiler_params=params(),
        cost_estimate=cost(rows * width, rows * width),
        name="merge_targets",
    )(place, given, *parts, *tables, *behind)


def gradient_kernel(place, logits, *refs):
    chunks, grad = (refs[:SIDE], refs[SIDE : 2 * SIDE]), refs[2 * SIDE]
    rows, width = logits.shape[0], refs[0].shape[1]
    stats, factors = joined([unpack_rows(part[rows:, :], 4) for part in chunks[0]])
    _, mass, peak, smass = stats
    total = sum(
        unpack_rows(part[rows:, :], 1)[0] * factor for part, factor in zip(chunks[1], factors)
    )
    total = total / mass
    floored = jnp.maximum(total, 1.0)
    scales = [factor / mass / floored for factor in factors]
    table = columns_of(scales + [total / floored / smass, peak, peak + jnp.log(smass)])
    share, peak, norm = (table[:, c : c + 1] for c in range(4, 7))
    terms = jnp.zeros((rows, width), F32)
    for step in range(SIDE):
        block = lax.rem(place[1] + SIDE - step, SIDE)
        for chunk, parts in enumerate(chunks):
            at = pl.ds(pl.multiple_of(block * 512 + chunk * width, width), width)
            scores = logits[:, at]
            target = parts[step][0:rows, :].astype(F32) * table[:, step : step + 1]
            positive = target > 0
            entropy = jnp.where(positive, target * jnp.log(jnp.where(positive, target, 1.0)), 0.0)
            terms += entropy - target * (scores - norm)
            value = share * jnp.exp(scores - peak) - target
            grad[at, :] = value.T.astype(BF16)
    grad[SIDE * 512 :, :] = pack_rows([jnp.sum(terms.T, axis=0, keepdims=True)])


def gradients(place, logits, parts):
    rows, cols = logits.shape
    return pl.pallas_call(
        gradient_kernel,
        out_shape=jax.ShapeDtypeStruct((cols + 16, rows), BF16),
        in_specs=[SMEM] + [VMEM] * (1 + 2 * SIDE),
        out_specs=VMEM,
        compiler_params=params(),
        cost_estimate=cost(60 * rows * cols, 8 * rows * cols, 2 * rows * cols),
        name="logit_grad",
    )(place, logits, *parts)


def stage_kernel(place, unembed, *refs):
    stage, sems = refs[-2:]
    first = place[3] == 0
    copies = []
    for major in range(SIDE):
        for minor in range(SIDE):
            index = major * SIDE + minor
            owner = jnp.where(first, index, minor * SIDE + major)
            start = pl.multiple_of(owner * 256 + place[3] * 128, 128)
            copies.append(
                pltpu.make_async_copy(
                    unembed.at[pl.ds(start, 128), :],
                    stage.at[pl.ds(index * 128, 128), :],
                    sems.at[index],
                )
            )
    for copy in copies:
        copy.start()
    for copy in copies:
        copy.wait()


def staged(place, unembed, behind):
    depth, cols = unembed.shape
    return pl.pallas_call(
        stage_kernel,
        out_shape=jax.ShapeDtypeStruct((depth // 2, cols), BF16),
        in_specs=[SMEM, pl.BlockSpec(memory_space=pltpu.HBM)] + [ANY] * len(behind),
        out_specs=VMEM,
        scratch_shapes=[pltpu.SemaphoreType.DMA((SIDE * SIDE,))],
        compiler_params=params(42),
        cost_estimate=cost(0, depth * cols),
        name="stage_unembed",
    )(place, unembed, *behind)


def own_kernel(stage, mine, out):
    depth = stage.shape[1]
    for step in range(SIDE):
        rows = slice(step * 512, step * 512 + 512)
        result = jnp.dot(stage[rows, :], mine[0:depth, :], preferred_element_type=F32)
        out[rows, :] = result.astype(BF16)


def own_hidden(stage, mine):
    depth, rows = stage.shape[0], mine.shape[1]
    return pl.pallas_call(
        own_kernel,
        out_shape=jax.ShapeDtypeStruct((depth, rows), BF16),
        in_specs=[VMEM, VMEM],
        out_specs=VMEM,
        compiler_params=params(),
        cost_estimate=cost(2 * stage.size * rows, 2 * stage.size),
        name="own_hidden",
    )(stage, mine)


def other_kernel(far_only, place, stage, mine, other, own, *refs):
    depth = stage.shape[1]
    rows = mine.shape[1]
    lanes = pl.ds(pl.multiple_of(place[3] * rows, rows), rows)
    other_lanes = pl.ds(pl.multiple_of((1 - place[3]) * rows, rows), rows)
    for index, step in enumerate((2,) if far_only else (0, 1, 3)):
        at = pl.ds(pl.multiple_of(lax.rem(place[4] + step, SIDE) * 512, 512), 512)
        result = jnp.dot(stage[at, :], other[0:depth, :], preferred_element_type=F32).astype(BF16)
        if far_only:
            for half, out in enumerate(refs[-2:]):
                out[0:256, other_lanes] = result[half * 256 : half * 256 + 256]
                out[256:272, lanes] = mine[depth : depth + 16, :]
                out[256:272, other_lanes] = other[depth : depth + 16, :]
                at = pl.multiple_of(lax.rem(place[4] + step, SIDE) * 512 + half * 256, 256)
                out[0:256, lanes] = own[pl.ds(at, 256), :]
        else:
            out = refs[index - 3]
            out[:, other_lanes] = result
            out[:, lanes] = own[at, :]


def other_hidden(far_only, place, stage, mine, other, own, behind=()):
    rows = mine.shape[1]
    shapes = [(272, 2 * rows)] * 2 if far_only else [(512, 2 * rows)] * 3
    return pl.pallas_call(
        functools.partial(other_kernel, far_only),
        out_shape=[jax.ShapeDtypeStruct(shape, BF16) for shape in shapes],
        in_specs=[SMEM] + [VMEM] * 4 + [ANY] * len(behind),
        out_specs=[VMEM] * len(shapes),
        compiler_params=params(),
        cost_estimate=cost((1 if far_only else 3) * stage.size * rows // 2, 2 * stage.size),
        name="other_hidden",
    )(place, stage, mine, other, own, *behind)


def pass_kernel(near, far, from_left, from_right, near_out, far_out):
    near_out[0:256, :] = (near[0:256, :].astype(F32) + from_left[0:256, :].astype(F32)).astype(BF16)
    near_out[256:512, :] = near[256:512, :]
    near_out[512:528, :] = from_left[256:272, :]
    far_out[0:256, :] = far[0:256, :]
    far_out[256:512, :] = (far[256:512, :].astype(F32) + from_right[0:256, :].astype(F32)).astype(BF16)


def passed(near, far, from_left, from_right):
    rows = near.shape[1]
    return pl.pallas_call(
        pass_kernel,
        out_shape=[jax.ShapeDtypeStruct((528, rows), BF16), jax.ShapeDtypeStruct((512, rows), BF16)],
        in_specs=[VMEM] * 4,
        out_specs=[VMEM] * 2,
        compiler_params=params(),
        cost_estimate=cost(512 * rows, 10 * 512 * rows),
        name="pass_grads",
    )(near, far, from_left, from_right)


def ordered_loss(index, pieces, ordered):
    for step, piece in pieces:
        ordered[lax.rem(index + step, SIDE)] = unpack_rows(piece, 1)[0]
    return ((ordered[0] + ordered[1]) + ordered[2]) + ordered[3]


def middle_kernel(place, own, left, right, mine, from_left, from_right, *refs):
    outs, ordered = refs[:SIDE], refs[SIDE]
    pieces = [
        (0, mine[256:272, :]),
        (3, from_left[256:272, :]),
        (1, from_right[256:272, :]),
        (2, left[512:528, :]),
    ]
    packed = pack_rows([ordered_loss(place[4], pieces, ordered)])
    for step in range(SIDE):
        at = pl.ds(pl.multiple_of(lax.rem(place[5] + step, SIDE) * 128, 128), 128)
        value = own[at, :].astype(F32) + left[at, :].astype(F32) + right[at, :].astype(F32)
        outs[step][0:128, :] = value.astype(BF16)
        outs[step][128:144, :] = packed


def middle(place, own, left, right, mine, from_left, from_right):
    rows = own.shape[1]
    return pl.pallas_call(
        middle_kernel,
        out_shape=[jax.ShapeDtypeStruct((144, rows), BF16)] * SIDE,
        in_specs=[SMEM] + [VMEM] * 6,
        out_specs=[VMEM] * SIDE,
        scratch_shapes=[pltpu.VMEM((SIDE, 1, rows), F32)],
        compiler_params=params(),
        cost_estimate=cost(4 * 512 * rows, 10 * 512 * rows),
        name="merge_grads",
    )(place, own, left, right, mine, from_left, from_right)


def total_kernel(place, *refs):
    parts = refs[:SIDE]
    keep, give, loss, ordered = refs[SIDE:]
    rows = keep.shape[1]
    mine = pl.ds(pl.multiple_of(place[3] * rows, rows), rows)
    other = pl.ds(pl.multiple_of((1 - place[3]) * rows, rows), rows)
    pieces = [((SIDE - step) % SIDE, part[128:144, :]) for step, part in enumerate(parts)]
    ordered[4] = ordered_loss(place[5], pieces, ordered)
    loss[...] = jnp.broadcast_to(ordered[4, :, mine], loss.shape)
    for lanes, out in ((other, give), (mine, keep)):
        value = parts[0][0:128, lanes].astype(F32)
        for part in parts[1:]:
            value += part[0:128, lanes].astype(F32)
        out[...] = value.astype(BF16)


def totals(place, parts):
    rows = parts[0].shape[1] // 2
    half = jax.ShapeDtypeStruct((128, rows), BF16)
    return pl.pallas_call(
        total_kernel,
        out_shape=[half, half, jax.ShapeDtypeStruct((8, rows), F32)],
        in_specs=[SMEM] + [VMEM] * SIDE,
        out_specs=[VMEM] * 3,
        scratch_shapes=[pltpu.VMEM((SIDE + 1, 1, 2 * rows), F32)],
        compiler_params=params(),
        cost_estimate=cost(8 * 128 * rows, 20 * 128 * rows),
        name="sum_grads",
    )(place, *parts)


def turn_kernel(place, keep, given, grad):
    mine = pl.ds(pl.multiple_of(place[3] * 128, 128), 128)
    other = pl.ds(pl.multiple_of((1 - place[3]) * 128, 128), 128)
    grad[:, mine] = keep[...].astype(F32).T.astype(BF16)
    grad[:, other] = given[...].astype(F32).T.astype(BF16)


def turned(place, keep, given):
    rows = keep.shape[1]
    return pl.pallas_call(
        turn_kernel,
        out_shape=jax.ShapeDtypeStruct((rows, 256), BF16),
        in_specs=[SMEM, VMEM, VMEM],
        out_specs=VMEM,
        compiler_params=params(),
        cost_estimate=cost(0, 4 * 256 * rows),
        name="turn_grads",
    )(place, keep, given)


def spread(parts, axis):
    return [parts[0]] + [send(parts[step], axis, step) for step in (1, 2, 3)]


def cross(value, step, first):
    def target(y, z, core):
        if (core == 0) == first:
            y = (y + step) % SIDE
        else:
            z = (z + step) % SIDE
        return (y * SIDE + z) * 2 + core

    places = [(y, z, core) for y in range(SIDE) for z in range(SIDE) for core in range(2)]
    pairs = [(i, target(*at)) for i, at in enumerate(places)]
    return lax.ppermute(value, ("vy", "vz", "tc"), pairs)


def shards(teacher_logits, student_hidden, student_unembed, tile_weights, tile_pairs, tile_count):
    y, z, x, core = (lax.axis_index(name) for name in ("vy", "vz", "tx", "tc"))
    crossing = [jnp.where(core == 0, y, z), jnp.where(core == 0, z, y)]
    place = jnp.stack([y, z, x, core] + crossing).astype(jnp.int32)
    rows = teacher_logits.shape[0]
    teacher = teacher_logits.astype(F32)
    peak = jnp.max(teacher, axis=1)
    shifted = jnp.exp(teacher - peak[:, None])
    mass = jnp.sum(shifted, axis=1)
    probs = shifted.astype(BF16)

    logits = jnp.dot(student_hidden, student_unembed, preferred_element_type=F32)
    speak = jnp.max(logits, axis=1)
    smass = jnp.sum(jnp.exp(logits - speak[:, None]), axis=1)

    before = jnp.stack([peak, mass, speak, smass] * 2)

    piece = tile_weights[:, :, : tile_weights.shape[2] // 2].reshape(-1, tile_weights.shape[2] // 2)
    probs = held(probs)
    (one,) = gated([turn(piece)], [mass, probs])
    two = turn(one)
    mine = [piece, one, two, *gated([turn(two)], [smass])]
    other = [swap(piece) for piece in mine]

    piece = sliced(tile_weights, 1, [mine[3]])
    one = turn(piece)
    *parts, total, probs = products(
        place, tile_pairs, tile_count, probs, before, mine, other, False, [piece]
    )
    (one,) = gated([one], [parts[0]])
    two = turn(one)
    own, near, far, to_right, to_left = parts
    left_part, right_part = send(to_right, "vy", 1), send(to_left, "vy", 3)
    near, far, given, table = relayed(near, far, left_part, right_part, to_right, [], [two])
    near, far = send(near, "vy", 1), send(far, "vy", 3)
    mine = [piece, one, two, *gated([turn(two)], [near, far])]
    later = products(
        place, tile_pairs, tile_count, probs, total, mine, [swap(piece) for piece in mine], True
    )

    *first, scales, factors = merged(place, given, [own, near, far], [], [later[0]])
    own, near, far, to_right, to_left = later
    left_part, right_part = send(to_right, "vy", 1), send(to_left, "vy", 3)
    stage = staged(place, student_unembed, [own])
    near, far, given = relayed(near, far, left_part, right_part, to_right, [table], [stage])
    parts = [own, send(near, "vy", 1), send(far, "vy", 3)]
    first = spread(first, "vz")
    second = merged(place, given, parts, [scales, factors])
    mine = gradients(place, logits, first + spread(second, "vz"))

    own = own_hidden(stage, mine)
    other = swap(mine)
    to_right, to_left = other_hidden(True, place, stage, mine, other, own)
    from_left, from_right = cross(to_right, 1, True), cross(to_left, 3, True)
    here, near, far = other_hidden(False, place, stage, mine, other, own, [to_right])
    near, far = passed(near, far, from_left, from_right)
    near, far = cross(near, 1, True), cross(far, 3, True)
    parts = middle(place, here, near, far, to_right, from_left, from_right)
    parts = [parts[0], *(cross(parts[step], step, False) for step in (1, 2, 3))]
    keep, give, loss = totals(place, parts)
    return turned(place, keep, swap(give)), loss[0]


def solution(mesh):
    grid = Mesh(mesh.devices.reshape(SIDE, SIDE, SIDE, 2), ("vy", "vz", "tx", "tc"))
    vocab, tokens = ("vy", "vz"), ("tx", "tc")
    return jax.shard_map(
        shards,
        mesh=grid,
        in_specs=(
            P(tokens, vocab),
            P(tokens, None),
            P(None, vocab),
            P(vocab, tokens, None),
            P(vocab, None),
            P(vocab),
        ),
        out_specs=(P(tokens, vocab), P(tokens)),
        check_vma=False,
    )
```

```python
import functools

import jax
import jax.numpy as jnp
from jax import lax
from jax.experimental import pallas as pl
from jax.experimental.pallas import tpu as pltpu
from jax.sharding import Mesh
from jax.sharding import PartitionSpec as P

F32 = jnp.float32
BF16 = jnp.bfloat16
SIDE = 4
VMEM = pl.BlockSpec(memory_space=pltpu.VMEM)
SMEM = pl.BlockSpec(memory_space=pltpu.SMEM)
ANY = pl.BlockSpec(memory_space=pl.ANY)
MIB = 1024 * 1024


def params(mib=16):
    return pltpu.CompilerParams(vmem_limit_bytes=mib * MIB)


def cost(flops, moved, transcendentals=0):
    return pl.CostEstimate(flops=flops, bytes_accessed=moved, transcendentals=transcendentals)


def send(value, axis, step):
    return lax.ppermute(value, axis, [(i, (i + step) % SIDE) for i in range(SIDE)])


def swap(value):
    return lax.ppermute(value, "tc", [(0, 1), (1, 0)])


def thirds(value):
    high = value.astype(BF16).astype(F32)
    rest = value - high
    middle = rest.astype(BF16).astype(F32)
    return high, middle, rest - middle


def slice_kernel(weights, *refs):
    piece = refs[-1]
    piece[...] = weights[...].reshape(piece.shape)


def sliced(weights, index, behind=()):
    slots, shard_rows, cols = weights.shape
    width = cols // 2
    return pl.pallas_call(
        slice_kernel,
        grid=(1,),
        out_shape=jax.ShapeDtypeStruct((slots * shard_rows, width), BF16),
        in_specs=[pl.BlockSpec((slots, shard_rows, width), lambda i: (0, 0, index))]
        + [ANY] * len(behind),
        out_specs=pl.BlockSpec((slots * shard_rows, width), lambda i: (0, 0)),
        compiler_params=params(),
        cost_estimate=cost(0, 2 * weights.size),
        name="slice_weights",
    )(weights, *behind)


def gate_kernel(*refs):
    pass


def gated(parts, behind):
    return pl.pallas_call(
        gate_kernel,
        out_shape=[jax.ShapeDtypeStruct(part.shape, part.dtype) for part in parts],
        in_specs=[ANY] * (len(parts) + len(behind)),
        out_specs=[ANY] * len(parts),
        input_output_aliases={i: i for i in range(len(parts))},
        compiler_params=params(),
        cost_estimate=cost(0, 0),
        name="gate",
    )(*parts, *behind)


def hold_kernel(source, out):
    out[...] = source[...]


def held(value):
    return pl.pallas_call(
        hold_kernel,
        out_shape=jax.ShapeDtypeStruct(value.shape, value.dtype),
        in_specs=[VMEM],
        out_specs=VMEM,
        compiler_params=params(),
        cost_estimate=cost(0, 4 * value.size),
        name="hold_probs",
    )(value)


def halves_kernel(right, left, *refs):
    top, low = refs[-2:]
    top[...] = right[...]
    low[...] = left[...]


def halves(right, left, behind):
    depth, width = right.shape
    shape = (depth // 2, width)
    return pl.pallas_call(
        halves_kernel,
        grid=(1,),
        out_shape=[jax.ShapeDtypeStruct(shape, BF16)] * 2,
        in_specs=[
            pl.BlockSpec(shape, lambda i: (0, 0)),
            pl.BlockSpec(shape, lambda i: (1, 0)),
        ]
        + [ANY] * len(behind),
        out_specs=[pl.BlockSpec(shape, lambda i: (0, 0))] * 2,
        compiler_params=params(),
        cost_estimate=cost(0, 4 * depth * width),
        name="take_halves",
    )(right, left, *behind)


def product_kernel(number, later, place, pairs, count, probs, before, *rest):
    pieces, (weights, total) = rest[:number], rest[-2:]
    outs = rest[-7:-2] if later else rest[-9:-4]
    block = 512
    rows, width = probs.shape[0], total.shape[2]
    half = rows // 2
    vocab_y = place[0]
    first_block = (vocab_y * SIDE + place[1]) * (probs.shape[1] // block)
    total[...] = jnp.zeros_like(total)
    starts = ((0, 0), (1, 0), (3, 0), (2, 0), (2, 512)) if number == 10 else ((0, 0), (1, 0), (2, 0), (3, 0))
    for core, parts in ((place[3], pieces[: number // 2]), (1 - place[3], pieces[number // 2 :])):
        for part, (step, start) in zip(parts, starts):
            x = lax.rem(place[2] + SIDE - step, SIDE)
            weights[x * 2 + core, start : start + part.shape[0]] = part[...]

    def tiles(group, carry):
        for member in range(4):
            slot = group * 4 + member
            teacher = pairs[slot, 0] - first_block
            owner = pairs[slot, 1] // SIDE
            columns = probs[:, pl.ds(pl.multiple_of(teacher * block, block), block)]
            matrix = weights[:, pl.ds(pl.multiple_of(slot * 64, 64), 64), :].reshape(block, width)
            product = jnp.dot(columns, matrix, preferred_element_type=F32)
            if member:
                product = jnp.where(slot < count[0], product, 0.0)
            total[owner] += product
        return carry

    lax.fori_loop(0, (count[0] + 3) // 4, tiles, 0)
    summed = jnp.zeros((rows, width), F32)
    for step in range(SIDE):
        start = lax.rem(vocab_y + step, SIDE) * SIDE
        for z in range(SIDE):
            value = total[start + z]
            summed += value
            value = value.astype(BF16)
            if step == 2:
                outs[3][z * half : z * half + half, :] = value[:half]
                outs[4][z * half : z * half + half, :] = value[half:]
            else:
                outs[step - step // 3][z * rows : z * rows + rows, :] = value
    line = jnp.sum(summed.T, axis=0, keepdims=True)
    if later:
        packed = pack_rows([line + before[0:1]])
    else:
        rest[-4][...] = jnp.broadcast_to(line, rest[-4].shape)
        rest[-3][...] = probs[...]
        packed = pack_rows([before[i : i + 1] for i in range(4)])
    for out in outs[3:]:
        out[SIDE * half : SIDE * half + 16, :] = packed


def products(place, pairs, count, probs, before, mine, other, later, behind=()):
    rows = probs.shape[0]
    depth, width = mine[0].shape
    pieces = [*mine, *other]
    outs = [jax.ShapeDtypeStruct((SIDE * rows, width), BF16)] * 3
    outs += [jax.ShapeDtypeStruct((SIDE * rows // 2 + 16, width), BF16)] * 2
    if not later:
        outs += [jax.ShapeDtypeStruct((8, rows), F32), jax.ShapeDtypeStruct(probs.shape, BF16)]
    return pl.pallas_call(
        functools.partial(product_kernel, len(pieces), later),
        out_shape=outs,
        in_specs=[SMEM, SMEM, SMEM] + [VMEM] * (2 + len(pieces)) + [ANY] * len(behind),
        out_specs=[VMEM] * len(outs),
        scratch_shapes=[
            pltpu.VMEM((2 * SIDE, depth, width), BF16),
            pltpu.VMEM((SIDE * SIDE, rows, width), F32),
        ],
        compiler_params=params(14),
        cost_estimate=cost(
            16 * 2 * rows * 512 * width, 2 * probs.size + 16 * depth * width + 32 * rows * width
        ),
        name="tile_products",
    )(place, pairs, count, probs, before, *pieces, *behind)


def pack_rows(lines):
    rows = [part for line in lines for part in thirds(line)]
    rows.append(jnp.zeros((16 - len(rows), rows[0].shape[1]), F32))
    return jnp.concatenate(rows, axis=0).astype(BF16)


def unpack_rows(packed, number):
    packed = packed.astype(F32)
    return [
        packed[3 * i : 3 * i + 1] + packed[3 * i + 1 : 3 * i + 2] + packed[3 * i + 2 : 3 * i + 3]
        for i in range(number)
    ]


def joined(stats):
    peak = functools.reduce(jnp.maximum, [line[0] for line in stats])
    speak = functools.reduce(jnp.maximum, [line[2] for line in stats])
    factors = [jnp.exp(line[0] - peak) for line in stats]
    mass = sum(line[1] * factor for line, factor in zip(stats, factors))
    smass = sum(line[3] * jnp.exp(line[2] - speak) for line in stats)
    return (peak, mass, speak, smass), factors


def columns_of(lines):
    lines = list(lines) + [jnp.zeros((128 - len(lines), lines[0].shape[1]), F32)]
    return jnp.concatenate(lines, axis=0).T


def relay_kernel(later, near, far, from_left, from_right, mine, *refs):
    depth = from_left.shape[0] - 16
    half = depth // SIDE
    rows = 2 * half
    number = 1 if later else 4
    stats = [unpack_rows(part[depth:, :], number) for part in (mine, from_left, from_right)]
    lines = stats[0] + stats[1] + stats[2]
    lines.append(jnp.zeros((16 - len(lines), rows), F32))
    if later:
        table = refs[0][...]
        near_out, far_out, kept = refs[-3:]
    else:
        near_out, far_out, kept, table_out = refs[-4:]
        own, left, right = (line[0] for line in stats)
        lane = lax.broadcasted_iota(jnp.int32, own.shape, 1)
        other = jnp.where(lane < half, left, right)
        peak = jnp.maximum(own, other)
        table = columns_of([jnp.exp(own - peak), jnp.exp(other - peak)])
        table_out[...] = table
    kept[...] = jnp.concatenate(lines, axis=0)
    near_out[SIDE * rows : SIDE * rows + 16, :] = from_left[depth : depth + 16, :]
    for z in range(SIDE):
        low, high = slice(z * rows, z * rows + half), slice(z * rows + half, (z + 1) * rows)
        part = slice(z * half, (z + 1) * half)
        value = table[:half, 0:1] * near[low, :].astype(F32) + table[:half, 1:2] * from_left[part, :].astype(F32)
        near_out[low, :] = value.astype(BF16)
        near_out[high, :] = near[high, :]
        value = table[half:, 0:1] * far[high, :].astype(F32) + table[half:, 1:2] * from_right[part, :].astype(F32)
        far_out[high, :] = value.astype(BF16)
        far_out[low, :] = far[low, :]


def relayed(near, far, from_left, from_right, mine, tables, behind=()):
    depth, width = near.shape
    rows = depth // SIDE
    outs = [
        jax.ShapeDtypeStruct((depth + 16, width), BF16),
        jax.ShapeDtypeStruct((depth, width), BF16),
        jax.ShapeDtypeStruct((16, rows), F32),
    ]
    if not tables:
        outs.append(jax.ShapeDtypeStruct((rows, 128), F32))
    return pl.pallas_call(
        functools.partial(relay_kernel, bool(tables)),
        out_shape=outs,
        in_specs=[VMEM] * (5 + len(tables)) + [ANY] * len(behind),
        out_specs=[VMEM] * len(outs),
        compiler_params=params(),
        cost_estimate=cost(depth * width, depth * width),
        name="relay_targets",
    )(near, far, from_left, from_right, mine, *tables, *behind)


def merge_kernel(later, place, given, *refs):
    parts = refs[:3]
    width = parts[0].shape[1]
    rows = parts[0].shape[0] // SIDE
    sent = parts[1][SIDE * rows :, :]
    if later:
        table, factors, outs = refs[3][...], refs[4], refs[-SIDE:]
        lines = [given[i : i + 1] for i in range(3)] + unpack_rows(sent, 1)
        packed = pack_rows([sum(line * factors[i : i + 1] for i, line in enumerate(lines))])
    else:
        outs = refs[-2 - SIDE : -2]
        lines = [[given[4 * i + j : 4 * i + j + 1] for j in range(4)] for i in range(3)]
        lines.append(unpack_rows(sent, 4))
        stats, factors = joined(lines)
        packed = pack_rows(stats)
        own, left, right, across = (line[0] for line in lines)
        lane = lax.broadcasted_iota(jnp.int32, own.shape, 1)
        low = lane < rows // 2
        left = jnp.where(low, jnp.maximum(left, across), left)
        right = jnp.where(low, right, jnp.maximum(right, across))
        table = columns_of([jnp.exp(base - stats[0]) for base in (own, left, right)])
        refs[-2][...] = table
        refs[-1][...] = jnp.concatenate(factors + [jnp.zeros((4, rows), F32)], axis=0)
    for step in range(SIDE):
        at = pl.ds(pl.multiple_of(lax.rem(place[1] + step, SIDE) * rows, rows), rows)
        value = table[:, 0:1] * parts[0][at, :].astype(F32)
        for d in range(1, 3):
            value += table[:, d : d + 1] * parts[d][at, :].astype(F32)
        outs[step][0:rows, :] = value.astype(BF16)
        outs[step][rows : rows + 16, :] = packed


def merged(place, given, parts, tables, behind=()):
    width = parts[0].shape[1]
    rows = parts[0].shape[0] // SIDE
    outs = [jax.ShapeDtypeStruct((rows + 16, width), BF16)] * SIDE
    if not tables:
        outs += [jax.ShapeDtypeStruct((rows, 128), F32), jax.ShapeDtypeStruct((8, rows), F32)]
    return pl.pallas_call(
        functools.partial(merge_kernel, bool(tables)),
        out_shape=outs,
        in_specs=[SMEM] + [VMEM] * (4 + len(tables)) + [ANY] * len(behind),
        out_specs=[VMEM] * len(outs),
        compiler_params=params(),
        cost_estimate=cost(rows * width, rows * width),
        name="merge_targets",
    )(place, given, *parts, *tables, *behind)


def gradient_kernel(place, logits, *refs):
    chunks, grad = (refs[:SIDE], refs[SIDE : 2 * SIDE]), refs[2 * SIDE]
    rows, width = logits.shape[0], refs[0].shape[1]
    stats, factors = joined([unpack_rows(part[rows:, :], 4) for part in chunks[0]])
    _, mass, peak, smass = stats
    total = sum(
        unpack_rows(part[rows:, :], 1)[0] * factor for part, factor in zip(chunks[1], factors)
    )
    total = total / mass
    floored = jnp.maximum(total, 1.0)
    scales = [factor / mass / floored for factor in factors]
    table = columns_of(scales + [total / floored / smass, peak, peak + jnp.log(smass)])
    share, peak, norm = (table[:, c : c + 1] for c in range(4, 7))
    terms = jnp.zeros((rows, width), F32)
    for step in range(SIDE):
        block = lax.rem(place[1] + SIDE - step, SIDE)
        for chunk, parts in enumerate(chunks):
            at = pl.ds(pl.multiple_of(block * 512 + chunk * width, width), width)
            scores = logits[:, at]
            target = parts[step][0:rows, :].astype(F32) * table[:, step : step + 1]
            positive = target > 0
            entropy = jnp.where(positive, target * jnp.log(jnp.where(positive, target, 1.0)), 0.0)
            terms += entropy - target * (scores - norm)
            value = share * jnp.exp(scores - peak) - target
            grad[at, :] = value.T.astype(BF16)
    grad[SIDE * 512 :, :] = pack_rows([jnp.sum(terms.T, axis=0, keepdims=True)])


def gradients(place, logits, parts):
    rows, cols = logits.shape
    return pl.pallas_call(
        gradient_kernel,
        out_shape=jax.ShapeDtypeStruct((cols + 16, rows), BF16),
        in_specs=[SMEM] + [VMEM] * (1 + 2 * SIDE),
        out_specs=VMEM,
        compiler_params=params(),
        cost_estimate=cost(60 * rows * cols, 8 * rows * cols, 2 * rows * cols),
        name="logit_grad",
    )(place, logits, *parts)


def stage_kernel(place, unembed, *refs):
    stage, sems = refs[-2:]
    first = place[3] == 0
    copies = []
    for major in range(SIDE):
        for minor in range(SIDE):
            index = major * SIDE + minor
            owner = jnp.where(first, index, minor * SIDE + major)
            start = pl.multiple_of(owner * 256 + place[3] * 128, 128)
            copies.append(
                pltpu.make_async_copy(
                    unembed.at[pl.ds(start, 128), :],
                    stage.at[pl.ds(index * 128, 128), :],
                    sems.at[index],
                )
            )
    for copy in copies:
        copy.start()
    for copy in copies:
        copy.wait()


def staged(place, unembed, behind):
    depth, cols = unembed.shape
    return pl.pallas_call(
        stage_kernel,
        out_shape=jax.ShapeDtypeStruct((depth // 2, cols), BF16),
        in_specs=[SMEM, pl.BlockSpec(memory_space=pltpu.HBM)] + [ANY] * len(behind),
        out_specs=VMEM,
        scratch_shapes=[pltpu.SemaphoreType.DMA((SIDE * SIDE,))],
        compiler_params=params(42),
        cost_estimate=cost(0, depth * cols),
        name="stage_unembed",
    )(place, unembed, *behind)


def own_kernel(stage, mine, out):
    depth = stage.shape[1]
    for step in range(SIDE):
        rows = slice(step * 512, step * 512 + 512)
        result = jnp.dot(stage[rows, :], mine[0:depth, :], preferred_element_type=F32)
        out[rows, :] = result.astype(BF16)


def own_hidden(stage, mine):
    depth, rows = stage.shape[0], mine.shape[1]
    return pl.pallas_call(
        own_kernel,
        out_shape=jax.ShapeDtypeStruct((depth, rows), BF16),
        in_specs=[VMEM, VMEM],
        out_specs=VMEM,
        compiler_params=params(),
        cost_estimate=cost(2 * stage.size * rows, 2 * stage.size),
        name="own_hidden",
    )(stage, mine)


def other_kernel(far_only, place, stage, mine, other, own, *refs):
    depth = stage.shape[1]
    rows = mine.shape[1]
    lanes = pl.ds(pl.multiple_of(place[3] * rows, rows), rows)
    other_lanes = pl.ds(pl.multiple_of((1 - place[3]) * rows, rows), rows)
    for index, step in enumerate((2,) if far_only else (0, 1, 3)):
        at = pl.ds(pl.multiple_of(lax.rem(place[4] + step, SIDE) * 512, 512), 512)
        result = jnp.dot(stage[at, :], other[0:depth, :], preferred_element_type=F32).astype(BF16)
        if far_only:
            for half, out in enumerate(refs[-2:]):
                out[0:256, other_lanes] = result[half * 256 : half * 256 + 256]
                out[256:272, lanes] = mine[depth : depth + 16, :]
                out[256:272, other_lanes] = other[depth : depth + 16, :]
                at = pl.multiple_of(lax.rem(place[4] + step, SIDE) * 512 + half * 256, 256)
                out[0:256, lanes] = own[pl.ds(at, 256), :]
        else:
            out = refs[index - 3]
            out[:, other_lanes] = result
            out[:, lanes] = own[at, :]


def other_hidden(far_only, place, stage, mine, other, own, behind=()):
    rows = mine.shape[1]
    shapes = [(272, 2 * rows)] * 2 if far_only else [(512, 2 * rows)] * 3
    return pl.pallas_call(
        functools.partial(other_kernel, far_only),
        out_shape=[jax.ShapeDtypeStruct(shape, BF16) for shape in shapes],
        in_specs=[SMEM] + [VMEM] * 4 + [ANY] * len(behind),
        out_specs=[VMEM] * len(shapes),
        compiler_params=params(),
        cost_estimate=cost((1 if far_only else 3) * stage.size * rows // 2, 2 * stage.size),
        name="other_hidden",
    )(place, stage, mine, other, own, *behind)


def pass_kernel(near, far, from_left, from_right, near_low, near_high, far_low, far_high):
    near_low[0:256, :] = (near[0:256, :].astype(F32) + from_left[0:256, :].astype(F32)).astype(BF16)
    near_low[256:272, :] = from_left[256:272, :]
    near_high[...] = near[256:512, :]
    far_low[...] = far[0:256, :]
    far_high[...] = (far[256:512, :].astype(F32) + from_right[0:256, :].astype(F32)).astype(BF16)


def passed(near, far, from_left, from_right):
    rows = near.shape[1]
    return pl.pallas_call(
        pass_kernel,
        out_shape=[jax.ShapeDtypeStruct((depth, rows), BF16) for depth in (272, 256, 256, 256)],
        in_specs=[VMEM] * 4,
        out_specs=[VMEM] * 4,
        compiler_params=params(),
        cost_estimate=cost(512 * rows, 10 * 512 * rows),
        name="pass_grads",
    )(near, far, from_left, from_right)


def ordered_loss(index, pieces, ordered):
    for step, piece in pieces:
        ordered[lax.rem(index + step, SIDE)] = unpack_rows(piece, 1)[0]
    return ((ordered[0] + ordered[1]) + ordered[2]) + ordered[3]


def middle_kernel(place, own, left_low, left_high, right_low, right_high, mine, from_left, from_right, *refs):
    outs, ordered, summed = refs[:SIDE], refs[SIDE], refs[SIDE + 1]
    pieces = [
        (0, mine[256:272, :]),
        (3, from_left[256:272, :]),
        (1, from_right[256:272, :]),
        (2, left_low[256:272, :]),
    ]
    packed = pack_rows([ordered_loss(place[4], pieces, ordered)])
    for start, left, right in ((0, left_low, right_low), (256, left_high, right_high)):
        value = own[start : start + 256, :].astype(F32) + left[0:256, :].astype(F32)
        summed[start : start + 256, :] = (value + right[...].astype(F32)).astype(BF16)
    for step in range(SIDE):
        at = pl.ds(pl.multiple_of(lax.rem(place[5] + step, SIDE) * 128, 128), 128)
        outs[step][0:128, :] = summed[at, :]
        outs[step][128:144, :] = packed


def middle(place, own, *parts):
    rows = own.shape[1]
    return pl.pallas_call(
        middle_kernel,
        out_shape=[jax.ShapeDtypeStruct((144, rows), BF16)] * SIDE,
        in_specs=[SMEM] + [VMEM] * (1 + len(parts)),
        out_specs=[VMEM] * SIDE,
        scratch_shapes=[pltpu.VMEM((SIDE, 1, rows), F32), pltpu.VMEM((512, rows), BF16)],
        compiler_params=params(),
        cost_estimate=cost(4 * 512 * rows, 10 * 512 * rows),
        name="merge_grads",
    )(place, own, *parts)


def total_kernel(place, *refs):
    parts = refs[:SIDE]
    keep, give, loss, ordered = refs[SIDE:]
    rows = keep.shape[1]
    mine = pl.ds(pl.multiple_of(place[3] * rows, rows), rows)
    other = pl.ds(pl.multiple_of((1 - place[3]) * rows, rows), rows)
    pieces = [((SIDE - step) % SIDE, part[128:144, :]) for step, part in enumerate(parts)]
    ordered[4] = ordered_loss(place[5], pieces, ordered)
    loss[...] = jnp.broadcast_to(ordered[4, :, mine], loss.shape)
    for lanes, out in ((other, give), (mine, keep)):
        value = parts[0][0:128, lanes].astype(F32)
        for part in parts[1:]:
            value += part[0:128, lanes].astype(F32)
        out[...] = value.astype(BF16)


def totals(place, parts):
    rows = parts[0].shape[1] // 2
    half = jax.ShapeDtypeStruct((128, rows), BF16)
    return pl.pallas_call(
        total_kernel,
        out_shape=[half, half, jax.ShapeDtypeStruct((8, rows), F32)],
        in_specs=[SMEM] + [VMEM] * SIDE,
        out_specs=[VMEM] * 3,
        scratch_shapes=[pltpu.VMEM((SIDE + 1, 1, 2 * rows), F32)],
        compiler_params=params(),
        cost_estimate=cost(8 * 128 * rows, 20 * 128 * rows),
        name="sum_grads",
    )(place, *parts)


def turn_kernel(place, keep, given, grad):
    mine = pl.ds(pl.multiple_of(place[3] * 128, 128), 128)
    other = pl.ds(pl.multiple_of((1 - place[3]) * 128, 128), 128)
    grad[:, mine] = keep[...].astype(F32).T.astype(BF16)
    grad[:, other] = given[...].astype(F32).T.astype(BF16)


def turned(place, keep, given):
    rows = keep.shape[1]
    return pl.pallas_call(
        turn_kernel,
        out_shape=jax.ShapeDtypeStruct((rows, 256), BF16),
        in_specs=[SMEM, VMEM, VMEM],
        out_specs=VMEM,
        compiler_params=params(),
        cost_estimate=cost(0, 4 * 256 * rows),
        name="turn_grads",
    )(place, keep, given)


def spread(parts, axis):
    return [parts[0]] + [send(parts[step], axis, step) for step in (1, 2, 3)]


def cross(value, step, first):
    def target(y, z, core):
        if (core == 0) == first:
            y = (y + step) % SIDE
        else:
            z = (z + step) % SIDE
        return (y * SIDE + z) * 2 + core

    places = [(y, z, core) for y in range(SIDE) for z in range(SIDE) for core in range(2)]
    pairs = [(i, target(*at)) for i, at in enumerate(places)]
    return lax.ppermute(value, ("vy", "vz", "tc"), pairs)


def shards(teacher_logits, student_hidden, student_unembed, tile_weights, tile_pairs, tile_count):
    y, z, x, core = (lax.axis_index(name) for name in ("vy", "vz", "tx", "tc"))
    crossing = [jnp.where(core == 0, y, z), jnp.where(core == 0, z, y)]
    place = jnp.stack([y, z, x, core] + crossing).astype(jnp.int32)
    rows = teacher_logits.shape[0]
    teacher = teacher_logits.astype(F32)
    peak = jnp.max(teacher, axis=1)
    shifted = jnp.exp(teacher - peak[:, None])
    mass = jnp.sum(shifted, axis=1)
    probs = shifted.astype(BF16)

    logits = jnp.dot(student_hidden, student_unembed, preferred_element_type=F32)
    speak = jnp.max(logits, axis=1)
    smass = jnp.sum(jnp.exp(logits - speak[:, None]), axis=1)

    before = jnp.stack([peak, mass, speak, smass] * 2)

    piece = tile_weights[:, :, : tile_weights.shape[2] // 2].reshape(-1, tile_weights.shape[2] // 2)
    probs = held(probs)
    mine = [piece, *gated(spread([piece] * SIDE, "tx")[1:], [mass, smass, probs])]
    other = [swap(piece) for piece in mine]

    piece = sliced(tile_weights, 1, [mine[1]])
    right, left = send(piece, "tx", 1), send(piece, "tx", 3)
    *parts, total, probs = products(
        place, tile_pairs, tile_count, probs, before, mine, other, False, [piece]
    )
    top, low = halves(right, left, [parts[0]])
    own, near, far, to_right, to_left = parts
    left_part, right_part = send(to_right, "vy", 1), send(to_left, "vy", 3)
    near, far, given, table = relayed(near, far, left_part, right_part, to_right, [], [right, left])
    near, far = send(near, "vy", 1), send(far, "vy", 3)
    top, low = gated([send(top, "tx", 1), send(low, "tx", 3)], [near, far])
    mine = [piece, right, left, top, low]
    later = products(
        place, tile_pairs, tile_count, probs, total, mine, [swap(piece) for piece in mine], True
    )

    *first, scales, factors = merged(place, given, [own, near, far], [], [later[0]])
    own, near, far, to_right, to_left = later
    left_part, right_part = send(to_right, "vy", 1), send(to_left, "vy", 3)
    stage = staged(place, student_unembed, [own])
    near, far, given = relayed(near, far, left_part, right_part, to_right, [table], [stage])
    parts = [own, send(near, "vy", 1), send(far, "vy", 3)]
    first = spread(first, "vz")
    second = merged(place, given, parts, [scales, factors])
    mine = gradients(place, logits, first + spread(second, "vz"))

    own = own_hidden(stage, mine)
    other = swap(mine)
    to_right, to_left = other_hidden(True, place, stage, mine, other, own)
    from_left, from_right = cross(to_right, 1, True), cross(to_left, 3, True)
    here, near, far = other_hidden(False, place, stage, mine, other, own, [to_right])
    sent = passed(near, far, from_left, from_right)
    sent = [cross(part, step, True) for part, step in zip(sent, (1, 1, 3, 3))]
    parts = middle(place, here, *sent, to_right, from_left, from_right)
    parts = [parts[0], *(cross(parts[step], step, False) for step in (1, 2, 3))]
    keep, give, loss = totals(place, parts)
    return turned(place, keep, swap(give)), loss[0]


def solution(mesh):
    grid = Mesh(mesh.devices.reshape(SIDE, SIDE, SIDE, 2), ("vy", "vz", "tx", "tc"))
    vocab, tokens = ("vy", "vz"), ("tx", "tc")
    return jax.shard_map(
        shards,
        mesh=grid,
        in_specs=(
            P(tokens, vocab),
            P(tokens, None),
            P(None, vocab),
            P(vocab, tokens, None),
            P(vocab, None),
            P(vocab),
        ),
        out_specs=(P(tokens, vocab), P(tokens)),
        check_vma=False,
    )
```
